32 devices in a mesh: gx: 8 (over y, x, core), gy: 4 (over z).
Axes of the slice: x: 2, y: 2, z: 4, core: 2. Of those that a mesh axis runs over, the one named last changes fastest.
Arguments:
- points: bfloat16 [32768, 64], P(('gx', 'gy')), may hold values from -6 to 6
- pivots: int32 [2, 128], replicated, may hold values from 0 to 1023, as said below
- owners: int32 [2], replicated, may hold values from 0 to 31
- coeffs: float32 [256, 64], replicated, may hold values from -6 to 6
- noise: float32 [32768, 64], P(('gx', 'gy')), may hold values from -4 to 4
Outputs:
- kernel_probes: float32 [32768, 64], P(('gx', 'gy'))
- factor: float32 [32768, 256], P(('gx', 'gy'))
The draws below stay inside these ranges and needn't reach their ends.
Inputs may be any that keep to these rules, and one draw needn't show every extreme that they name: `pivots`: the two rows together hold 256 distinct indices, among them 0 and 1023.
All inputs are finite; a program needn't handle non-finite values.
Results may differ from the reference program's by a relative error of at most 0.0003.
Values may be sent and summed in bfloat16 or wider, within the bound.
No kernel may reach another device: no remote copies, remote signals or barrier semaphores. Data moves between devices by JAX's collectives and lax.ppermute only.
A program may use at most 64 MiB of HBM per device.

```python
import jax
import jax.numpy as jnp
from jax import lax

D = 64
PROBE_VECTORS = 64
PIVOTS = 128
KERNEL_SCALE = 32
P_DEV = 1024
N = 32768
RANK = 256
N_GX = 8
N_GY = 4


latent_rank = 8


def draw_pivots(key, part):
    key_inner, key_order = jax.random.split(jax.random.fold_in(key, 17))
    inner = jax.random.permutation(key_inner, jnp.arange(P_DEV - 2, dtype=jnp.int32)) + 1
    chosen = jnp.concatenate([jnp.array([0, P_DEV - 1], dtype=jnp.int32), inner[:2 * PIVOTS - 2].astype(jnp.int32)])
    order = jax.random.permutation(key_order, jnp.arange(2 * PIVOTS, dtype=jnp.int32))
    return chosen[order].reshape(2, PIVOTS)


def draw_points(key, part):
    key_map, key_latent, key_rough = jax.random.split(jax.random.fold_in(key, 29), 3)
    mixing = jax.random.normal(key_map, (latent_rank, D), jnp.float32) / jnp.sqrt(1.0 * D)
    kernel_spread = jnp.sqrt(KERNEL_SCALE / 4.0)
    latent = jax.random.normal(key_latent, (N, latent_rank), jnp.float32) * kernel_spread
    rough_scale = 0.05
    values = jnp.dot(latent, mixing, precision=lax.Precision.HIGHEST)
    values = values + rough_scale * jax.random.normal(key_rough, (N, D), jnp.float32)
    return jnp.clip(values, -6.0, 6.0).astype(jnp.bfloat16)


def block_scale(stream_key, shape, cuts, smallest, largest):
    def one(dim, shards_of):
        heights = jax.random.uniform(jax.random.fold_in(jax.random.fold_in(stream_key, 6), dim), (shards_of,), jnp.float32, smallest / len(cuts), largest / len(cuts))
        return jnp.repeat(jnp.exp(heights), shape[dim] // shards_of).reshape((-1,) + (1,) * (len(shape) - dim - 1))

    loudness = one(*cuts[0])
    for cut in cuts[1:]:
        loudness = loudness * one(*cut)
    return loudness


def scatter_about(own_key, shape, width, bound, cuts=(), held_as=jnp.bfloat16):
    result = width * jax.random.normal(own_key, shape, jnp.float32)
    if cuts:
        result = result * block_scale(own_key, shape, cuts, -0.22, 0.18)
    return jnp.clip(result, -bound, bound).astype(held_as)


def setup_inputs(seed: int = 0) -> dict:
    keys = jax.random.split(jax.random.key(seed), 6)
    points = draw_points(jax.random.fold_in(keys[5], 71), 0)
    pivots = draw_pivots(jax.random.fold_in(keys[5], 71), 0)
    owners = jax.random.randint(keys[2], (2,), 0, N_GX * N_GY).astype(jnp.int32)
    coeffs = scatter_about(keys[3], (RANK, PROBE_VECTORS), 1.0, 6.0, (), jnp.float32)
    noise = scatter_about(keys[4], (N, PROBE_VECTORS), 0.5, 4.0, ((0, 32),), jnp.float32)
    return {"points": points, "pivots": pivots, "owners": owners, "coeffs": coeffs, "noise": noise}


jitter = 0.1
noise_weight = 0.5

def kern(left, right):
    left32 = left.astype(jnp.float32)
    right32 = right.astype(jnp.float32)
    left_square_norm = lax.optimization_barrier(jnp.sum(left32 * left32, axis=1))
    right_square_norm = lax.optimization_barrier(jnp.sum(right32 * right32, axis=1))
    cross_term = jnp.dot(left32.astype(jnp.float32), right32.T.astype(jnp.float32), precision=lax.Precision.HIGHEST, preferred_element_type=jnp.float32)
    return jnp.exp(-(left_square_norm[:, None] + right_square_norm[None, :] - 2.0 * cross_term) / (1.0 * KERNEL_SCALE))

def reference(points, pivots, owners, coeffs, noise):
    block_list = N_GX * N_GY
    hp = lax.Precision.HIGHEST
    solve = jax.scipy.linalg.solve_triangular

    def pick(round_index):
        start = (owners[round_index] * P_DEV).astype(jnp.int32)
        owner_block = lax.dynamic_slice_in_dim(points, start, P_DEV, 0)
        return owner_block[pivots[round_index]]
    first = pick(0)
    second = pick(1)
    ident = jnp.eye(PIVOTS, dtype=jnp.float32)
    chol_one = jnp.linalg.cholesky(kern(first, first) + jitter * ident)
    first_cols = solve(chol_one, kern(points, first).T, lower=True).T
    rows = solve(chol_one, kern(second, first).T, lower=True).T
    chol_two = jnp.linalg.cholesky(kern(second, second) - jnp.dot(rows, rows.T, precision=hp) + jitter * ident)
    residual_cols = kern(points, second) - jnp.dot(first_cols, rows.T, precision=hp)
    second_cols = solve(chol_two, residual_cols.T, lower=True).T
    factor = jnp.concatenate([first_cols, second_cols], axis=1)
    probes = jnp.dot(factor.astype(jnp.float32), coeffs.astype(jnp.float32), precision=hp, preferred_element_type=jnp.float32) + noise
    probe_bf = probes.astype(jnp.bfloat16)

    def one_block(block_index):
        left_block = lax.dynamic_slice_in_dim(points, (block_index * P_DEV).astype(jnp.int32), P_DEV, 0)
        total = jnp.zeros((P_DEV, PROBE_VECTORS), jnp.float32)
        for block_offset in range(-3, 4):
            other = (block_index + block_offset) % block_list * P_DEV
            other = other.astype(jnp.int32)
            right_block = lax.dynamic_slice_in_dim(points, other, P_DEV, 0)
            right_probe = lax.dynamic_slice_in_dim(probe_bf, other, P_DEV, 0)
            tile = kern(left_block, right_block).astype(jnp.bfloat16)
            total = total + jnp.dot(tile.astype(jnp.float32), right_probe.astype(jnp.float32), precision=hp, preferred_element_type=jnp.float32)
        return total
    banded = lax.map(one_block, jnp.arange(block_list, dtype=jnp.int32)).reshape(N, PROBE_VECTORS)
    kernel_probes = banded / jnp.sqrt(1.0 * P_DEV) + noise_weight * probes
    return (kernel_probes, factor)
```

```python
import jax
import jax.numpy as jnp
from jax import lax
from jax.sharding import PartitionSpec as P

PIVOTS = 128
KERNEL_SCALE = 32
BAND = 3


jitter = 0.1
noise_weight = 0.5


def shifted(value, axis, steps):
    count = lax.axis_size(axis)
    return lax.ppermute(value, axis, [((i + steps) % count, i) for i in range(count)])


def summed(value, axis):
    count = lax.axis_size(axis)
    if count > 8:
        return lax.psum(value, axis)
    total = value
    for steps in range(1, count):
        total = total + shifted(value, axis, steps)
    return total


def kern(left, right):
    left_square_norm = jnp.sum(jnp.square(left.astype(jnp.float32)), axis=1)
    right_square_norm = jnp.sum(jnp.square(right.astype(jnp.float32)), axis=1)
    cross_term = jnp.dot(left, right.T, preferred_element_type=jnp.float32)
    return jnp.exp(
        -(left_square_norm[:, None] + right_square_norm[None, :] - 2.0 * cross_term)
        / (1.0 * KERNEL_SCALE)
    )


def neighbours(value, tall):
    outer, inner = lax.axis_size("gx"), lax.axis_size("gy")
    if not tall:
        return [shifted(value, ("gx", "gy"), k) for k in range(-BAND, BAND + 1) if k != 0]
    own, other = [], []
    for k in range(1, inner):
        own.append(shifted(value, "gy", k))
    for k in range(1, inner):
        pairs = []
        for x in range(outer):
            for z in range(inner):
                source = (x - 1 if z + k < inner else x + 1) % outer
                pairs.append((source * inner + z, x * inner + z))
        other.append(lax.ppermute(own[k - 1], ("gx", "gy"), pairs))
    return own + other


def shards(points, pivots, owners, coeffs, noise):
    hp = lax.Precision.HIGHEST
    solve = jax.scipy.linalg.solve_triangular
    count, width = points.shape
    tall = lax.axis_size("gy") == BAND + 1
    me = lax.axis_index(("gx", "gy"))

    index = lax.broadcasted_iota(jnp.int32, (2, PIVOTS, count), 2)
    wanted = jnp.where((owners == me)[:, None], pivots, -1)
    chosen = (index == wanted[:, :, None]).astype(jnp.bfloat16).reshape(2 * PIVOTS, count)
    picked = jnp.dot(chosen, points, preferred_element_type=jnp.float32).astype(jnp.bfloat16)
    pivot_points = summed(summed(picked, "gy"), "gx")
    near_points = neighbours(points, tall)

    size = 2 * PIVOTS
    ident = jnp.eye(size, dtype=jnp.float32)
    chol = jnp.linalg.cholesky(kern(pivot_points, pivot_points) + jitter * ident)
    inverse = solve(chol, ident, lower=True)
    cols = kern(points, pivot_points)
    weights = jnp.dot(inverse.T, coeffs, precision=hp)
    probes = jnp.dot(cols, weights, precision=hp, preferred_element_type=jnp.float32) + noise
    sent = probes.astype(jnp.bfloat16)
    near_probes = neighbours(sent, tall)
    factor = jnp.dot(cols, inverse.T, precision=hp, preferred_element_type=jnp.float32)

    total = jnp.zeros((count, probes.shape[1]), jnp.float32)
    for other, probe in zip([points] + near_points, [sent] + near_probes):
        tile = kern(points, other).astype(jnp.bfloat16)
        total = total + jnp.dot(tile, probe, preferred_element_type=jnp.float32)
    kernel_probes = total / jnp.sqrt(1.0 * count) + noise_weight * probes
    return (kernel_probes, factor)


def solution(mesh):
    in_specs = (P(("gx", "gy"), None), P(), P(), P(), P(("gx", "gy"), None))
    out_specs = (P(("gx", "gy"), None), P(("gx", "gy"), None))
    return jax.shard_map(shards, mesh=mesh, in_specs=in_specs, out_specs=out_specs, check_vma=False)
```

```python
import jax
import jax.numpy as jnp
from jax import lax
from jax.experimental import pallas as pl
from jax.experimental.pallas import tpu as pltpu
from jax.sharding import PartitionSpec as P

PIVOTS = 128
KERNEL_SCALE = 32
BAND = 3
STRIP = 8
LANES = 128


jitter = 0.1
noise_weight = 0.5


def shifted(value, axis, steps):
    count = lax.axis_size(axis)
    return lax.ppermute(value, axis, [((i + steps) % count, i) for i in range(count)])


def summed(value, axis):
    count = lax.axis_size(axis)
    if count > 8:
        return lax.psum(value, axis)
    total = value
    for steps in range(1, count):
        total = total + shifted(value, axis, steps)
    return total


def kern(left, right):
    left_square_norm = jnp.sum(jnp.square(left.astype(jnp.float32)), axis=1)
    right_square_norm = jnp.sum(jnp.square(right.astype(jnp.float32)), axis=1)
    cross_term = jnp.dot(left, right.T, preferred_element_type=jnp.float32)
    return jnp.exp(
        -(left_square_norm[:, None] + right_square_norm[None, :] - 2.0 * cross_term)
        / (1.0 * KERNEL_SCALE)
    )


def column(strip, lane):
    index = jnp.full(strip.shape, lane, jnp.int32)
    return jnp.take_along_axis(strip, index, axis=1, mode="promise_in_bounds")


def row(strip, i):
    return jnp.broadcast_to(strip[i:i + 1, :], strip.shape)


def halves(value):
    return jnp.concatenate([value, value], axis=1)


def thirds(value):
    high = value.astype(jnp.bfloat16).astype(jnp.float32)
    rest = value - high
    middle = rest.astype(jnp.bfloat16).astype(jnp.float32)
    return high, middle, rest - middle


def invert_factor_kernel(pivot_ref, coeff_ref, inverse_ref, weight_ref, state_ref):
    size = pivot_ref.shape[0]
    pivots = pivot_ref[...]
    cross = lax.dot_general(pivots, pivots, (((1,), (1,)), ((), ())), preferred_element_type=jnp.float32)
    equal = lax.broadcasted_iota(jnp.int32, cross.shape, 0) == lax.broadcasted_iota(jnp.int32, cross.shape, 1)
    diagonal = jnp.where(equal, cross, 0.0)
    norms = jnp.sum(diagonal, axis=1, keepdims=True) + jnp.sum(diagonal, axis=0, keepdims=True)
    state_ref[...] = jnp.exp(-(norms - 2.0 * cross) * (1.0 / KERNEL_SCALE)) + jnp.where(equal, jitter, 0.0)
    lane = lax.broadcasted_iota(jnp.int32, (STRIP, size), 1)
    level = lax.broadcasted_iota(jnp.int32, (STRIP, size), 0)
    low = level[:, :LANES]

    def body(p, carry):
        strip, before = carry
        start = p * STRIP
        base = lax.rem(start, LANES)

        def part(wide):
            return jnp.where(start < LANES, wide[:, :LANES], wide[:, LANES:])

        high, middle, little = thirds(before)
        left = jnp.concatenate([high, high, middle, high, little, middle], axis=0).astype(jnp.bfloat16)
        right = jnp.concatenate([high, middle, high, little, high, middle], axis=0).astype(jnp.bfloat16)
        change = lax.dot_general(left, right, (((0,), (0,)), ((), ())), preferred_element_type=jnp.float32)
        all_lanes = lax.broadcasted_iota(jnp.int32, change.shape, 1)
        cleared = (all_lanes >= start - STRIP) & (all_lanes < start)
        state_ref[...] = jnp.where(cleared, 0.0, state_ref[...]) - change

        near = part(strip)
        columns = [column(near, base + k) for k in range(STRIP)]
        a = [[row(columns[k], i) for k in range(i + 1)] for i in range(STRIP)]
        scale = [None] * STRIP
        for k in range(STRIP):
            scale[k] = lax.rsqrt(a[k][k])
            for i in range(k + 1, STRIP):
                a[i][k] = a[i][k] * scale[k]
            for i in range(k + 1, STRIP):
                for j in range(k + 1, i + 1):
                    a[i][j] = a[i][j] - a[i][k] * a[j][k]
        t = [[None] * STRIP for _ in range(STRIP)]
        for j in range(STRIP):
            t[j][j] = scale[j]
            for i in range(j + 1, STRIP):
                total = a[i][j] * t[j][j]
                for q in range(j + 1, i):
                    total = total + a[i][q] * t[q][j]
                t[i][j] = -scale[i] * total

        own = (lane >= start) & (lane < start + STRIP)
        entered = jnp.where(own, jnp.where(lane - start == level, 1.0, 0.0), strip)
        done = jnp.zeros_like(strip)
        for k in range(STRIP):
            t_column = jnp.zeros((STRIP, LANES), jnp.float32)
            for i in range(k, STRIP):
                t_column = jnp.where(low == i, t[i][k], t_column)
            done = done + halves(t_column) * row(entered, k)
        inverse_ref[pl.ds(pl.multiple_of(start, STRIP), STRIP), :] = jnp.where(lane < start + STRIP, done, 0.0)

        following = jnp.minimum(start + STRIP, size - STRIP)
        coming = state_ref[pl.ds(pl.multiple_of(following, STRIP), STRIP), :]
        near = part(coming)
        columns = [column(near, base + k) for k in range(STRIP)]
        update = jnp.zeros_like(strip)
        for k in range(STRIP):
            l_column = columns[0] * t[k][0]
            for j in range(1, k + 1):
                l_column = l_column + columns[j] * t[k][j]
            update = update + halves(l_column) * row(done, k)
        return jnp.where(own, 0.0, coming) - update, done

    first = state_ref[0:STRIP, :]
    lax.fori_loop(0, size // STRIP, body, (first, jnp.zeros_like(first)))
    weight_ref[...] = lax.dot_general(
        inverse_ref[...],
        coeff_ref[...],
        (((0,), (0,)), ((), ())),
        precision=lax.Precision.HIGHEST,
        preferred_element_type=jnp.float32,
    )


def invert_factor(pivots, coeffs):
    size = pivots.shape[0]
    return pl.pallas_call(
        invert_factor_kernel,
        out_shape=(
            jax.ShapeDtypeStruct((size, size), jnp.float32),
            jax.ShapeDtypeStruct(coeffs.shape, jnp.float32),
        ),
        in_specs=[pl.BlockSpec(memory_space=pltpu.VMEM)] * 2,
        out_specs=(pl.BlockSpec(memory_space=pltpu.VMEM),) * 2,
        scratch_shapes=[pltpu.VMEM((size, size), jnp.float32)],
        cost_estimate=pl.CostEstimate(flops=size * size * size * 6, bytes_accessed=size * size * 4, transcendentals=size * size),
        name="invert_factor",
    )(pivots, coeffs)


def neighbours(value, tall):
    outer, inner = lax.axis_size("gx"), lax.axis_size("gy")
    if not tall:
        return [shifted(value, ("gx", "gy"), k) for k in range(-BAND, BAND + 1) if k != 0]
    own, other = [], []
    for k in range(1, inner):
        own.append(shifted(value, "gy", k))
    for k in range(1, inner):
        pairs = []
        for x in range(outer):
            for z in range(inner):
                source = (x - 1 if z + k < inner else x + 1) % outer
                pairs.append((source * inner + z, x * inner + z))
        other.append(lax.ppermute(own[k - 1], ("gx", "gy"), pairs))
    return own + other


def shards(points, pivots, owners, coeffs, noise):
    hp = lax.Precision.HIGHEST
    count, width = points.shape
    tall = lax.axis_size("gy") == BAND + 1
    me = lax.axis_index(("gx", "gy"))

    index = lax.broadcasted_iota(jnp.int32, (2, PIVOTS, count), 2)
    wanted = jnp.where((owners == me)[:, None], pivots, -1)
    chosen = (index == wanted[:, :, None]).astype(jnp.bfloat16).reshape(2 * PIVOTS, count)
    picked = jnp.dot(chosen, points, preferred_element_type=jnp.float32).astype(jnp.bfloat16)
    pivot_points = summed(summed(picked, "gy"), "gx")
    near_points = neighbours(points, tall)

    inverse, weights = invert_factor(pivot_points, coeffs)
    cols = kern(points, pivot_points)
    probes = jnp.dot(cols, weights, precision=hp, preferred_element_type=jnp.float32) + noise
    sent = probes.astype(jnp.bfloat16)
    near_probes = neighbours(sent, tall)
    factor = jnp.dot(cols, inverse.T, precision=hp, preferred_element_type=jnp.float32)

    total = jnp.zeros((count, probes.shape[1]), jnp.float32)
    for other, probe in zip([points] + near_points, [sent] + near_probes):
        tile = kern(points, other).astype(jnp.bfloat16)
        total = total + jnp.dot(tile, probe, preferred_element_type=jnp.float32)
    kernel_probes = total / jnp.sqrt(1.0 * count) + noise_weight * probes
    return (kernel_probes, factor)


def solution(mesh):
    in_specs = (P(("gx", "gy"), None), P(), P(), P(), P(("gx", "gy"), None))
    out_specs = (P(("gx", "gy"), None), P(("gx", "gy"), None))
    return jax.shard_map(shards, mesh=mesh, in_specs=in_specs, out_specs=out_specs, check_vma=False)
```

```python
import jax
import jax.numpy as jnp
from jax import lax
from jax.experimental import pallas as pl
from jax.experimental.pallas import tpu as pltpu
from jax.sharding import PartitionSpec as P

PIVOTS = 128
KERNEL_SCALE = 32
BAND = 3
STRIP = 8
LANES = 128


jitter = 0.1
noise_weight = 0.5


def shifted(value, axis, steps):
    count = lax.axis_size(axis)
    return lax.ppermute(value, axis, [((i + steps) % count, i) for i in range(count)])


def kern(left, right):
    left_square_norm = jnp.sum(jnp.square(left.astype(jnp.float32)), axis=1)
    right_square_norm = jnp.sum(jnp.square(right.astype(jnp.float32)), axis=1)
    cross_term = jnp.dot(left, right.T, preferred_element_type=jnp.float32)
    return jnp.exp(
        -(left_square_norm[:, None] + right_square_norm[None, :] - 2.0 * cross_term)
        / (1.0 * KERNEL_SCALE)
    )


def column(strip, lane):
    index = jnp.full(strip.shape, lane, jnp.int32)
    return jnp.take_along_axis(strip, index, axis=1, mode="promise_in_bounds")


def row(strip, i):
    return jnp.broadcast_to(strip[i:i + 1, :], strip.shape)


def halves(value):
    return jnp.concatenate([value, value], axis=1)


def thirds(value):
    high = value.astype(jnp.bfloat16).astype(jnp.float32)
    rest = value - high
    middle = rest.astype(jnp.bfloat16).astype(jnp.float32)
    return high, middle, rest - middle


def invert_factor_kernel(pivot_ref, coeff_ref, inverse_ref, weight_ref, state_ref):
    size = pivot_ref.shape[0]
    pivots = pivot_ref[...]
    cross = lax.dot_general(pivots, pivots, (((1,), (1,)), ((), ())), preferred_element_type=jnp.float32)
    equal = lax.broadcasted_iota(jnp.int32, cross.shape, 0) == lax.broadcasted_iota(jnp.int32, cross.shape, 1)
    diagonal = jnp.where(equal, cross, 0.0)
    norms = jnp.sum(diagonal, axis=1, keepdims=True) + jnp.sum(diagonal, axis=0, keepdims=True)
    state_ref[...] = jnp.exp(-(norms - 2.0 * cross) * (1.0 / KERNEL_SCALE)) + jnp.where(equal, jitter, 0.0)
    lane = lax.broadcasted_iota(jnp.int32, (STRIP, size), 1)
    level = lax.broadcasted_iota(jnp.int32, (STRIP, size), 0)
    low = level[:, :LANES]

    def body(p, carry):
        strip, before = carry
        start = p * STRIP
        base = lax.rem(start, LANES)

        def part(wide):
            return jnp.where(start < LANES, wide[:, :LANES], wide[:, LANES:])

        high, middle, little = thirds(before)
        left = jnp.concatenate([high, high, middle, high, little, middle], axis=0).astype(jnp.bfloat16)
        right = jnp.concatenate([high, middle, high, little, high, middle], axis=0).astype(jnp.bfloat16)
        change = lax.dot_general(left, right, (((0,), (0,)), ((), ())), preferred_element_type=jnp.float32)
        all_lanes = lax.broadcasted_iota(jnp.int32, change.shape, 1)
        cleared = (all_lanes >= start - STRIP) & (all_lanes < start)
        state_ref[...] = jnp.where(cleared, 0.0, state_ref[...]) - change

        near = part(strip)
        columns = [column(near, base + k) for k in range(STRIP)]
        a = [[row(columns[k], i) for k in range(i + 1)] for i in range(STRIP)]
        scale = [None] * STRIP
        for k in range(STRIP):
            scale[k] = lax.rsqrt(a[k][k])
            for i in range(k + 1, STRIP):
                a[i][k] = a[i][k] * scale[k]
            for i in range(k + 1, STRIP):
                for j in range(k + 1, i + 1):
                    a[i][j] = a[i][j] - a[i][k] * a[j][k]
        t = [[None] * STRIP for _ in range(STRIP)]
        for j in range(STRIP):
            t[j][j] = scale[j]
            for i in range(j + 1, STRIP):
                total = a[i][j] * t[j][j]
                for q in range(j + 1, i):
                    total = total + a[i][q] * t[q][j]
                t[i][j] = -scale[i] * total

        own = (lane >= start) & (lane < start + STRIP)
        entered = jnp.where(own, jnp.where(lane - start == level, 1.0, 0.0), strip)
        done = jnp.zeros_like(strip)
        for k in range(STRIP):
            t_column = jnp.zeros((STRIP, LANES), jnp.float32)
            for i in range(k, STRIP):
                t_column = jnp.where(low == i, t[i][k], t_column)
            done = done + halves(t_column) * row(entered, k)
        inverse_ref[pl.ds(pl.multiple_of(start, STRIP), STRIP), :] = jnp.where(lane < start + STRIP, done, 0.0)

        following = jnp.minimum(start + STRIP, size - STRIP)
        coming = state_ref[pl.ds(pl.multiple_of(following, STRIP), STRIP), :]
        near = part(coming)
        columns = [column(near, base + k) for k in range(STRIP)]
        update = jnp.zeros_like(strip)
        for k in range(STRIP):
            l_column = columns[0] * t[k][0]
            for j in range(1, k + 1):
                l_column = l_column + columns[j] * t[k][j]
            update = update + halves(l_column) * row(done, k)
        return jnp.where(own, 0.0, coming) - update, done

    first = state_ref[0:STRIP, :]
    lax.fori_loop(0, size // STRIP, body, (first, jnp.zeros_like(first)))
    weight_ref[...] = lax.dot_general(
        inverse_ref[...],
        coeff_ref[...],
        (((0,), (0,)), ((), ())),
        precision=lax.Precision.HIGHEST,
        preferred_element_type=jnp.float32,
    )


def invert_factor(pivots, coeffs):
    size = pivots.shape[0]
    return pl.pallas_call(
        invert_factor_kernel,
        out_shape=(
            jax.ShapeDtypeStruct((size, size), jnp.float32),
            jax.ShapeDtypeStruct(coeffs.shape, jnp.float32),
        ),
        in_specs=[pl.BlockSpec(memory_space=pltpu.VMEM)] * 2,
        out_specs=(pl.BlockSpec(memory_space=pltpu.VMEM),) * 2,
        scratch_shapes=[pltpu.VMEM((size, size), jnp.float32)],
        cost_estimate=pl.CostEstimate(flops=size * size * size * 6, bytes_accessed=size * size * 4, transcendentals=size * size),
        name="invert_factor",
    )(pivots, coeffs)


def from_owners(picked, owners):
    outer, inner = lax.axis_size("gx"), lax.axis_size("gy")
    rounds = picked.reshape(2, PIVOTS, -1)

    def owned(offered, places):
        return jnp.stack([lax.dynamic_index_in_dim(offered, places[r], 0, keepdims=False)[r] for r in range(2)])

    if outer * inner <= 64:
        kept = owned(lax.all_gather(rounds, ("gx", "gy")), owners)
    else:
        kept = owned(lax.all_gather(rounds, "gy"), lax.rem(owners, inner))
        kept = owned(lax.all_gather(kept, "gx"), lax.div(owners, inner))
    return kept.reshape(picked.shape)


def column_blocks(value):
    return lax.all_gather(value, "gy", axis=0, tiled=True)


def crossing(value, count):
    outer, inner = lax.axis_size("gx"), lax.axis_size("gy")
    z = lax.axis_index("gy")
    pair = jnp.where(z < 2, value[2 * count:], value[:2 * count])
    order = (1, 0, 3, 2)
    single = lax.dynamic_slice_in_dim(value, jnp.where(z < 2, 1 - z, 5 - z) * count, count, 0)

    def send(piece, before):
        pairs = []
        for x in range(outer):
            for place in range(inner):
                source = (x - 1 if place in before else x + 1) % outer
                pairs.append((source * inner + place, x * inner + place))
        return lax.ppermute(piece, ("gx", "gy"), pairs)

    return [send(pair, (0, 1)), send(single, (0, 2))]


def band(value, tall):
    count = value.shape[0]
    if not tall:
        return [value] + [shifted(value, ("gx", "gy"), k) for k in range(-BAND, BAND + 1) if k != 0]
    whole = column_blocks(value)
    return [whole] + crossing(whole, count)


def shards(points, pivots, owners, coeffs, noise):
    hp = lax.Precision.HIGHEST
    count, width = points.shape
    tall = lax.axis_size("gy") == BAND + 1

    index = lax.broadcasted_iota(jnp.int32, (2, PIVOTS, count), 2)
    chosen = (index == pivots[:, :, None]).astype(jnp.bfloat16).reshape(2 * PIVOTS, count)
    picked = jnp.dot(chosen, points, preferred_element_type=jnp.float32).astype(jnp.bfloat16)
    pivot_points = from_owners(picked, owners)
    near_points = band(points, tall)

    inverse, weights = invert_factor(pivot_points, coeffs)
    cols = kern(points, pivot_points)
    probes = jnp.dot(cols, weights, precision=hp, preferred_element_type=jnp.float32) + noise
    sent = probes.astype(jnp.bfloat16)
    near_probes = band(sent, tall)
    factor = jnp.dot(cols, inverse.T, precision=hp, preferred_element_type=jnp.float32)

    total = jnp.zeros((count, probes.shape[1]), jnp.float32)
    for other, probe in zip(near_points, near_probes):
        tile = kern(points, other).astype(jnp.bfloat16)
        total = total + jnp.dot(tile, probe, preferred_element_type=jnp.float32)
    kernel_probes = total / jnp.sqrt(1.0 * count) + noise_weight * probes
    return (kernel_probes, factor)


def solution(mesh):
    in_specs = (P(("gx", "gy"), None), P(), P(), P(), P(("gx", "gy"), None))
    out_specs = (P(("gx", "gy"), None), P(("gx", "gy"), None))
    return jax.shard_map(shards, mesh=mesh, in_specs=in_specs, out_specs=out_specs, check_vma=False)
```

```python
import jax
import jax.numpy as jnp
from jax import lax
from jax.experimental import pallas as pl
from jax.experimental.pallas import tpu as pltpu
from jax.sharding import PartitionSpec as P

PIVOTS = 128
KERNEL_SCALE = 32
BAND = 3
STRIP = 8
LANES = 128


jitter = 0.1
noise_weight = 0.5


def shifted(value, axis, steps):
    count = lax.axis_size(axis)
    return lax.ppermute(value, axis, [((i + steps) % count, i) for i in range(count)])


def swapped(value, axis, bit):
    return lax.ppermute(value, axis, [(i ^ bit, i) for i in range(lax.axis_size(axis))])


def summed(value, axis):
    bit = 1
    while bit < lax.axis_size(axis):
        value = value + swapped(value, axis, bit)
        bit *= 2
    return value


def kern(left, right):
    left_square_norm = jnp.sum(jnp.square(left.astype(jnp.float32)), axis=1)
    right_square_norm = jnp.sum(jnp.square(right.astype(jnp.float32)), axis=1)
    cross_term = jnp.dot(left, right.T, preferred_element_type=jnp.float32)
    return jnp.exp(
        -(left_square_norm[:, None] + right_square_norm[None, :] - 2.0 * cross_term)
        / (1.0 * KERNEL_SCALE)
    )


def column(strip, lane):
    index = jnp.full(strip.shape, lane, jnp.int32)
    return jnp.take_along_axis(strip, index, axis=1, mode="promise_in_bounds")


def row(strip, i):
    return jnp.broadcast_to(strip[i:i + 1, :], strip.shape)


def halves(value):
    return jnp.concatenate([value, value], axis=1)


def thirds(value):
    high = value.astype(jnp.bfloat16).astype(jnp.float32)
    rest = value - high
    middle = rest.astype(jnp.bfloat16).astype(jnp.float32)
    return high, middle, rest - middle


def invert_factor_kernel(pivot_ref, coeff_ref, inverse_ref, weight_ref, state_ref):
    size = pivot_ref.shape[0]
    pivots = pivot_ref[...]
    cross = lax.dot_general(pivots, pivots, (((1,), (1,)), ((), ())), preferred_element_type=jnp.float32)
    equal = lax.broadcasted_iota(jnp.int32, cross.shape, 0) == lax.broadcasted_iota(jnp.int32, cross.shape, 1)
    diagonal = jnp.where(equal, cross, 0.0)
    norms = jnp.sum(diagonal, axis=1, keepdims=True) + jnp.sum(diagonal, axis=0, keepdims=True)
    state_ref[...] = jnp.exp(-(norms - 2.0 * cross) * (1.0 / KERNEL_SCALE)) + jnp.where(equal, jitter, 0.0)
    lane = lax.broadcasted_iota(jnp.int32, (STRIP, size), 1)
    level = lax.broadcasted_iota(jnp.int32, (STRIP, size), 0)
    low = level[:, :LANES]

    def body(p, carry):
        strip, before = carry
        start = p * STRIP
        base = lax.rem(start, LANES)

        def part(wide):
            return jnp.where(start < LANES, wide[:, :LANES], wide[:, LANES:])

        high, middle, little = thirds(before)
        left = jnp.concatenate([high, high, middle, high, little, middle], axis=0).astype(jnp.bfloat16)
        right = jnp.concatenate([high, middle, high, little, high, middle], axis=0).astype(jnp.bfloat16)
        change = lax.dot_general(left, right, (((0,), (0,)), ((), ())), preferred_element_type=jnp.float32)
        all_lanes = lax.broadcasted_iota(jnp.int32, change.shape, 1)
        cleared = (all_lanes >= start - STRIP) & (all_lanes < start)
        state_ref[...] = jnp.where(cleared, 0.0, state_ref[...]) - change

        near = part(strip)
        columns = [column(near, base + k) for k in range(STRIP)]
        a = [[row(columns[k], i) for k in range(i + 1)] for i in range(STRIP)]
        scale = [None] * STRIP
        for k in range(STRIP):
            scale[k] = lax.rsqrt(a[k][k])
            for i in range(k + 1, STRIP):
                a[i][k] = a[i][k] * scale[k]
            for i in range(k + 1, STRIP):
                for j in range(k + 1, i + 1):
                    a[i][j] = a[i][j] - a[i][k] * a[j][k]
        t = [[None] * STRIP for _ in range(STRIP)]
        for j in range(STRIP):
            t[j][j] = scale[j]
            for i in range(j + 1, STRIP):
                total = a[i][j] * t[j][j]
                for q in range(j + 1, i):
                    total = total + a[i][q] * t[q][j]
                t[i][j] = -scale[i] * total

        own = (lane >= start) & (lane < start + STRIP)
        entered = jnp.where(own, jnp.where(lane - start == level, 1.0, 0.0), strip)
        done = jnp.zeros_like(strip)
        for k in range(STRIP):
            t_column = jnp.zeros((STRIP, LANES), jnp.float32)
            for i in range(k, STRIP):
                t_column = jnp.where(low == i, t[i][k], t_column)
            done = done + halves(t_column) * row(entered, k)
        inverse_ref[pl.ds(pl.multiple_of(start, STRIP), STRIP), :] = jnp.where(lane < start + STRIP, done, 0.0)

        following = jnp.minimum(start + STRIP, size - STRIP)
        coming = state_ref[pl.ds(pl.multiple_of(following, STRIP), STRIP), :]
        near = part(coming)
        columns = [column(near, base + k) for k in range(STRIP)]
        update = jnp.zeros_like(strip)
        for k in range(STRIP):
            l_column = columns[0] * t[k][0]
            for j in range(1, k + 1):
                l_column = l_column + columns[j] * t[k][j]
            update = update + halves(l_column) * row(done, k)
        return jnp.where(own, 0.0, coming) - update, done

    first = state_ref[0:STRIP, :]
    lax.fori_loop(0, size // STRIP, body, (first, jnp.zeros_like(first)))
    weight_ref[...] = lax.dot_general(
        inverse_ref[...],
        coeff_ref[...],
        (((0,), (0,)), ((), ())),
        precision=lax.Precision.HIGHEST,
        preferred_element_type=jnp.float32,
    )


def invert_factor(pivots, coeffs):
    size = pivots.shape[0]
    return pl.pallas_call(
        invert_factor_kernel,
        out_shape=(
            jax.ShapeDtypeStruct((size, size), jnp.float32),
            jax.ShapeDtypeStruct(coeffs.shape, jnp.float32),
        ),
        in_specs=[pl.BlockSpec(memory_space=pltpu.VMEM)] * 2,
        out_specs=(pl.BlockSpec(memory_space=pltpu.VMEM),) * 2,
        scratch_shapes=[pltpu.VMEM((size, size), jnp.float32)],
        cost_estimate=pl.CostEstimate(flops=size * size * size * 6, bytes_accessed=size * size * 4, transcendentals=size * size),
        name="invert_factor",
    )(pivots, coeffs)


def neighbours(value, tall):
    outer, inner = lax.axis_size("gx"), lax.axis_size("gy")
    if not tall:
        return [shifted(value, ("gx", "gy"), k) for k in range(-BAND, BAND + 1) if k != 0]

    def cross(piece, bits):
        pairs = []
        for x in range(outer):
            for z in range(inner):
                source = (x - 1 if z ^ bits > z else x + 1) % outer
                pairs.append((source * inner + z, x * inner + z))
        return lax.ppermute(piece, ("gx", "gy"), pairs)

    two = swapped(value, "gy", 2)
    one = swapped(value, "gy", 1)
    three = swapped(two, "gy", 1)
    return [one, two, cross(one, 1), cross(two, 2), three, cross(three, 3)]


def shards(points, pivots, owners, coeffs, noise):
    hp = lax.Precision.HIGHEST
    count, width = points.shape
    tall = lax.axis_size("gy") == BAND + 1
    me = lax.axis_index(("gx", "gy"))

    index = lax.broadcasted_iota(jnp.int32, (2, PIVOTS, count), 2)
    wanted = jnp.where((owners == me)[:, None], pivots, -1)
    chosen = (index == wanted[:, :, None]).astype(jnp.bfloat16).reshape(2 * PIVOTS, count)
    picked = jnp.dot(chosen, points, preferred_element_type=jnp.float32).astype(jnp.bfloat16)
    picked, settled = lax.optimization_barrier((summed(picked, "gy"), points))
    pivot_points = summed(picked, "gx")
    near_points = neighbours(settled, tall)

    inverse, weights = invert_factor(pivot_points, coeffs)
    cols = kern(points, pivot_points)
    probes = jnp.dot(cols, weights, precision=hp, preferred_element_type=jnp.float32) + noise
    sent = probes.astype(jnp.bfloat16)
    near_probes = neighbours(sent, tall)
    factor = jnp.dot(cols, inverse.T, precision=hp, preferred_element_type=jnp.float32)

    total = jnp.zeros((count, probes.shape[1]), jnp.float32)
    for other, probe in zip([points] + near_points, [sent] + near_probes):
        tile = kern(points, other).astype(jnp.bfloat16)
        total = total + jnp.dot(tile, probe, preferred_element_type=jnp.float32)
    kernel_probes = total / jnp.sqrt(1.0 * count) + noise_weight * probes
    return (kernel_probes, factor)


def solution(mesh):
    in_specs = (P(("gx", "gy"), None), P(), P(), P(), P(("gx", "gy"), None))
    out_specs = (P(("gx", "gy"), None), P(("gx", "gy"), None))
    return jax.shard_map(shards, mesh=mesh, in_specs=in_specs, out_specs=out_specs, check_vma=False)
```

```python
import jax
import jax.numpy as jnp
from jax import lax
from jax.experimental import pallas as pl
from jax.experimental.pallas import tpu as pltpu
from jax.sharding import PartitionSpec as P

PIVOTS = 128
KERNEL_SCALE = 32
BAND = 3
STRIP = 8
LANES = 128


jitter = 0.1
noise_weight = 0.5


def shifted(value, axis, steps):
    count = lax.axis_size(axis)
    return lax.ppermute(value, axis, [((i + steps) % count, i) for i in range(count)])


def swapped(value, axis, bit):
    return lax.ppermute(value, axis, [(i ^ bit, i) for i in range(lax.axis_size(axis))])


def summed(value, axis):
    copies = jnp.broadcast_to(value, (lax.axis_size(axis),) + value.shape)
    return jnp.sum(lax.all_to_all(copies, axis, 0, 0), axis=0, dtype=value.dtype)


def kern(left, right):
    left_square_norm = jnp.sum(jnp.square(left.astype(jnp.float32)), axis=1)
    right_square_norm = jnp.sum(jnp.square(right.astype(jnp.float32)), axis=1)
    cross_term = jnp.dot(left, right.T, preferred_element_type=jnp.float32)
    return jnp.exp(
        -(left_square_norm[:, None] + right_square_norm[None, :] - 2.0 * cross_term)
        / (1.0 * KERNEL_SCALE)
    )


def column(strip, lane):
    index = jnp.full(strip.shape, lane, jnp.int32)
    return jnp.take_along_axis(strip, index, axis=1, mode="promise_in_bounds")


def row(strip, i):
    return jnp.broadcast_to(strip[i:i + 1, :], strip.shape)


def halves(value):
    return jnp.concatenate([value, value], axis=1)


def thirds(value):
    high = value.astype(jnp.bfloat16).astype(jnp.float32)
    rest = value - high
    middle = rest.astype(jnp.bfloat16).astype(jnp.float32)
    return high, middle, rest - middle


def invert_factor_kernel(pivot_ref, coeff_ref, inverse_ref, weight_ref, state_ref):
    size = pivot_ref.shape[0]
    pivots = pivot_ref[...]
    cross = lax.dot_general(pivots, pivots, (((1,), (1,)), ((), ())), preferred_element_type=jnp.float32)
    equal = lax.broadcasted_iota(jnp.int32, cross.shape, 0) == lax.broadcasted_iota(jnp.int32, cross.shape, 1)
    diagonal = jnp.where(equal, cross, 0.0)
    norms = jnp.sum(diagonal, axis=1, keepdims=True) + jnp.sum(diagonal, axis=0, keepdims=True)
    state_ref[...] = jnp.exp(-(norms - 2.0 * cross) * (1.0 / KERNEL_SCALE)) + jnp.where(equal, jitter, 0.0)
    lane = lax.broadcasted_iota(jnp.int32, (STRIP, size), 1)
    level = lax.broadcasted_iota(jnp.int32, (STRIP, size), 0)
    low = level[:, :LANES]

    def body(p, carry):
        strip, before = carry
        start = p * STRIP
        base = lax.rem(start, LANES)

        def part(wide):
            return jnp.where(start < LANES, wide[:, :LANES], wide[:, LANES:])

        high, middle, little = thirds(before)
        left = jnp.concatenate([high, high, middle, high, little, middle], axis=0).astype(jnp.bfloat16)
        right = jnp.concatenate([high, middle, high, little, high, middle], axis=0).astype(jnp.bfloat16)
        change = lax.dot_general(left, right, (((0,), (0,)), ((), ())), preferred_element_type=jnp.float32)
        all_lanes = lax.broadcasted_iota(jnp.int32, change.shape, 1)
        cleared = (all_lanes >= start - STRIP) & (all_lanes < start)
        state_ref[...] = jnp.where(cleared, 0.0, state_ref[...]) - change

        near = part(strip)
        columns = [column(near, base + k) for k in range(STRIP)]
        a = [[row(columns[k], i) for k in range(i + 1)] for i in range(STRIP)]
        scale = [None] * STRIP
        for k in range(STRIP):
            scale[k] = lax.rsqrt(a[k][k])
            for i in range(k + 1, STRIP):
                a[i][k] = a[i][k] * scale[k]
            for i in range(k + 1, STRIP):
                for j in range(k + 1, i + 1):
                    a[i][j] = a[i][j] - a[i][k] * a[j][k]
        t = [[None] * STRIP for _ in range(STRIP)]
        for j in range(STRIP):
            t[j][j] = scale[j]
            for i in range(j + 1, STRIP):
                total = a[i][j] * t[j][j]
                for q in range(j + 1, i):
                    total = total + a[i][q] * t[q][j]
                t[i][j] = -scale[i] * total

        own = (lane >= start) & (lane < start + STRIP)
        entered = jnp.where(own, jnp.where(lane - start == level, 1.0, 0.0), strip)
        done = jnp.zeros_like(strip)
        for k in range(STRIP):
            t_column = jnp.zeros((STRIP, LANES), jnp.float32)
            for i in range(k, STRIP):
                t_column = jnp.where(low == i, t[i][k], t_column)
            done = done + halves(t_column) * row(entered, k)
        inverse_ref[pl.ds(pl.multiple_of(start, STRIP), STRIP), :] = jnp.where(lane < start + STRIP, done, 0.0)

        following = jnp.minimum(start + STRIP, size - STRIP)
        coming = state_ref[pl.ds(pl.multiple_of(following, STRIP), STRIP), :]
        near = part(coming)
        columns = [column(near, base + k) for k in range(STRIP)]
        update = jnp.zeros_like(strip)
        for k in range(STRIP):
            l_column = columns[0] * t[k][0]
            for j in range(1, k + 1):
                l_column = l_column + columns[j] * t[k][j]
            update = update + halves(l_column) * row(done, k)
        return jnp.where(own, 0.0, coming) - update, done

    first = state_ref[0:STRIP, :]
    lax.fori_loop(0, size // STRIP, body, (first, jnp.zeros_like(first)))
    weight_ref[...] = lax.dot_general(
        inverse_ref[...],
        coeff_ref[...],
        (((0,), (0,)), ((), ())),
        precision=lax.Precision.HIGHEST,
        preferred_element_type=jnp.float32,
    )


def invert_factor(pivots, coeffs):
    size = pivots.shape[0]
    return pl.pallas_call(
        invert_factor_kernel,
        out_shape=(
            jax.ShapeDtypeStruct((size, size), jnp.float32),
            jax.ShapeDtypeStruct(coeffs.shape, jnp.float32),
        ),
        in_specs=[pl.BlockSpec(memory_space=pltpu.VMEM)] * 2,
        out_specs=(pl.BlockSpec(memory_space=pltpu.VMEM),) * 2,
        scratch_shapes=[pltpu.VMEM((size, size), jnp.float32)],
        cost_estimate=pl.CostEstimate(flops=size * size * size * 6, bytes_accessed=size * size * 4, transcendentals=size * size),
        name="invert_factor",
    )(pivots, coeffs)


def neighbours(value, tall):
    outer, inner = lax.axis_size("gx"), lax.axis_size("gy")
    if not tall:
        return [shifted(value, ("gx", "gy"), k) for k in range(-BAND, BAND + 1) if k != 0]

    def cross(piece, bits):
        pairs = []
        for x in range(outer):
            for z in range(inner):
                source = (x - 1 if z ^ bits > z else x + 1) % outer
                pairs.append((source * inner + z, x * inner + z))
        return lax.ppermute(piece, ("gx", "gy"), pairs)

    two = swapped(value, "gy", 2)
    one = swapped(value, "gy", 1)
    three = swapped(two, "gy", 1)
    return [one, two, cross(one, 1), cross(two, 2), three, cross(three, 3)]


def shards(points, pivots, owners, coeffs, noise):
    hp = lax.Precision.HIGHEST
    count, width = points.shape
    tall = lax.axis_size("gy") == BAND + 1
    me = lax.axis_index(("gx", "gy"))

    index = lax.broadcasted_iota(jnp.int32, (2, PIVOTS, count), 2)
    wanted = jnp.where((owners == me)[:, None], pivots, -1)
    chosen = (index == wanted[:, :, None]).astype(jnp.bfloat16).reshape(2 * PIVOTS, count)
    picked = jnp.dot(chosen, points, preferred_element_type=jnp.float32).astype(jnp.bfloat16)
    picked, settled = lax.optimization_barrier((summed(picked, "gy"), points))
    pivot_points = summed(picked, "gx")
    near_points = neighbours(settled, tall)

    inverse, weights = invert_factor(pivot_points, coeffs)
    cols = kern(points, pivot_points)
    probes = jnp.dot(cols, weights, precision=hp, preferred_element_type=jnp.float32) + noise
    sent = probes.astype(jnp.bfloat16)
    near_probes = neighbours(sent, tall)
    factor = jnp.dot(cols, inverse.T, precision=hp, preferred_element_type=jnp.float32)

    total = jnp.zeros((count, probes.shape[1]), jnp.float32)
    for other, probe in zip([points] + near_points, [sent] + near_probes):
        tile = kern(points, other).astype(jnp.bfloat16)
        total = total + jnp.dot(tile, probe, preferred_element_type=jnp.float32)
    kernel_probes = total / jnp.sqrt(1.0 * count) + noise_weight * probes
    return (kernel_probes, factor)


def solution(mesh):
    in_specs = (P(("gx", "gy"), None), P(), P(), P(), P(("gx", "gy"), None))
    out_specs = (P(("gx", "gy"), None), P(("gx", "gy"), None))
    return jax.shard_map(shards, mesh=mesh, in_specs=in_specs, out_specs=out_specs, check_vma=False)
```

```python
import functools

import jax
import jax.numpy as jnp
from jax import lax
from jax.experimental import pallas as pl
from jax.experimental.pallas import tpu as pltpu
from jax.sharding import PartitionSpec as P

PIVOTS = 128
KERNEL_SCALE = 32
BAND = 3
STRIP = 8
LANES = 128
EXTRA = 16
CHUNK = 256


jitter = 0.1
noise_weight = 0.5


def shifted(value, axis, steps):
    count = lax.axis_size(axis)
    return lax.ppermute(value, axis, [((i + steps) % count, i) for i in range(count)])


def swapped(value, axis, bit):
    return lax.ppermute(value, axis, [(i ^ bit, i) for i in range(lax.axis_size(axis))])


def summed(value, axis):
    bit = 1
    while bit < lax.axis_size(axis):
        value = value + swapped(value, axis, bit)
        bit *= 2
    return value


def neighbours(value, tall):
    outer, inner = lax.axis_size("gx"), lax.axis_size("gy")
    if not tall:
        return [shifted(value, ("gx", "gy"), k) for k in range(-BAND, BAND + 1) if k != 0]

    def cross(piece, bits):
        pairs = []
        for x in range(outer):
            for z in range(inner):
                source = (x - 1 if z ^ bits > z else x + 1) % outer
                pairs.append((source * inner + z, x * inner + z))
        return lax.ppermute(piece, ("gx", "gy"), pairs)

    two = swapped(value, "gy", 2)
    one = swapped(value, "gy", 1)
    three = swapped(two, "gy", 1)
    return [one, two, cross(one, 1), cross(two, 2), three, cross(three, 3)]


def in_vmem(count):
    return [pl.BlockSpec(memory_space=pltpu.VMEM)] * count


def thirds(value):
    high = value.astype(jnp.bfloat16)
    rest = value - high.astype(jnp.float32)
    middle = rest.astype(jnp.bfloat16)
    return high, middle, (rest - middle.astype(jnp.float32)).astype(jnp.bfloat16)


def product(left, right, contract, precision=None):
    return lax.dot_general(
        left, right, (contract, ((), ())), precision=precision, preferred_element_type=jnp.float32
    )


def extended(columns, ones_first):
    wide = columns.astype(jnp.float32)
    half = -0.5 * jnp.sum(wide * wide, axis=0, keepdims=True)
    terms = [term.astype(jnp.float32) for term in thirds(half)]
    shape = (EXTRA, columns.shape[1])
    level = lax.broadcasted_iota(jnp.int32, shape, 0)
    first = 0 if ones_first else 3
    below = jnp.where((level >= first) & (level < first + 3), 1.0, 0.0)
    for i, term in enumerate(terms):
        below = jnp.where(level == 3 - first + i, jnp.broadcast_to(term, shape), below)
    return jnp.concatenate([wide, below], axis=0)


def kernel_of(product_of_extended):
    return jnp.exp(product_of_extended * (2.0 / KERNEL_SCALE))


def pick_kernel(owner_ref, pivot_ref, point_ref, out_ref):
    count = point_ref.shape[1]
    wanted = [jnp.where(owner_ref[r] == owner_ref[2], pivot_ref[r:r + 1, :], -1) for r in range(2)]
    wanted = jnp.concatenate(wanted, axis=1)
    place = lax.broadcasted_iota(jnp.int32, (count, wanted.shape[1]), 0)
    chosen = jnp.where(place == wanted, 1.0, 0.0).astype(jnp.bfloat16)
    out_ref[...] = product(point_ref[...], chosen, ((1,), (0,))).astype(jnp.bfloat16)


def pick(owners, pivots, points_t):
    return pl.pallas_call(
        pick_kernel,
        out_shape=jax.ShapeDtypeStruct((points_t.shape[0], 2 * PIVOTS), jnp.bfloat16),
        in_specs=[pl.BlockSpec(memory_space=pltpu.SMEM)] + in_vmem(2),
        out_specs=in_vmem(1)[0],
        name="pick",
    )(owners, pivots, points_t)


def column(strip, lane):
    return jnp.broadcast_to(strip[:, lane:lane + 1], strip.shape)


def row(strip, i):
    return jnp.broadcast_to(strip[i:i + 1, :], strip.shape)


def small_inverse(strip, start):
    columns = [column(strip, start + k) for k in range(STRIP)]
    a = [[row(columns[k], i) for k in range(i + 1)] for i in range(STRIP)]
    scale = [None] * STRIP
    for k in range(STRIP):
        scale[k] = lax.rsqrt(a[k][k])
        for i in range(k + 1, STRIP):
            a[i][k] = a[i][k] * scale[k]
        for i in range(k + 1, STRIP):
            for j in range(k + 1, i + 1):
                a[i][j] = a[i][j] - a[i][k] * a[j][k]
    t = [[None] * STRIP for _ in range(STRIP)]
    for j in range(STRIP):
        t[j][j] = scale[j]
        for i in range(j + 1, STRIP):
            total = a[i][j] * t[j][j]
            for q in range(j + 1, i):
                total = total + a[i][q] * t[q][j]
            t[i][j] = -scale[i] * total
    return t


def inverse_factor(strips):
    lane = lax.broadcasted_iota(jnp.int32, (STRIP, LANES), 1)
    level = lax.broadcasted_iota(jnp.int32, (STRIP, LANES), 0)
    strips = list(strips)
    result = []
    for p in range(len(strips)):
        start = p * STRIP
        t = small_inverse(strips[p], start)
        own = (lane >= start) & (lane < start + STRIP)
        entered = jnp.where(own, jnp.where(lane - start == level, 1.0, 0.0), strips[p])
        done = None
        for k in range(STRIP):
            t_column = t[STRIP - 1][k]
            for i in range(STRIP - 2, k - 1, -1):
                t_column = jnp.where(level == i, t[i][k], t_column)
            if k:
                t_column = jnp.where(level < k, 0.0, t_column)
            term = t_column * row(entered, k)
            done = term if done is None else done + term
        result.append(jnp.where(lane < start + STRIP, done, 0.0))
        rows = [row(done, k) for k in range(STRIP)]
        for r in range(p + 1, len(strips)):
            columns = [column(strips[r], start + j) for j in range(STRIP)]
            update = None
            for k in range(STRIP):
                l_column = columns[0] * t[k][0]
                for j in range(1, k + 1):
                    l_column = l_column + columns[j] * t[k][j]
                term = l_column * rows[k]
                update = term if update is None else update + term
            strips[r] = jnp.where(own, 0.0, strips[r]) - update
    return result


def probe_kernel(
    pivot_ref, point_ref, coeff_ref, noise_ref, inverse_ref, probe_ref, sent_ref, high_ref, middle_ref, little_ref
):
    hp = lax.Precision.HIGHEST
    size = pivot_ref.shape[1]
    half = size // 2
    pivots = extended(pivot_ref[...], True).astype(jnp.bfloat16)
    others = extended(pivot_ref[...], False).astype(jnp.bfloat16)
    points = extended(point_ref[...], False).astype(jnp.bfloat16)
    cols = kernel_of(product(pivots, points, ((0,), (0,))))
    high_ref[...], middle_ref[...], little_ref[...] = thirds(cols)

    gram = kernel_of(product(pivots, others, ((0,), (0,))))
    equal = lax.broadcasted_iota(jnp.int32, gram.shape, 0) == lax.broadcasted_iota(jnp.int32, gram.shape, 1)
    gram = gram + jnp.where(equal, jitter, 0.0)

    def inverted(block):
        strips = [block[s:s + STRIP, :] for s in range(0, half, STRIP)]
        return jnp.concatenate(inverse_factor(strips), axis=0)

    one = inverted(gram[:half, :half])
    below = product(gram[half:, :half], one, ((1,), (1,)), hp)
    back = product(below, one, ((1,), (0,)), hp)
    two = inverted(gram[half:, half:] - product(below, below, ((1,), (1,)), hp))
    coeffs = coeff_ref[...]
    start = product(coeffs[:, :half], one, ((1,), (0,)), hp)
    later = product(coeffs[:, half:], two, ((1,), (0,)), hp)
    weights = jnp.concatenate([start - product(later, back, ((1,), (0,)), hp), later], axis=1)

    rows = weights.shape[0]
    stacked = jnp.concatenate(thirds(weights), axis=0)
    by_high = product(stacked, high_ref[...], ((1,), (0,)))
    by_middle = product(stacked[:2 * rows], middle_ref[...], ((1,), (0,)))
    by_little = product(stacked[:rows], little_ref[...], ((1,), (0,)))
    small = by_high[2 * rows:] + by_middle[rows:] + by_little
    probes = by_high[:rows] + (by_high[rows:2 * rows] + by_middle[:rows] + small) + noise_ref[...]
    probe_ref[...] = probes
    sent_ref[...] = probes.astype(jnp.bfloat16)

    inverse_ref[:half, :half] = one
    inverse_ref[:half, half:] = jnp.zeros((half, half), jnp.float32)
    inverse_ref[half:, :half] = -product(two, back, ((1,), (0,)), hp)
    inverse_ref[half:, half:] = two


def probes_of(pivots_t, points_t, coeffs_t, noise_t):
    size = pivots_t.shape[1]
    count = points_t.shape[1]
    return pl.pallas_call(
        probe_kernel,
        out_shape=(
            jax.ShapeDtypeStruct((size, size), jnp.float32),
            jax.ShapeDtypeStruct(noise_t.shape, jnp.float32),
            jax.ShapeDtypeStruct(noise_t.shape, jnp.bfloat16),
        ),
        in_specs=in_vmem(4),
        out_specs=tuple(in_vmem(3)),
        scratch_shapes=[pltpu.VMEM((size, count), jnp.bfloat16)] * 3,
        compiler_params=pltpu.CompilerParams(vmem_limit_bytes=32 * 1024 * 1024),
        name="probes",
    )(pivots_t, points_t, coeffs_t, noise_t)


def factor_kernel(pivot_ref, point_ref, inverse_ref, factor_ref):
    pivots = extended(pivot_ref[...], True).astype(jnp.bfloat16)
    points = extended(point_ref[...], False).astype(jnp.bfloat16)
    cols = kernel_of(product(points, pivots, ((0,), (0,))))
    factor_ref[...] = product(cols, inverse_ref[...], ((1,), (1,)), lax.Precision.HIGHEST)


def factor_of(pivots_t, points_t, inverse):
    size = pivots_t.shape[1]
    count = points_t.shape[1]
    return pl.pallas_call(
        factor_kernel,
        out_shape=jax.ShapeDtypeStruct((count, size), jnp.float32),
        in_specs=in_vmem(3),
        out_specs=in_vmem(1)[0],
        compiler_params=pltpu.CompilerParams(vmem_limit_bytes=32 * 1024 * 1024),
        cost_estimate=pl.CostEstimate(flops=12 * count * size * size, bytes_accessed=4 * count * size, transcendentals=count * size),
        name="factor",
    )(pivots_t, points_t, inverse)


def band_kernel(pieces, first, last, *refs):
    own_ref = refs[0]
    piece_refs = refs[1:1 + 2 * pieces]
    at = 1 + 2 * pieces
    total_ref = out_ref = refs[-1]
    count = own_ref.shape[1]
    before_ref = None
    if not first:
        before_ref = refs[at]
        at += 1
    if last:
        probe_ref = refs[at]
    own = extended(own_ref[...], True)
    own = jnp.concatenate([own, jnp.zeros((LANES - own.shape[0], count), jnp.float32)], axis=0)
    own = jnp.transpose(own).astype(jnp.bfloat16)
    others = []
    for i in range(pieces):
        other = extended(piece_refs[2 * i][...], False)
        other = jnp.concatenate([other, jnp.zeros((LANES - other.shape[0], count), jnp.float32)], axis=0)
        others.append(other.astype(jnp.bfloat16))
    for s in range(0, count, CHUNK):
        total = None if first else before_ref[s:s + CHUNK, :]
        for i in range(pieces):
            tile = kernel_of(product(own[s:s + CHUNK, :], others[i], ((1,), (0,)))).astype(jnp.bfloat16)
            term = product(tile, piece_refs[2 * i + 1][...], ((1,), (1,)))
            total = term if total is None else total + term
        if last:
            scale = 1.0 / (count ** 0.5)
            out_ref[:, s:s + CHUNK] = jnp.transpose(total) * scale + noise_weight * probe_ref[:, s:s + CHUNK]
        else:
            total_ref[s:s + CHUNK, :] = total


def band_sum(own, pieces, before=None, probes=None):
    depth, count = own.shape
    width = pieces[0][1].shape[0]
    first, last = before is None, probes is not None
    operands = [own] + [array for piece in pieces for array in piece]
    operands += ([] if first else [before]) + ([probes] if last else [])
    return pl.pallas_call(
        functools.partial(band_kernel, len(pieces), first, last),
        out_shape=jax.ShapeDtypeStruct((width, count) if last else (count, width), jnp.float32),
        in_specs=in_vmem(len(operands)),
        out_specs=in_vmem(1)[0],
        compiler_params=pltpu.CompilerParams(vmem_limit_bytes=32 * 1024 * 1024),
        cost_estimate=pl.CostEstimate(
            flops=len(pieces) * 4 * count * count * LANES,
            bytes_accessed=4 * count * width * len(operands),
            transcendentals=len(pieces) * count * count,
        ),
        name="band_sum",
    )(*operands)


def shards(points, pivots, owners, coeffs, noise):
    tall = lax.axis_size("gy") == BAND + 1
    points = points.T
    me = lax.axis_index(("gx", "gy"))
    picked = pick(jnp.concatenate([owners, jnp.reshape(me, (1,))]), pivots, points)
    picked, settled = lax.optimization_barrier((summed(picked, "gy"), points))
    pivot_points = summed(picked, "gx")
    near_points = neighbours(settled, tall)

    inverse, probes, sent = probes_of(pivot_points, points, coeffs.T, noise.T)
    near_probes = neighbours(sent, tall)
    factor = factor_of(pivot_points, points, inverse)
    near = list(zip(near_points, near_probes))
    total = band_sum(points, [(points, sent)])
    total = band_sum(points, near[:2], total)
    total = band_sum(points, near[2:4], total)
    kernel_probes = band_sum(points, near[4:], total, probes).T
    return (kernel_probes, factor)


def solution(mesh):
    in_specs = (P(("gx", "gy"), None), P(), P(), P(), P(("gx", "gy"), None))
    out_specs = (P(("gx", "gy"), None), P(("gx", "gy"), None))
    return jax.shard_map(shards, mesh=mesh, in_specs=in_specs, out_specs=out_specs, check_vma=False)
```

```python
import functools

import jax
import jax.numpy as jnp
from jax import lax
from jax.experimental import pallas as pl
from jax.experimental.pallas import tpu as pltpu
from jax.sharding import PartitionSpec as P

PIVOTS = 128
KERNEL_SCALE = 32
BAND = 3
STRIP = 8
LANES = 128
EXTRA = 16
CHUNK = 256


jitter = 0.1
noise_weight = 0.5


def shifted(value, axis, steps):
    count = lax.axis_size(axis)
    return lax.ppermute(value, axis, [((i + steps) % count, i) for i in range(count)])


def swapped(value, axis, bit):
    return lax.ppermute(value, axis, [(i ^ bit, i) for i in range(lax.axis_size(axis))])


def after(value, *others):
    return lax.optimization_barrier((value,) + others)[0]


def spread(value):
    sums = [value]
    for axis in ("gx", "gy"):
        bits = [1 << i for i in range(lax.axis_size(axis).bit_length() - 1)]
        for bit in bits if axis == "gx" else bits[::-1]:
            sums.append(sums[-1] + swapped(sums[-1], axis, bit))
    return sums[1:]


def cross(piece, bits):
    outer, inner = lax.axis_size("gx"), lax.axis_size("gy")
    pairs = []
    for x in range(outer):
        for z in range(inner):
            source = (x - 1 if z ^ bits > z else x + 1) % outer
            pairs.append((source * inner + z, x * inner + z))
    return lax.ppermute(piece, ("gx", "gy"), pairs)


def neighbours(value, steps=()):
    if lax.axis_size("gy") != BAND + 1:
        return [shifted(value, ("gx", "gy"), k) for k in range(-BAND, BAND + 1) if k != 0]

    def at(piece, step):
        return after(piece, steps[min(step, len(steps) - 1)]) if steps else piece

    two = swapped(value, "gy", 2)
    one = swapped(at(value, 0), "gy", 1)
    three = swapped(at(two, 1), "gy", 1)
    cross_one = cross(at(one, 2), 1)
    cross_two = cross(at(two, 3), 2)
    return [one, two, cross_one, cross_two, three, cross(at(three, 4), 3)]


def in_vmem(count):
    return [pl.BlockSpec(memory_space=pltpu.VMEM)] * count


def thirds(value):
    high = value.astype(jnp.bfloat16)
    rest = value - high.astype(jnp.float32)
    middle = rest.astype(jnp.bfloat16)
    return high, middle, (rest - middle.astype(jnp.float32)).astype(jnp.bfloat16)


def product(left, right, contract, precision=None):
    return lax.dot_general(
        left, right, (contract, ((), ())), precision=precision, preferred_element_type=jnp.float32
    )


def extended(columns, ones_first):
    wide = columns.astype(jnp.float32)
    half = -0.5 * jnp.sum(wide * wide, axis=0, keepdims=True)
    terms = [term.astype(jnp.float32) for term in thirds(half)]
    shape = (EXTRA, columns.shape[1])
    level = lax.broadcasted_iota(jnp.int32, shape, 0)
    first = 0 if ones_first else 3
    below = jnp.where((level >= first) & (level < first + 3), 1.0, 0.0)
    for i, term in enumerate(terms):
        below = jnp.where(level == 3 - first + i, jnp.broadcast_to(term, shape), below)
    return jnp.concatenate([wide, below], axis=0)


def kernel_of(product_of_extended):
    return jnp.exp(product_of_extended * (2.0 / KERNEL_SCALE))


def pick_kernel(owner_ref, pivot_ref, point_ref, out_ref):
    count = point_ref.shape[1]
    me = lax.axis_index(("gx", "gy"))
    wanted = [jnp.where(owner_ref[r] == me, pivot_ref[r:r + 1, :], -1) for r in range(2)]
    wanted = jnp.concatenate(wanted, axis=1)
    place = lax.broadcasted_iota(jnp.int32, (count, wanted.shape[1]), 0)
    chosen = jnp.where(place == wanted, 1.0, 0.0).astype(jnp.bfloat16)
    out_ref[...] = product(point_ref[...], chosen, ((1,), (0,))).astype(jnp.bfloat16)


def pick(owners, pivots, points_t):
    return pl.pallas_call(
        pick_kernel,
        out_shape=jax.ShapeDtypeStruct((points_t.shape[0], 2 * PIVOTS), jnp.bfloat16),
        in_specs=[pl.BlockSpec(memory_space=pltpu.SMEM)] + in_vmem(2),
        out_specs=in_vmem(1)[0],
        name="pick",
    )(owners, pivots, points_t)


def column(strip, lane):
    return jnp.broadcast_to(strip[:, lane:lane + 1], strip.shape)


def row(strip, i):
    return jnp.broadcast_to(strip[i:i + 1, :], strip.shape)


def small_inverse(strip, start):
    columns = [column(strip, start + k) for k in range(STRIP)]
    a = [[row(columns[k], i) for k in range(i + 1)] for i in range(STRIP)]
    scale = [None] * STRIP
    for k in range(STRIP):
        scale[k] = lax.rsqrt(a[k][k])
        for i in range(k + 1, STRIP):
            a[i][k] = a[i][k] * scale[k]
        for i in range(k + 1, STRIP):
            for j in range(k + 1, i + 1):
                a[i][j] = a[i][j] - a[i][k] * a[j][k]
    t = [[None] * STRIP for _ in range(STRIP)]
    for j in range(STRIP):
        t[j][j] = scale[j]
        for i in range(j + 1, STRIP):
            total = a[i][j] * t[j][j]
            for q in range(j + 1, i):
                total = total + a[i][q] * t[q][j]
            t[i][j] = -scale[i] * total
    return t


def inverse_factor(strips):
    lane = lax.broadcasted_iota(jnp.int32, (STRIP, LANES), 1)
    level = lax.broadcasted_iota(jnp.int32, (STRIP, LANES), 0)
    strips = list(strips)
    result = []
    for p in range(len(strips)):
        start = p * STRIP
        t = small_inverse(strips[p], start)
        own = (lane >= start) & (lane < start + STRIP)
        entered = jnp.where(own, jnp.where(lane - start == level, 1.0, 0.0), strips[p])
        done = None
        for k in range(STRIP):
            t_column = t[STRIP - 1][k]
            for i in range(STRIP - 2, k - 1, -1):
                t_column = jnp.where(level == i, t[i][k], t_column)
            if k:
                t_column = jnp.where(level < k, 0.0, t_column)
            term = t_column * row(entered, k)
            done = term if done is None else done + term
        result.append(jnp.where(lane < start + STRIP, done, 0.0))
        rows = [row(done, k) for k in range(STRIP)]
        for r in range(p + 1, len(strips)):
            columns = [column(strips[r], start + j) for j in range(STRIP)]
            update = None
            for k in range(STRIP):
                l_column = columns[0] * t[k][0]
                for j in range(1, k + 1):
                    l_column = l_column + columns[j] * t[k][j]
                term = l_column * rows[k]
                update = term if update is None else update + term
            strips[r] = jnp.where(own, 0.0, strips[r]) - update
    return result


def probe_kernel(pivot_ref, point_ref, coeff_ref, noise_ref, *refs):
    inverse_ref, probe_ref, sent_ref, high_ref, middle_ref, little_ref = refs[-6:]
    hp = lax.Precision.HIGHEST
    size = pivot_ref.shape[1]
    half = size // 2
    pivots = extended(pivot_ref[...], True).astype(jnp.bfloat16)
    others = extended(pivot_ref[...], False).astype(jnp.bfloat16)
    points = extended(point_ref[...], False).astype(jnp.bfloat16)
    cols = kernel_of(product(pivots, points, ((0,), (0,))))
    high_ref[...], middle_ref[...], little_ref[...] = thirds(cols)

    gram = kernel_of(product(pivots, others, ((0,), (0,))))
    equal = lax.broadcasted_iota(jnp.int32, gram.shape, 0) == lax.broadcasted_iota(jnp.int32, gram.shape, 1)
    gram = gram + jnp.where(equal, jitter, 0.0)

    def inverted(block):
        strips = [block[s:s + STRIP, :] for s in range(0, half, STRIP)]
        return jnp.concatenate(inverse_factor(strips), axis=0)

    one = inverted(gram[:half, :half])
    below = product(gram[half:, :half], one, ((1,), (1,)), hp)
    back = product(below, one, ((1,), (0,)), hp)
    two = inverted(gram[half:, half:] - product(below, below, ((1,), (1,)), hp))
    coeffs = coeff_ref[...]
    start = product(coeffs[:, :half], one, ((1,), (0,)), hp)
    later = product(coeffs[:, half:], two, ((1,), (0,)), hp)
    weights = jnp.concatenate([start - product(later, back, ((1,), (0,)), hp), later], axis=1)

    rows = weights.shape[0]
    stacked = jnp.concatenate(thirds(weights), axis=0)
    by_high = product(stacked, high_ref[...], ((1,), (0,)))
    by_middle = product(stacked[:2 * rows], middle_ref[...], ((1,), (0,)))
    by_little = product(stacked[:rows], little_ref[...], ((1,), (0,)))
    small = by_high[2 * rows:] + by_middle[rows:] + by_little
    probes = by_high[:rows] + (by_high[rows:2 * rows] + by_middle[:rows] + small) + noise_ref[...]
    probe_ref[...] = probes
    sent_ref[...] = probes.astype(jnp.bfloat16)

    inverse_ref[:half, :half] = one
    inverse_ref[:half, half:] = jnp.zeros((half, half), jnp.float32)
    inverse_ref[half:, :half] = -product(two, back, ((1,), (0,)), hp)
    inverse_ref[half:, half:] = two


def probes_of(pivots_t, points_t, coeffs_t, noise_t, awaited):
    size = pivots_t.shape[1]
    count = points_t.shape[1]
    return pl.pallas_call(
        probe_kernel,
        out_shape=(
            jax.ShapeDtypeStruct((size, size), jnp.float32),
            jax.ShapeDtypeStruct(noise_t.shape, jnp.float32),
            jax.ShapeDtypeStruct(noise_t.shape, jnp.bfloat16),
        ),
        in_specs=in_vmem(4) + [pl.BlockSpec(memory_space=pl.ANY)] * len(awaited),
        out_specs=tuple(in_vmem(3)),
        scratch_shapes=[pltpu.VMEM((size, count), jnp.bfloat16)] * 3,
        compiler_params=pltpu.CompilerParams(vmem_limit_bytes=32 * 1024 * 1024),
        name="probes",
    )(pivots_t, points_t, coeffs_t, noise_t, *awaited)


def factor_kernel(pivot_ref, point_ref, inverse_ref, factor_ref):
    pivots = extended(pivot_ref[...], True).astype(jnp.bfloat16)
    points = extended(point_ref[...], False).astype(jnp.bfloat16)
    cols = kernel_of(product(points, pivots, ((0,), (0,))))
    factor_ref[...] = product(cols, inverse_ref[...], ((1,), (1,)), lax.Precision.HIGHEST)


def factor_of(pivots_t, points_t, inverse):
    size = pivots_t.shape[1]
    count = points_t.shape[1]
    return pl.pallas_call(
        factor_kernel,
        out_shape=jax.ShapeDtypeStruct((count, size), jnp.float32),
        in_specs=in_vmem(3),
        out_specs=in_vmem(1)[0],
        compiler_params=pltpu.CompilerParams(vmem_limit_bytes=32 * 1024 * 1024),
        cost_estimate=pl.CostEstimate(flops=12 * count * size * size, bytes_accessed=4 * count * size, transcendentals=count * size),
        name="factor",
    )(pivots_t, points_t, inverse)


def band_kernel(pieces, first, last, *refs):
    own_ref = refs[0]
    piece_refs = refs[1:1 + 2 * pieces]
    at = 1 + 2 * pieces
    total_ref = out_ref = refs[-1]
    count = own_ref.shape[1]
    before_ref = None
    if not first:
        before_ref = refs[at]
        at += 1
    if last:
        probe_ref = refs[at]
    own = extended(own_ref[...], True)
    own = jnp.concatenate([own, jnp.zeros((LANES - own.shape[0], count), jnp.float32)], axis=0)
    own = jnp.transpose(own).astype(jnp.bfloat16)
    others = []
    for i in range(pieces):
        other = extended(piece_refs[2 * i][...], False)
        other = jnp.concatenate([other, jnp.zeros((LANES - other.shape[0], count), jnp.float32)], axis=0)
        others.append(other.astype(jnp.bfloat16))
    for s in range(0, count, CHUNK):
        total = None if first else before_ref[s:s + CHUNK, :]
        for i in range(pieces):
            tile = kernel_of(product(own[s:s + CHUNK, :], others[i], ((1,), (0,)))).astype(jnp.bfloat16)
            term = product(tile, piece_refs[2 * i + 1][...], ((1,), (1,)))
            total = term if total is None else total + term
        if last:
            scale = 1.0 / (count ** 0.5)
            out_ref[:, s:s + CHUNK] = jnp.transpose(total) * scale + noise_weight * probe_ref[:, s:s + CHUNK]
        else:
            total_ref[s:s + CHUNK, :] = total


def band_sum(own, pieces, before=None, probes=None):
    depth, count = own.shape
    width = pieces[0][1].shape[0]
    first, last = before is None, probes is not None
    operands = [own] + [array for piece in pieces for array in piece]
    operands += ([] if first else [before]) + ([probes] if last else [])
    return pl.pallas_call(
        functools.partial(band_kernel, len(pieces), first, last),
        out_shape=jax.ShapeDtypeStruct((width, count) if last else (count, width), jnp.float32),
        in_specs=in_vmem(len(operands)),
        out_specs=in_vmem(1)[0],
        compiler_params=pltpu.CompilerParams(vmem_limit_bytes=32 * 1024 * 1024),
        cost_estimate=pl.CostEstimate(
            flops=len(pieces) * 4 * count * count * LANES,
            bytes_accessed=4 * count * width * len(operands),
            transcendentals=len(pieces) * count * count,
        ),
        name="band_sum",
    )(*operands)


def shards(points, pivots, owners, coeffs, noise):
    points = points.T
    rounds = spread(pick(owners, pivots, points))
    pivot_points = rounds[-1]
    near_points = neighbours(points, rounds)

    inverse, probes, sent = probes_of(pivot_points, points, coeffs.T, noise.T, near_points[:5])
    near_probes = neighbours(sent)
    factor = factor_of(pivot_points, points, inverse)
    near = list(zip(near_points, near_probes))
    total = band_sum(points, [(points, sent)])
    total = band_sum(points, near[:2], total)
    total = band_sum(points, near[2:4], total)
    kernel_probes = band_sum(points, near[4:], total, probes).T
    return (kernel_probes, factor)


def solution(mesh):
    in_specs = (P(("gx", "gy"), None), P(), P(), P(), P(("gx", "gy"), None))
    out_specs = (P(("gx", "gy"), None), P(("gx", "gy"), None))
    return jax.shard_map(shards, mesh=mesh, in_specs=in_specs, out_specs=out_specs, check_vma=False)
```

```python
import functools

import jax
import jax.numpy as jnp
from jax import lax
from jax.experimental import pallas as pl
from jax.experimental.pallas import tpu as pltpu
from jax.sharding import PartitionSpec as P

PIVOTS = 128
KERNEL_SCALE = 32
BAND = 3
STRIP = 8
LANES = 128
EXTRA = 16
CHUNK = 256


jitter = 0.1
noise_weight = 0.5


def shifted(value, axis, steps):
    count = lax.axis_size(axis)
    return lax.ppermute(value, axis, [((i + steps) % count, i) for i in range(count)])


def swapped(value, axis, bit):
    return lax.ppermute(value, axis, [(i ^ bit, i) for i in range(lax.axis_size(axis))])


def after(value, *others):
    return lax.optimization_barrier((value,) + others)[0]


def spread(value):
    sums = [value]
    for axis in ("gx", "gy"):
        bits = [1 << i for i in range(lax.axis_size(axis).bit_length() - 1)]
        for bit in bits if axis == "gx" else bits[::-1]:
            sums.append(sums[-1] + swapped(sums[-1], axis, bit))
    return sums[1:]


def cross(piece, bits):
    outer, inner = lax.axis_size("gx"), lax.axis_size("gy")
    pairs = []
    for x in range(outer):
        for z in range(inner):
            source = (x - 1 if z ^ bits > z else x + 1) % outer
            pairs.append((source * inner + z, x * inner + z))
    return lax.ppermute(piece, ("gx", "gy"), pairs)


def tied(value, *tokens):
    return pl.pallas_call(
        lambda *refs: None,
        out_shape=jax.ShapeDtypeStruct(value.shape, value.dtype),
        in_specs=[pl.BlockSpec(memory_space=pl.ANY)] * (1 + len(tokens)),
        out_specs=pl.BlockSpec(memory_space=pl.ANY),
        input_output_aliases={0: 0},
        name="tied",
    )(value, *tokens)


def neighbours(value, steps=(), between=()):
    if lax.axis_size("gy") != BAND + 1:
        return [shifted(value, ("gx", "gy"), k) for k in range(-BAND, BAND + 1) if k != 0]

    def at(piece, step):
        return after(piece, steps[min(step, len(steps) - 1)]) if steps else piece

    two = swapped(value, "gy", 2)
    one = swapped(at(value, 0), "gy", 1)
    if between:
        two = tied(two, *between)
    three = swapped(at(two, 1), "gy", 1)
    cross_one = cross(at(one, 2), 1)
    cross_two = cross(at(two, 3), 2)
    return [one, two, cross_one, cross_two, three, cross(at(three, 4), 3)]


def in_vmem(count):
    return [pl.BlockSpec(memory_space=pltpu.VMEM)] * count


def thirds(value):
    high = value.astype(jnp.bfloat16)
    rest = value - high.astype(jnp.float32)
    middle = rest.astype(jnp.bfloat16)
    return high, middle, (rest - middle.astype(jnp.float32)).astype(jnp.bfloat16)


def product(left, right, contract, precision=None):
    return lax.dot_general(
        left, right, (contract, ((), ())), precision=precision, preferred_element_type=jnp.float32
    )


def extended(columns, ones_first):
    wide = columns.astype(jnp.float32)
    half = -0.5 * jnp.sum(wide * wide, axis=0, keepdims=True)
    terms = [term.astype(jnp.float32) for term in thirds(half)]
    shape = (EXTRA, columns.shape[1])
    level = lax.broadcasted_iota(jnp.int32, shape, 0)
    first = 0 if ones_first else 3
    below = jnp.where((level >= first) & (level < first + 3), 1.0, 0.0)
    for i, term in enumerate(terms):
        below = jnp.where(level == 3 - first + i, jnp.broadcast_to(term, shape), below)
    return jnp.concatenate([wide, below], axis=0)


def kernel_of(product_of_extended):
    return jnp.exp(product_of_extended * (2.0 / KERNEL_SCALE))


def pick_kernel(owner_ref, pivot_ref, point_ref, out_ref):
    count = point_ref.shape[1]
    me = lax.axis_index(("gx", "gy"))
    wanted = [jnp.where(owner_ref[r] == me, pivot_ref[r:r + 1, :], -1) for r in range(2)]
    wanted = jnp.concatenate(wanted, axis=1)
    place = lax.broadcasted_iota(jnp.int32, (count, wanted.shape[1]), 0)
    chosen = jnp.where(place == wanted, 1.0, 0.0).astype(jnp.bfloat16)
    out_ref[...] = product(point_ref[...], chosen, ((1,), (0,))).astype(jnp.bfloat16)


def pick(owners, pivots, points_t):
    return pl.pallas_call(
        pick_kernel,
        out_shape=jax.ShapeDtypeStruct((points_t.shape[0], 2 * PIVOTS), jnp.bfloat16),
        in_specs=[pl.BlockSpec(memory_space=pltpu.SMEM)] + in_vmem(2),
        out_specs=in_vmem(1)[0],
        name="pick",
    )(owners, pivots, points_t)


def column(strip, lane):
    return jnp.broadcast_to(strip[:, lane:lane + 1], strip.shape)


def row(strip, i):
    return jnp.broadcast_to(strip[i:i + 1, :], strip.shape)


def total_of(terms):
    while len(terms) > 1:
        terms = [terms[i] + terms[i + 1] if i + 1 < len(terms) else terms[i] for i in range(0, len(terms), 2)]
    return terms[0]


def four_pivots(a):
    rows = len(a)
    x = [[None] * 4 for _ in range(4)]
    scale = [None] * 4
    product_so_far = None
    for k in range(4):
        pivot = a[k][k]
        x[k][k] = product_so_far
        product_so_far = pivot if k == 0 else product_so_far * pivot
        scale[k] = lax.rsqrt(product_so_far)
        for i in range(k + 1, rows):
            for j in range(k + 1, min(i, 3) + 1):
                a[i][j] = pivot * a[i][j] - a[i][k] * a[j][k]
        for i in range(k + 1, 4):
            for j in range(k):
                x[i][j] = pivot * x[i][j] - a[i][k] * x[k][j]
            x[i][k] = -a[i][k] if k == 0 else -a[i][k] * x[k][k]
        yield
    factor = [[a[i][k] * scale[k] for k in range(4)] for i in range(4, rows)]
    inverse = [[scale[i] if x[i][j] is None else x[i][j] * scale[i] for j in range(i + 1)] for i in range(4)]
    return factor, inverse


def small_inverse(columns):
    a = [[row(columns[k], i) for k in range(i + 1)] for i in range(STRIP)]
    yield
    below, one = yield from four_pivots([list(entries) for entries in a])
    rest = [
        [a[4 + i][4 + j] - total_of([below[i][k] * below[j][k] for k in range(4)]) for j in range(i + 1)]
        for i in range(4)
    ]
    back = [[total_of([below[i][k] * one[k][j] for k in range(j, 4)]) for j in range(4)] for i in range(4)]
    _, two = yield from four_pivots(rest)
    corner = [[-total_of([two[i][m] * back[m][j] for m in range(i + 1)]) for j in range(4)] for i in range(4)]
    return one + [corner[i] + two[i] for i in range(4)]


def inverse_factor(strips):
    lane = lax.broadcasted_iota(jnp.int32, (STRIP, LANES), 1)
    level = lax.broadcasted_iota(jnp.int32, (STRIP, LANES), 0)
    strips = list(strips)
    result = [None] * len(strips)
    waiting = []

    def factor_columns(r, start, t):
        columns = [column(strips[r], start + j) for j in range(STRIP)]
        return [total_of([columns[j] * t[k][j] for j in range(k + 1)]) for k in range(STRIP)]

    def finish(p, t, found):
        start = p * STRIP
        own = (lane >= start) & (lane < start + STRIP)
        rows = []

        def scaled():
            entered = jnp.where(own, jnp.where(lane - start == level, 1.0, 0.0), strips[p])
            terms = []
            for k in range(STRIP):
                t_column = t[STRIP - 1][k]
                for i in range(STRIP - 2, k - 1, -1):
                    t_column = jnp.where(level == i, t[i][k], t_column)
                if k:
                    t_column = jnp.where(level < k, 0.0, t_column)
                terms.append(t_column * row(entered, k))
            done = total_of(terms)
            result[p] = jnp.where(lane < start + STRIP, done, 0.0)
            rows.extend(row(done, k) for k in range(STRIP))

        def updated(r):
            l_columns = found if r == p + 1 else factor_columns(r, start, t)
            update = total_of([l_columns[k] * rows[k] for k in range(STRIP)])
            strips[r] = jnp.where(own, 0.0, strips[r]) - update

        return [scaled] + [functools.partial(updated, r) for r in range(p + 1, len(strips))]

    columns = [column(strips[0], k) for k in range(STRIP)]
    for p in range(len(strips)):
        steps = small_inverse(columns)
        while True:
            try:
                next(steps)
            except StopIteration as ended:
                t = ended.value
                break
            for _ in range(2):
                if waiting:
                    waiting.pop(0)()
        while waiting:
            waiting.pop(0)()
        found = None
        if p + 1 < len(strips):
            start = p * STRIP
            found = factor_columns(p + 1, start, t)
            columns = [
                column(strips[p + 1], start + STRIP + j) - total_of([found[k] * row(found[k], j) for k in range(STRIP)])
                for j in range(STRIP)
            ]
        waiting = finish(p, t, found)
    while waiting:
        waiting.pop(0)()
    return result


def probe_kernel(pivot_ref, point_ref, coeff_ref, noise_ref, *refs):
    inverse_ref, probe_ref, sent_ref, high_ref, middle_ref, little_ref = refs[-6:]
    hp = lax.Precision.HIGHEST
    size = pivot_ref.shape[1]
    half = size // 2
    pivots = extended(pivot_ref[...], True).astype(jnp.bfloat16)
    others = extended(pivot_ref[...], False).astype(jnp.bfloat16)
    points = extended(point_ref[...], False).astype(jnp.bfloat16)
    cols = kernel_of(product(pivots, points, ((0,), (0,))))
    high_ref[...], middle_ref[...], little_ref[...] = thirds(cols)

    gram = kernel_of(product(pivots, others, ((0,), (0,))))
    equal = lax.broadcasted_iota(jnp.int32, gram.shape, 0) == lax.broadcasted_iota(jnp.int32, gram.shape, 1)
    gram = gram + jnp.where(equal, jitter, 0.0)

    def inverted(block):
        strips = [block[s:s + STRIP, :] for s in range(0, half, STRIP)]
        return jnp.concatenate(inverse_factor(strips), axis=0)

    one = inverted(gram[:half, :half])
    below = product(gram[half:, :half], one, ((1,), (1,)), hp)
    back = product(below, one, ((1,), (0,)), hp)
    two = inverted(gram[half:, half:] - product(below, below, ((1,), (1,)), hp))
    coeffs = coeff_ref[...]
    start = product(coeffs[:, :half], one, ((1,), (0,)), hp)
    later = product(coeffs[:, half:], two, ((1,), (0,)), hp)
    weights = jnp.concatenate([start - product(later, back, ((1,), (0,)), hp), later], axis=1)

    rows = weights.shape[0]
    stacked = jnp.concatenate(thirds(weights), axis=0)
    by_high = product(stacked, high_ref[...], ((1,), (0,)))
    by_middle = product(stacked[:2 * rows], middle_ref[...], ((1,), (0,)))
    by_little = product(stacked[:rows], little_ref[...], ((1,), (0,)))
    small = by_high[2 * rows:] + by_middle[rows:] + by_little
    probes = by_high[:rows] + (by_high[rows:2 * rows] + by_middle[:rows] + small) + noise_ref[...]
    probe_ref[...] = probes
    sent_ref[...] = probes.astype(jnp.bfloat16)

    inverse_ref[:half, :half] = one
    inverse_ref[:half, half:] = jnp.zeros((half, half), jnp.float32)
    inverse_ref[half:, :half] = -product(two, back, ((1,), (0,)), hp)
    inverse_ref[half:, half:] = two


def probes_of(pivots_t, points_t, coeffs_t, noise_t, awaited):
    size = pivots_t.shape[1]
    count = points_t.shape[1]
    return pl.pallas_call(
        probe_kernel,
        out_shape=(
            jax.ShapeDtypeStruct((size, size), jnp.float32),
            jax.ShapeDtypeStruct(noise_t.shape, jnp.float32),
            jax.ShapeDtypeStruct(noise_t.shape, jnp.bfloat16),
        ),
        in_specs=in_vmem(4) + [pl.BlockSpec(memory_space=pl.ANY)] * len(awaited),
        out_specs=tuple(in_vmem(3)),
        scratch_shapes=[pltpu.VMEM((size, count), jnp.bfloat16)] * 3,
        compiler_params=pltpu.CompilerParams(vmem_limit_bytes=32 * 1024 * 1024),
        name="probes",
    )(pivots_t, points_t, coeffs_t, noise_t, *awaited)


def factor_kernel(pivot_ref, point_ref, inverse_ref, factor_ref):
    pivots = extended(pivot_ref[...], True).astype(jnp.bfloat16)
    points = extended(point_ref[...], False).astype(jnp.bfloat16)
    cols = kernel_of(product(points, pivots, ((0,), (0,))))
    factor_ref[...] = product(cols, inverse_ref[...], ((1,), (1,)), lax.Precision.HIGHEST)


def factor_of(pivots_t, points_t, inverse):
    size = pivots_t.shape[1]
    count = points_t.shape[1]
    return pl.pallas_call(
        factor_kernel,
        out_shape=jax.ShapeDtypeStruct((count, size), jnp.float32),
        in_specs=in_vmem(3),
        out_specs=in_vmem(1)[0],
        compiler_params=pltpu.CompilerParams(vmem_limit_bytes=32 * 1024 * 1024),
        cost_estimate=pl.CostEstimate(flops=12 * count * size * size, bytes_accessed=4 * count * size, transcendentals=count * size),
        name="factor",
    )(pivots_t, points_t, inverse)


def band_kernel(pieces, first, last, *refs):
    own_ref = refs[0]
    piece_refs = refs[1:1 + 2 * pieces]
    at = 1 + 2 * pieces
    total_ref = out_ref = refs[-1]
    count = own_ref.shape[1]
    before_ref = None
    if not first:
        before_ref = refs[at]
        at += 1
    if last:
        probe_ref = refs[at]
    own = extended(own_ref[...], True)
    own = jnp.concatenate([own, jnp.zeros((LANES - own.shape[0], count), jnp.float32)], axis=0)
    own = jnp.transpose(own).astype(jnp.bfloat16)
    others = []
    for i in range(pieces):
        other = extended(piece_refs[2 * i][...], False)
        other = jnp.concatenate([other, jnp.zeros((LANES - other.shape[0], count), jnp.float32)], axis=0)
        others.append(other.astype(jnp.bfloat16))
    for s in range(0, count, CHUNK):
        total = None if first else before_ref[s:s + CHUNK, :]
        for i in range(pieces):
            tile = kernel_of(product(own[s:s + CHUNK, :], others[i], ((1,), (0,)))).astype(jnp.bfloat16)
            term = product(tile, piece_refs[2 * i + 1][...], ((1,), (1,)))
            total = term if total is None else total + term
        if last:
            scale = 1.0 / (count ** 0.5)
            out_ref[:, s:s + CHUNK] = jnp.transpose(total) * scale + noise_weight * probe_ref[:, s:s + CHUNK]
        else:
            total_ref[s:s + CHUNK, :] = total


def band_sum(own, pieces, before=None, probes=None):
    depth, count = own.shape
    width = pieces[0][1].shape[0]
    first, last = before is None, probes is not None
    operands = [own] + [array for piece in pieces for array in piece]
    operands += ([] if first else [before]) + ([probes] if last else [])
    return pl.pallas_call(
        functools.partial(band_kernel, len(pieces), first, last),
        out_shape=jax.ShapeDtypeStruct((width, count) if last else (count, width), jnp.float32),
        in_specs=in_vmem(len(operands)),
        out_specs=in_vmem(1)[0],
        compiler_params=pltpu.CompilerParams(vmem_limit_bytes=32 * 1024 * 1024),
        cost_estimate=pl.CostEstimate(
            flops=len(pieces) * 4 * count * count * LANES,
            bytes_accessed=4 * count * width * len(operands),
            transcendentals=len(pieces) * count * count,
        ),
        name="band_sum",
    )(*operands)


def shards(points, pivots, owners, coeffs, noise):
    points = points.T
    rounds = spread(pick(owners, pivots, points))
    pivot_points = rounds[-1]
    near_points = neighbours(points, rounds)

    inverse, probes, sent = probes_of(pivot_points, points, coeffs.T, noise.T, near_points[:5])
    factor = factor_of(pivot_points, points, inverse)
    total = band_sum(points, [(points, sent)])
    near_probes = neighbours(sent, between=(total, factor))
    near = list(zip(near_points, near_probes))
    total = band_sum(points, near[:2], total)
    total = band_sum(points, near[2:4], total)
    kernel_probes = band_sum(points, near[4:], total, probes).T
    return (kernel_probes, factor)


def solution(mesh):
    in_specs = (P(("gx", "gy"), None), P(), P(), P(), P(("gx", "gy"), None))
    out_specs = (P(("gx", "gy"), None), P(("gx", "gy"), None))
    return jax.shard_map(shards, mesh=mesh, in_specs=in_specs, out_specs=out_specs, check_vma=False)
```

```python
import functools
import math

import jax
import jax.numpy as jnp
from jax import lax
from jax.experimental import pallas as pl
from jax.experimental.pallas import tpu as pltpu
from jax.sharding import PartitionSpec as P

PIVOTS = 128
KERNEL_SCALE = 32
BAND = 3
STRIP = 8
LANES = 128
EXTRA = 16
CHUNK = 256


jitter = 0.1
noise_weight = 0.5


def shifted(value, axis, steps):
    count = lax.axis_size(axis)
    return lax.ppermute(value, axis, [((i + steps) % count, i) for i in range(count)])


def swapped(value, axis, bit):
    return lax.ppermute(value, axis, [(i ^ bit, i) for i in range(lax.axis_size(axis))])


def spread(value):
    sums = [value]
    for axis in ("gx", "gy"):
        bits = [1 << i for i in range(lax.axis_size(axis).bit_length() - 1)]
        for bit in bits if axis == "gx" else bits[::-1]:
            sums.append(sums[-1] + swapped(sums[-1], axis, bit))
    return sums[1:]


def cross(piece, bits):
    outer, inner = lax.axis_size("gx"), lax.axis_size("gy")
    pairs = []
    for x in range(outer):
        for z in range(inner):
            source = (x - 1 if z ^ bits > z else x + 1) % outer
            pairs.append((source * inner + z, x * inner + z))
    return lax.ppermute(piece, ("gx", "gy"), pairs)


def tied(value, *tokens):
    for token in tokens:
        value = jnp.where(token[0, 0] == jnp.inf, jnp.zeros_like(value), value)
    return value


def column_blocks(value):
    two = swapped(value, "gy", 2)
    return swapped(value, "gy", 1), two, swapped(two, "gy", 1)


def direct_blocks(value):
    return [shifted(value, ("gx", "gy"), k) for k in range(-BAND, BAND + 1) if k != 0]


def in_vmem(count):
    return [pl.BlockSpec(memory_space=pltpu.VMEM)] * count


def thirds(value):
    high = value.astype(jnp.bfloat16)
    rest = value - high.astype(jnp.float32)
    middle = rest.astype(jnp.bfloat16)
    return high, middle, (rest - middle.astype(jnp.float32)).astype(jnp.bfloat16)


def product(left, right, contract, precision=None):
    return lax.dot_general(
        left, right, (contract, ((), ())), precision=precision, preferred_element_type=jnp.float32
    )


def extended(columns, ones_first):
    wide = columns.astype(jnp.float32)
    half = -0.5 * jnp.sum(wide * wide, axis=0, keepdims=True)
    terms = [term.astype(jnp.float32) for term in thirds(half)]
    shape = (EXTRA, columns.shape[1])
    level = lax.broadcasted_iota(jnp.int32, shape, 0)
    first = 0 if ones_first else 3
    below = jnp.where((level >= first) & (level < first + 3), 1.0, 0.0)
    for i, term in enumerate(terms):
        below = jnp.where(level == 3 - first + i, jnp.broadcast_to(term, shape), below)
    return jnp.concatenate([wide, below], axis=0)


def kernel_of(product_of_extended):
    return jnp.exp2(product_of_extended * (2.0 / KERNEL_SCALE * math.log2(math.e)))


def pick_kernel(owner_ref, pivot_ref, point_ref, out_ref):
    count = point_ref.shape[1]
    me = lax.axis_index(("gx", "gy"))
    wanted = [jnp.where(owner_ref[r] == me, pivot_ref[r:r + 1, :], -1) for r in range(2)]
    wanted = jnp.concatenate(wanted, axis=1)
    place = lax.broadcasted_iota(jnp.int32, (count, wanted.shape[1]), 0)
    chosen = jnp.where(place == wanted, 1.0, 0.0).astype(jnp.bfloat16)
    out_ref[...] = product(point_ref[...], chosen, ((1,), (0,))).astype(jnp.bfloat16)


def pick(owners, pivots, points_t):
    return pl.pallas_call(
        pick_kernel,
        out_shape=pltpu.VMEM((points_t.shape[0], 2 * PIVOTS), jnp.bfloat16),
        in_specs=[pl.BlockSpec(memory_space=pltpu.SMEM)] + in_vmem(2),
        out_specs=in_vmem(1)[0],
        name="pick",
    )(owners, pivots, points_t)


def column(strip, lane):
    return jnp.broadcast_to(strip[:, lane:lane + 1], strip.shape)


def row(strip, i):
    return jnp.broadcast_to(strip[i:i + 1, :], strip.shape)


def total_of(terms):
    while len(terms) > 1:
        terms = [terms[i] + terms[i + 1] if i + 1 < len(terms) else terms[i] for i in range(0, len(terms), 2)]
    return terms[0]


def four_pivots(a):
    rows = len(a)
    x = [[None] * 4 for _ in range(4)]
    scale = [None] * 4
    product_so_far = None
    for k in range(4):
        pivot = a[k][k]
        x[k][k] = product_so_far
        product_so_far = pivot if k == 0 else product_so_far * pivot
        scale[k] = lax.rsqrt(product_so_far)
        for i in range(k + 1, rows):
            for j in range(k + 1, min(i, 3) + 1):
                a[i][j] = pivot * a[i][j] - a[i][k] * a[j][k]
        for i in range(k + 1, 4):
            for j in range(k):
                x[i][j] = pivot * x[i][j] - a[i][k] * x[k][j]
            x[i][k] = -a[i][k] if k == 0 else -a[i][k] * x[k][k]
        yield
    factor = [[a[i][k] * scale[k] for k in range(4)] for i in range(4, rows)]
    inverse = [[scale[i] if x[i][j] is None else x[i][j] * scale[i] for j in range(i + 1)] for i in range(4)]
    return factor, inverse


def small_inverse(columns):
    a = [[row(columns[k], i) for k in range(i + 1)] for i in range(STRIP)]
    yield
    below, one = yield from four_pivots([list(entries) for entries in a])
    rest = [
        [a[4 + i][4 + j] - total_of([below[i][k] * below[j][k] for k in range(4)]) for j in range(i + 1)]
        for i in range(4)
    ]
    back = [[total_of([below[i][k] * one[k][j] for k in range(j, 4)]) for j in range(4)] for i in range(4)]
    _, two = yield from four_pivots(rest)
    corner = [[-total_of([two[i][m] * back[m][j] for m in range(i + 1)]) for j in range(4)] for i in range(4)]
    return one + [corner[i] + two[i] for i in range(4)]


def inverse_factor(strips):
    lane = lax.broadcasted_iota(jnp.int32, (STRIP, LANES), 1)
    level = lax.broadcasted_iota(jnp.int32, (STRIP, LANES), 0)
    strips = list(strips)
    result = [None] * len(strips)
    waiting = []

    def factor_columns(r, start, t):
        columns = [column(strips[r], start + j) for j in range(STRIP)]
        return [total_of([columns[j] * t[k][j] for j in range(k + 1)]) for k in range(STRIP)]

    def finish(p, t, found):
        start = p * STRIP
        own = (lane >= start) & (lane < start + STRIP)
        rows = []

        def scaled():
            entered = jnp.where(own, jnp.where(lane - start == level, 1.0, 0.0), strips[p])
            terms = []
            for k in range(STRIP):
                t_column = t[STRIP - 1][k]
                for i in range(STRIP - 2, k - 1, -1):
                    t_column = jnp.where(level == i, t[i][k], t_column)
                if k:
                    t_column = jnp.where(level < k, 0.0, t_column)
                terms.append(t_column * row(entered, k))
            done = total_of(terms)
            result[p] = jnp.where(lane < start + STRIP, done, 0.0)
            rows.extend(row(done, k) for k in range(STRIP))

        def updated(r):
            l_columns = found if r == p + 1 else factor_columns(r, start, t)
            update = total_of([l_columns[k] * rows[k] for k in range(STRIP)])
            strips[r] = jnp.where(own, 0.0, strips[r]) - update

        return [scaled] + [functools.partial(updated, r) for r in range(p + 1, len(strips))]

    columns = [column(strips[0], k) for k in range(STRIP)]
    for p in range(len(strips)):
        steps = small_inverse(columns)
        while True:
            try:
                next(steps)
            except StopIteration as ended:
                t = ended.value
                break
            for _ in range(2):
                if waiting:
                    waiting.pop(0)()
        while waiting:
            waiting.pop(0)()
        found = None
        if p + 1 < len(strips):
            start = p * STRIP
            found = factor_columns(p + 1, start, t)
            columns = [
                column(strips[p + 1], start + STRIP + j) - total_of([found[k] * row(found[k], j) for k in range(STRIP)])
                for j in range(STRIP)
            ]
        waiting = finish(p, t, found)
    while waiting:
        waiting.pop(0)()
    return result


def probe_kernel(pivot_ref, point_ref, coeff_ref, noise_ref, *refs):
    inverse_ref, probe_ref, sent_ref, high_ref, middle_ref, little_ref = refs[-6:]
    hp = lax.Precision.HIGHEST
    size = pivot_ref.shape[1]
    half = size // 2
    pivots = extended(pivot_ref[...], True).astype(jnp.bfloat16)
    others = extended(pivot_ref[...], False).astype(jnp.bfloat16)
    points = extended(point_ref[...], False).astype(jnp.bfloat16)
    cols = kernel_of(product(pivots, points, ((0,), (0,))))
    high_ref[...], middle_ref[...], little_ref[...] = thirds(cols)

    gram = kernel_of(product(pivots, others, ((0,), (0,))))
    equal = lax.broadcasted_iota(jnp.int32, gram.shape, 0) == lax.broadcasted_iota(jnp.int32, gram.shape, 1)
    gram = gram + jnp.where(equal, jitter, 0.0)

    def inverted(block):
        strips = [block[s:s + STRIP, :] for s in range(0, half, STRIP)]
        return jnp.concatenate(inverse_factor(strips), axis=0)

    one = inverted(gram[:half, :half])
    below = product(gram[half:, :half], one, ((1,), (1,)), hp)
    back = product(below, one, ((1,), (0,)), hp)
    two = inverted(gram[half:, half:] - product(below, below, ((1,), (1,)), hp))
    coeffs = coeff_ref[...]
    start = product(coeffs[:, :half], one, ((1,), (0,)), hp)
    later = product(coeffs[:, half:], two, ((1,), (0,)), hp)
    weights = jnp.concatenate([start - product(later, back, ((1,), (0,)), hp), later], axis=1)

    rows = weights.shape[0]
    stacked = jnp.concatenate(thirds(weights), axis=0)
    by_high = product(stacked, high_ref[...], ((1,), (0,)))
    by_middle = product(stacked[:2 * rows], middle_ref[...], ((1,), (0,)))
    by_little = product(stacked[:rows], little_ref[...], ((1,), (0,)))
    small = by_high[2 * rows:] + by_middle[rows:] + by_little
    probes = by_high[:rows] + (by_high[rows:2 * rows] + by_middle[:rows] + small) + noise_ref[...]
    probe_ref[...] = probes
    sent_ref[...] = probes.astype(jnp.bfloat16)

    inverse_ref[:half, :half] = one
    inverse_ref[:half, half:] = jnp.zeros((half, half), jnp.float32)
    inverse_ref[half:, :half] = -product(two, back, ((1,), (0,)), hp)
    inverse_ref[half:, half:] = two


def probes_of(pivots_t, points_t, coeffs_t, noise_t, awaited):
    size = pivots_t.shape[1]
    count = points_t.shape[1]
    return pl.pallas_call(
        probe_kernel,
        out_shape=(
            jax.ShapeDtypeStruct((size, size), jnp.float32),
            jax.ShapeDtypeStruct(noise_t.shape, jnp.float32),
            pltpu.VMEM(noise_t.shape, jnp.bfloat16),
        ),
        in_specs=in_vmem(4) + [pl.BlockSpec(memory_space=pl.ANY)] * len(awaited),
        out_specs=tuple(in_vmem(3)),
        scratch_shapes=[pltpu.VMEM((size, count), jnp.bfloat16)] * 3,
        compiler_params=pltpu.CompilerParams(vmem_limit_bytes=32 * 1024 * 1024),
        name="probes",
    )(pivots_t, points_t, coeffs_t, noise_t, *awaited)


def factor_kernel(pivot_ref, point_ref, inverse_ref, factor_ref):
    pivots = extended(pivot_ref[...], True).astype(jnp.bfloat16)
    points = extended(point_ref[...], False).astype(jnp.bfloat16)
    cols = kernel_of(product(points, pivots, ((0,), (0,))))
    factor_ref[...] = product(cols, inverse_ref[...], ((1,), (1,)), lax.Precision.HIGHEST)


def factor_of(pivots_t, points_t, inverse):
    size = pivots_t.shape[1]
    count = points_t.shape[1]
    return pl.pallas_call(
        factor_kernel,
        out_shape=jax.ShapeDtypeStruct((count, size), jnp.float32),
        in_specs=in_vmem(3),
        out_specs=in_vmem(1)[0],
        compiler_params=pltpu.CompilerParams(vmem_limit_bytes=32 * 1024 * 1024),
        cost_estimate=pl.CostEstimate(flops=12 * count * size * size, bytes_accessed=4 * count * size, transcendentals=count * size),
        name="factor",
    )(pivots_t, points_t, inverse)


def band_kernel(parts, first, last, *refs):
    refs = list(refs)
    out_ref = refs.pop()
    own_ref = refs.pop(0)
    count = own_ref.shape[1]
    pieces = []
    for part in parts:
        if part == 2:
            pieces.append((refs.pop(0)[...], refs.pop(0)[...]))
        else:
            stacked = refs.pop(0)
            pieces.append((stacked[:own_ref.shape[0], :], stacked[own_ref.shape[0]:, :]))
    before_ref = None if first else refs.pop(0)

    def padded(value):
        return jnp.concatenate([value, jnp.zeros((LANES - value.shape[0], count), jnp.float32)], axis=0)

    own = jnp.transpose(padded(extended(own_ref[...], True))).astype(jnp.bfloat16)
    others = [padded(extended(block, False)).astype(jnp.bfloat16) for block, _ in pieces]
    for s in range(0, count, CHUNK):
        total = None if first else before_ref[s:s + CHUNK, :]
        for other, (_, probes) in zip(others, pieces):
            tile = kernel_of(product(own[s:s + CHUNK, :], other, ((1,), (0,)))).astype(jnp.bfloat16)
            term = product(tile, probes, ((1,), (1,)))
            total = term if total is None else total + term
        if last:
            scale = 1.0 / (count ** 0.5)
            out_ref[:, s:s + CHUNK] = jnp.transpose(total) * scale + noise_weight * refs[0][:, s:s + CHUNK]
        else:
            out_ref[s:s + CHUNK, :] = total


def band_sum(own, pieces, before=None, probes=None):
    depth, count = own.shape
    width = pieces[0][1].shape[0] if len(pieces[0]) == 2 else pieces[0][0].shape[0] - depth
    first, last = before is None, probes is not None
    operands = [own] + [array for piece in pieces for array in piece]
    operands += ([] if first else [before]) + ([probes] if last else [])
    return pl.pallas_call(
        functools.partial(band_kernel, tuple(len(piece) for piece in pieces), first, last),
        out_shape=jax.ShapeDtypeStruct((width, count) if last else (count, width), jnp.float32),
        in_specs=in_vmem(len(operands)),
        out_specs=in_vmem(1)[0],
        compiler_params=pltpu.CompilerParams(vmem_limit_bytes=32 * 1024 * 1024),
        cost_estimate=pl.CostEstimate(
            flops=len(pieces) * 4 * count * count * LANES,
            bytes_accessed=4 * count * width * len(operands),
            transcendentals=len(pieces) * count * count,
        ),
        name="band_sum",
    )(*operands)


def shards(points, pivots, owners, coeffs, noise):
    tall = lax.axis_size("gy") == BAND + 1
    points = points.T
    pivot_points = spread(pick(owners, pivots, points))[-1]
    near = column_blocks(points) if tall else direct_blocks(points)

    inverse, probes, sent = probes_of(pivot_points, points, coeffs.T, noise.T, near)
    factor = factor_of(pivot_points, points, inverse)
    total = band_sum(points, [(points, sent)])
    if tall:
        two = tied(swapped(sent, "gy", 2), total, factor)
        one = tied(swapped(sent, "gy", 1), total, factor)
        three = swapped(two, "gy", 1)
        crossed = [cross(jnp.concatenate([near[i], probe], axis=0), i + 1) for i, probe in enumerate((one, two))]
        total = band_sum(points, [(near[0], one), (near[1], two)], total)
        crossed.append(cross(jnp.concatenate([near[2], tied(three, total)], axis=0), 3))
        total = band_sum(points, [(crossed[0],), (crossed[1],), (near[2], three)], total)
        kernel_probes = band_sum(points, [(crossed[2],)], total, probes)
    else:
        pieces = list(zip(near, direct_blocks(sent)))
        total = band_sum(points, pieces[:3], total)
        kernel_probes = band_sum(points, pieces[3:], total, probes)
    return (kernel_probes.T, factor)


def solution(mesh):
    in_specs = (P(("gx", "gy"), None), P(), P(), P(), P(("gx", "gy"), None))
    out_specs = (P(("gx", "gy"), None), P(("gx", "gy"), None))
    return jax.shard_map(shards, mesh=mesh, in_specs=in_specs, out_specs=out_specs, check_vma=False)
```

```python
import functools
import math

import jax
import jax.numpy as jnp
from jax import lax
from jax.experimental import pallas as pl
from jax.experimental.pallas import tpu as pltpu
from jax.sharding import PartitionSpec as P

PIVOTS = 128
KERNEL_SCALE = 32
BAND = 3
STRIP = 8
LANES = 128
EXTRA = 16
CHUNK = 256


jitter = 0.1
noise_weight = 0.5


def shifted(value, axis, steps):
    count = lax.axis_size(axis)
    return lax.ppermute(value, axis, [((i + steps) % count, i) for i in range(count)])


def swapped(value, axis, bit):
    return lax.ppermute(value, axis, [(i ^ bit, i) for i in range(lax.axis_size(axis))])


def spread(value):
    sums = [value]
    for axis in ("gx", "gy"):
        bits = [1 << i for i in range(lax.axis_size(axis).bit_length() - 1)]
        for bit in bits if axis == "gx" else bits[::-1]:
            sums.append(sums[-1] + swapped(sums[-1], axis, bit))
    return sums[1:]


def cross(piece, bits):
    outer, inner = lax.axis_size("gx"), lax.axis_size("gy")
    pairs = []
    for x in range(outer):
        for z in range(inner):
            source = (x - 1 if z ^ bits > z else x + 1) % outer
            pairs.append((source * inner + z, x * inner + z))
    return lax.ppermute(piece, ("gx", "gy"), pairs)


def column_blocks(value):
    two = swapped(value, "gy", 2)
    return swapped(value, "gy", 1), two, swapped(two, "gy", 1)


def direct_blocks(value):
    return [shifted(value, ("gx", "gy"), k) for k in range(-BAND, BAND + 1) if k != 0]


def in_vmem(count):
    return [pl.BlockSpec(memory_space=pltpu.VMEM)] * count


def thirds(value):
    high = value.astype(jnp.bfloat16)
    rest = value - high.astype(jnp.float32)
    middle = rest.astype(jnp.bfloat16)
    return high, middle, (rest - middle.astype(jnp.float32)).astype(jnp.bfloat16)


def product(left, right, contract, precision=None):
    return lax.dot_general(
        left, right, (contract, ((), ())), precision=precision, preferred_element_type=jnp.float32
    )


def extended(columns, ones_first):
    wide = columns.astype(jnp.float32)
    half = -0.5 * jnp.sum(wide * wide, axis=0, keepdims=True)
    terms = [term.astype(jnp.float32) for term in thirds(half)]
    shape = (EXTRA, columns.shape[1])
    level = lax.broadcasted_iota(jnp.int32, shape, 0)
    first = 0 if ones_first else 3
    below = jnp.where((level >= first) & (level < first + 3), 1.0, 0.0)
    for i, term in enumerate(terms):
        below = jnp.where(level == 3 - first + i, jnp.broadcast_to(term, shape), below)
    return jnp.concatenate([wide, below], axis=0)


def kernel_of(product_of_extended):
    return jnp.exp2(product_of_extended * (2.0 / KERNEL_SCALE * math.log2(math.e)))


def pick_kernel(owner_ref, pivot_ref, point_ref, out_ref):
    count = point_ref.shape[1]
    me = lax.axis_index(("gx", "gy"))
    wanted = [jnp.where(owner_ref[r] == me, pivot_ref[r:r + 1, :], -1) for r in range(2)]
    wanted = jnp.concatenate(wanted, axis=1)
    place = lax.broadcasted_iota(jnp.int32, (count, wanted.shape[1]), 0)
    chosen = jnp.where(place == wanted, 1.0, 0.0).astype(jnp.bfloat16)
    out_ref[...] = product(point_ref[...], chosen, ((1,), (0,))).astype(jnp.bfloat16)


def pick(owners, pivots, points_t):
    return pl.pallas_call(
        pick_kernel,
        out_shape=pltpu.VMEM((points_t.shape[0], 2 * PIVOTS), jnp.bfloat16),
        in_specs=[pl.BlockSpec(memory_space=pltpu.SMEM)] + in_vmem(2),
        out_specs=in_vmem(1)[0],
        name="pick",
    )(owners, pivots, points_t)


def column(strip, lane):
    return jnp.broadcast_to(strip[:, lane:lane + 1], strip.shape)


def row(strip, i):
    return jnp.broadcast_to(strip[i:i + 1, :], strip.shape)


def total_of(terms):
    while len(terms) > 1:
        terms = [terms[i] + terms[i + 1] if i + 1 < len(terms) else terms[i] for i in range(0, len(terms), 2)]
    return terms[0]


def four_pivots(a):
    rows = len(a)
    x = [[None] * 4 for _ in range(4)]
    scale = [None] * 4
    product_so_far = None
    for k in range(4):
        pivot = a[k][k]
        x[k][k] = product_so_far
        product_so_far = pivot if k == 0 else product_so_far * pivot
        scale[k] = lax.rsqrt(product_so_far)
        for i in range(k + 1, rows):
            for j in range(k + 1, min(i, 3) + 1):
                a[i][j] = pivot * a[i][j] - a[i][k] * a[j][k]
        for i in range(k + 1, 4):
            for j in range(k):
                x[i][j] = pivot * x[i][j] - a[i][k] * x[k][j]
            x[i][k] = -a[i][k] if k == 0 else -a[i][k] * x[k][k]
        yield
    factor = [[a[i][k] * scale[k] for k in range(4)] for i in range(4, rows)]
    inverse = [[scale[i] if x[i][j] is None else x[i][j] * scale[i] for j in range(i + 1)] for i in range(4)]
    return factor, inverse


def small_inverse(columns):
    a = [[row(columns[k], i) for k in range(i + 1)] for i in range(STRIP)]
    yield
    below, one = yield from four_pivots([list(entries) for entries in a])
    rest = [
        [a[4 + i][4 + j] - total_of([below[i][k] * below[j][k] for k in range(4)]) for j in range(i + 1)]
        for i in range(4)
    ]
    back = [[total_of([below[i][k] * one[k][j] for k in range(j, 4)]) for j in range(4)] for i in range(4)]
    _, two = yield from four_pivots(rest)
    corner = [[-total_of([two[i][m] * back[m][j] for m in range(i + 1)]) for j in range(4)] for i in range(4)]
    return one + [corner[i] + two[i] for i in range(4)]


def inverse_factor(strips):
    lane = lax.broadcasted_iota(jnp.int32, (STRIP, LANES), 1)
    level = lax.broadcasted_iota(jnp.int32, (STRIP, LANES), 0)
    strips = list(strips)
    result = [None] * len(strips)
    waiting = []

    def factor_columns(r, start, t):
        columns = [column(strips[r], start + j) for j in range(STRIP)]
        return [total_of([columns[j] * t[k][j] for j in range(k + 1)]) for k in range(STRIP)]

    def finish(p, t, found):
        start = p * STRIP
        own = (lane >= start) & (lane < start + STRIP)
        rows = []

        def scaled():
            entered = jnp.where(own, jnp.where(lane - start == level, 1.0, 0.0), strips[p])
            terms = []
            for k in range(STRIP):
                t_column = t[STRIP - 1][k]
                for i in range(STRIP - 2, k - 1, -1):
                    t_column = jnp.where(level == i, t[i][k], t_column)
                if k:
                    t_column = jnp.where(level < k, 0.0, t_column)
                terms.append(t_column * row(entered, k))
            done = total_of(terms)
            result[p] = jnp.where(lane < start + STRIP, done, 0.0)
            rows.extend(row(done, k) for k in range(STRIP))

        def updated(r):
            l_columns = found if r == p + 1 else factor_columns(r, start, t)
            update = total_of([l_columns[k] * rows[k] for k in range(STRIP)])
            strips[r] = jnp.where(own, 0.0, strips[r]) - update

        return [scaled] + [functools.partial(updated, r) for r in range(p + 1, len(strips))]

    columns = [column(strips[0], k) for k in range(STRIP)]
    for p in range(len(strips)):
        steps = small_inverse(columns)
        while True:
            try:
                next(steps)
            except StopIteration as ended:
                t = ended.value
                break
            for _ in range(2):
                if waiting:
                    waiting.pop(0)()
        while waiting:
            waiting.pop(0)()
        found = None
        if p + 1 < len(strips):
            start = p * STRIP
            found = factor_columns(p + 1, start, t)
            columns = [
                column(strips[p + 1], start + STRIP + j) - total_of([found[k] * row(found[k], j) for k in range(STRIP)])
                for j in range(STRIP)
            ]
        waiting = finish(p, t, found)
    while waiting:
        waiting.pop(0)()
    return result


def probe_kernel(pivot_ref, point_ref, coeff_ref, noise_ref, *refs):
    inverse_ref, probe_ref, sent_ref, high_ref, middle_ref, little_ref = refs[-6:]
    hp = lax.Precision.HIGHEST
    size = pivot_ref.shape[1]
    half = size // 2
    pivots = extended(pivot_ref[...], True).astype(jnp.bfloat16)
    others = extended(pivot_ref[...], False).astype(jnp.bfloat16)
    points = extended(point_ref[...], False).astype(jnp.bfloat16)
    cols = kernel_of(product(pivots, points, ((0,), (0,))))
    high_ref[...], middle_ref[...], little_ref[...] = thirds(cols)

    gram = kernel_of(product(pivots, others, ((0,), (0,))))
    equal = lax.broadcasted_iota(jnp.int32, gram.shape, 0) == lax.broadcasted_iota(jnp.int32, gram.shape, 1)
    gram = gram + jnp.where(equal, jitter, 0.0)

    def inverted(block):
        strips = [block[s:s + STRIP, :] for s in range(0, half, STRIP)]
        return jnp.concatenate(inverse_factor(strips), axis=0)

    one = inverted(gram[:half, :half])
    below = product(gram[half:, :half], one, ((1,), (1,)), hp)
    back = product(below, one, ((1,), (0,)), hp)
    two = inverted(gram[half:, half:] - product(below, below, ((1,), (1,)), hp))
    coeffs = coeff_ref[...]
    start = product(coeffs[:, :half], one, ((1,), (0,)), hp)
    later = product(coeffs[:, half:], two, ((1,), (0,)), hp)
    weights = jnp.concatenate([start - product(later, back, ((1,), (0,)), hp), later], axis=1)

    rows = weights.shape[0]
    stacked = jnp.concatenate(thirds(weights), axis=0)
    by_high = product(stacked, high_ref[...], ((1,), (0,)))
    by_middle = product(stacked[:2 * rows], middle_ref[...], ((1,), (0,)))
    by_little = product(stacked[:rows], little_ref[...], ((1,), (0,)))
    small = by_high[2 * rows:] + by_middle[rows:] + by_little
    probes = by_high[:rows] + (by_high[rows:2 * rows] + by_middle[:rows] + small) + noise_ref[...]
    probe_ref[...] = probes
    sent_ref[...] = probes.astype(jnp.bfloat16)

    inverse_ref[:half, :half] = one
    inverse_ref[:half, half:] = jnp.zeros((half, half), jnp.float32)
    inverse_ref[half:, :half] = -product(two, back, ((1,), (0,)), hp)
    inverse_ref[half:, half:] = two


def probes_of(pivots_t, points_t, coeffs_t, noise_t, awaited):
    size = pivots_t.shape[1]
    count = points_t.shape[1]
    return pl.pallas_call(
        probe_kernel,
        out_shape=(
            jax.ShapeDtypeStruct((size, size), jnp.float32),
            jax.ShapeDtypeStruct(noise_t.shape, jnp.float32),
            pltpu.VMEM(noise_t.shape, jnp.bfloat16),
        ),
        in_specs=in_vmem(4) + [pl.BlockSpec(memory_space=pl.ANY)] * len(awaited),
        out_specs=tuple(in_vmem(3)),
        scratch_shapes=[pltpu.VMEM((size, count), jnp.bfloat16)] * 3,
        compiler_params=pltpu.CompilerParams(vmem_limit_bytes=32 * 1024 * 1024),
        name="probes",
    )(pivots_t, points_t, coeffs_t, noise_t, *awaited)


def padded(value):
    return jnp.concatenate([value, jnp.zeros((LANES - value.shape[0], value.shape[1]), value.dtype)], axis=0)


def tile_terms(own, other, probes):
    return product(kernel_of(product(own, other, ((1,), (0,)))).astype(jnp.bfloat16), probes, ((1,), (1,)))


def factor_kernel(pivot_ref, point_ref, inverse_ref, sent_ref, factor_ref, total_ref, zero_ref):
    count = point_ref.shape[1]
    own = jnp.transpose(padded(extended(point_ref[...], True))).astype(jnp.bfloat16)
    pivots = padded(extended(pivot_ref[...], False)).astype(jnp.bfloat16)
    other = padded(extended(point_ref[...], False)).astype(jnp.bfloat16)
    high, middle, _ = thirds(inverse_ref[...])
    for s in range(0, count, CHUNK):
        rows = own[s:s + CHUNK, :]
        cols_high, cols_middle, _ = thirds(kernel_of(product(rows, pivots, ((1,), (0,)))))
        factor_ref[s:s + CHUNK, :] = (
            product(cols_high, middle, ((1,), (1,))) + product(cols_middle, high, ((1,), (1,)))
        ) + product(cols_high, high, ((1,), (1,)))
        total_ref[s:s + CHUNK, :] = tile_terms(rows, other, sent_ref[...])
    zero_ref[...] = jnp.zeros_like(zero_ref)


def factor_of(pivots_t, points_t, inverse, sent_t):
    size = pivots_t.shape[1]
    count = points_t.shape[1]
    return pl.pallas_call(
        factor_kernel,
        out_shape=(
            jax.ShapeDtypeStruct((count, size), jnp.float32),
            jax.ShapeDtypeStruct((count, sent_t.shape[0]), jnp.float32),
            pltpu.VMEM(sent_t.shape, sent_t.dtype),
        ),
        in_specs=in_vmem(4),
        out_specs=tuple(in_vmem(3)),
        compiler_params=pltpu.CompilerParams(vmem_limit_bytes=32 * 1024 * 1024),
        cost_estimate=pl.CostEstimate(
            flops=6 * count * size * size + 4 * count * count * LANES,
            bytes_accessed=6 * count * size,
            transcendentals=count * (size + count),
        ),
        name="factor",
    )(pivots_t, points_t, inverse, sent_t)


def band_kernel(parts, last, *refs):
    refs = list(refs)
    own_ref = refs.pop(0)
    depth, count = own_ref.shape
    pieces = []
    for part in parts:
        if part == 2:
            pieces.append((refs.pop(0)[...], refs.pop(0)[...]))
        else:
            stacked = refs.pop(0)
            pieces.append((stacked[:depth, :], stacked[depth:, :]))
    before_ref = refs.pop(0)
    own = jnp.transpose(padded(extended(own_ref[...], True))).astype(jnp.bfloat16)
    others = [padded(extended(block, False)).astype(jnp.bfloat16) for block, _ in pieces]
    for s in range(0, count, CHUNK):
        total = before_ref[s:s + CHUNK, :]
        for other, (_, probes) in zip(others, pieces):
            total = total + tile_terms(own[s:s + CHUNK, :], other, probes)
        if last:
            probe_ref, out_ref = refs
            scale = 1.0 / (count ** 0.5)
            out_ref[:, s:s + CHUNK] = jnp.transpose(total) * scale + noise_weight * probe_ref[:, s:s + CHUNK]
        else:
            refs[0][s:s + CHUNK, :] = total
    if not last:
        refs[1][...] = jnp.zeros_like(refs[1])


def band_sum(own, pieces, before, probes=None):
    depth, count = own.shape
    width = before.shape[1]
    last = probes is not None
    operands = [own] + [array for piece in pieces for array in piece] + [before] + ([probes] if last else [])
    if last:
        out_shape = jax.ShapeDtypeStruct((width, count), jnp.float32)
    else:
        out_shape = (jax.ShapeDtypeStruct(before.shape, jnp.float32), pltpu.VMEM((width, count), jnp.bfloat16))
    return pl.pallas_call(
        functools.partial(band_kernel, tuple(len(piece) for piece in pieces), last),
        out_shape=out_shape,
        in_specs=in_vmem(len(operands)),
        out_specs=in_vmem(1)[0] if last else tuple(in_vmem(2)),
        compiler_params=pltpu.CompilerParams(vmem_limit_bytes=32 * 1024 * 1024),
        cost_estimate=pl.CostEstimate(
            flops=len(pieces) * 4 * count * count * LANES,
            bytes_accessed=4 * count * width * len(operands),
            transcendentals=len(pieces) * count * count,
        ),
        name="band_sum",
    )(*operands)


def shards(points, pivots, owners, coeffs, noise):
    tall = lax.axis_size("gy") == BAND + 1
    points = points.T
    pivot_points = spread(pick(owners, pivots, points))[-1]
    near = column_blocks(points) if tall else direct_blocks(points)

    inverse, probes, sent = probes_of(pivot_points, points, coeffs.T, noise.T, near)
    factor, total, zeros = factor_of(pivot_points, points, inverse, sent)
    if tall:
        two = swapped(sent, "gy", 2) + zeros
        one = swapped(sent, "gy", 1) + zeros
        three = swapped(two, "gy", 1)
        crossed = [cross(jnp.concatenate([near[i], probe], axis=0), i + 1) for i, probe in enumerate((one, two))]
        total, zeros = band_sum(points, [(near[0], one), (near[1], two)], total)
        crossed.append(cross(jnp.concatenate([near[2], three + zeros], axis=0), 3))
        total, _ = band_sum(points, [(crossed[0],), (crossed[1],), (near[2], three)], total)
        kernel_probes = band_sum(points, [(crossed[2],)], total, probes)
    else:
        pieces = list(zip(near, direct_blocks(sent)))
        total, _ = band_sum(points, pieces[:3], total)
        kernel_probes = band_sum(points, pieces[3:], total, probes)
    return (kernel_probes.T, factor)


def solution(mesh):
    in_specs = (P(("gx", "gy"), None), P(), P(), P(), P(("gx", "gy"), None))
    out_specs = (P(("gx", "gy"), None), P(("gx", "gy"), None))
    return jax.shard_map(shards, mesh=mesh, in_specs=in_specs, out_specs=out_specs, check_vma=False)
```

```python
import functools
import math

import jax
import jax.numpy as jnp
from jax import lax
from jax.experimental import pallas as pl
from jax.experimental.pallas import tpu as pltpu
from jax.sharding import PartitionSpec as P

PIVOTS = 128
KERNEL_SCALE = 32
BAND = 3
STRIP = 8
LANES = 128
EXTRA = 16
CHUNK = 256


jitter = 0.1
noise_weight = 0.5


def shifted(value, axis, steps):
    count = lax.axis_size(axis)
    return lax.ppermute(value, axis, [((i + steps) % count, i) for i in range(count)])


def swapped(value, axis, bit):
    return lax.ppermute(value, axis, [(i ^ bit, i) for i in range(lax.axis_size(axis))])


def spread(value):
    for axis in ("gx", "gy"):
        count = lax.axis_size(axis)
        bit = 1
        while bit < count:
            wide = 2 if (count // bit).bit_length() % 2 == 0 else 4
            value = sum((swapped(value, axis, bit * k) for k in range(1, wide)), value)
            bit *= wide
    return value


def cross(piece, bits):
    outer, inner = lax.axis_size("gx"), lax.axis_size("gy")
    pairs = []
    for x in range(outer):
        for z in range(inner):
            source = (x - 1 if z ^ bits > z else x + 1) % outer
            pairs.append((source * inner + z, x * inner + z))
    return lax.ppermute(piece, ("gx", "gy"), pairs)


def direct_blocks(value):
    return [shifted(value, ("gx", "gy"), k) for k in range(-BAND, BAND + 1) if k != 0]


def in_vmem(count):
    return [pl.BlockSpec(memory_space=pltpu.VMEM)] * count


def thirds(value):
    high = value.astype(jnp.bfloat16)
    rest = value - high.astype(jnp.float32)
    middle = rest.astype(jnp.bfloat16)
    return high, middle, (rest - middle.astype(jnp.float32)).astype(jnp.bfloat16)


def product(left, right, contract, precision=None):
    return lax.dot_general(
        left, right, (contract, ((), ())), precision=precision, preferred_element_type=jnp.float32
    )


def extended(columns, ones_first):
    wide = columns.astype(jnp.float32)
    half = -0.5 * jnp.sum(wide * wide, axis=0, keepdims=True)
    terms = [term.astype(jnp.float32) for term in thirds(half)]
    shape = (EXTRA, columns.shape[1])
    level = lax.broadcasted_iota(jnp.int32, shape, 0)
    first = 0 if ones_first else 3
    below = jnp.where((level >= first) & (level < first + 3), 1.0, 0.0)
    for i, term in enumerate(terms):
        below = jnp.where(level == 3 - first + i, jnp.broadcast_to(term, shape), below)
    return jnp.concatenate([wide, below], axis=0)


def kernel_of(product_of_extended):
    return jnp.exp2(product_of_extended * (2.0 / KERNEL_SCALE * math.log2(math.e)))


def pick_kernel(owner_ref, pivot_ref, point_ref, out_ref):
    count = point_ref.shape[1]
    me = lax.axis_index(("gx", "gy"))
    wanted = [jnp.where(owner_ref[r] == me, pivot_ref[r:r + 1, :], -1) for r in range(2)]
    wanted = jnp.concatenate(wanted, axis=1)
    place = lax.broadcasted_iota(jnp.int32, (count, wanted.shape[1]), 0)
    chosen = jnp.where(place == wanted, 1.0, 0.0).astype(jnp.bfloat16)
    out_ref[...] = product(point_ref[...], chosen, ((1,), (0,))).astype(jnp.bfloat16)


def pick(owners, pivots, points_t):
    return pl.pallas_call(
        pick_kernel,
        out_shape=pltpu.VMEM((points_t.shape[0], 2 * PIVOTS), jnp.bfloat16),
        in_specs=[pl.BlockSpec(memory_space=pltpu.SMEM)] + in_vmem(2),
        out_specs=in_vmem(1)[0],
        name="pick",
    )(owners, pivots, points_t)


def column(strip, lane):
    return jnp.broadcast_to(strip[:, lane:lane + 1], strip.shape)


def row(strip, i):
    return jnp.broadcast_to(strip[i:i + 1, :], strip.shape)


def total_of(terms):
    while len(terms) > 1:
        terms = [terms[i] + terms[i + 1] if i + 1 < len(terms) else terms[i] for i in range(0, len(terms), 2)]
    return terms[0]


def four_pivots(a):
    rows = len(a)
    x = [[None] * 4 for _ in range(4)]
    scale = [None] * 4
    product_so_far = None
    for k in range(4):
        pivot = a[k][k]
        x[k][k] = product_so_far
        product_so_far = pivot if k == 0 else product_so_far * pivot
        scale[k] = lax.rsqrt(product_so_far)
        for i in range(k + 1, rows):
            for j in range(k + 1, min(i, 3) + 1):
                a[i][j] = pivot * a[i][j] - a[i][k] * a[j][k]
        for i in range(k + 1, 4):
            for j in range(k):
                x[i][j] = pivot * x[i][j] - a[i][k] * x[k][j]
            x[i][k] = -a[i][k] if k == 0 else -a[i][k] * x[k][k]
        yield
    factor = [[a[i][k] * scale[k] for k in range(4)] for i in range(4, rows)]
    inverse = [[scale[i] if x[i][j] is None else x[i][j] * scale[i] for j in range(i + 1)] for i in range(4)]
    return factor, inverse


def small_inverse(columns):
    a = [[row(columns[k], i) for k in range(i + 1)] for i in range(STRIP)]
    yield
    below, one = yield from four_pivots([list(entries) for entries in a])
    rest = [
        [a[4 + i][4 + j] - total_of([below[i][k] * below[j][k] for k in range(4)]) for j in range(i + 1)]
        for i in range(4)
    ]
    back = [[total_of([below[i][k] * one[k][j] for k in range(j, 4)]) for j in range(4)] for i in range(4)]
    _, two = yield from four_pivots(rest)
    corner = [[-total_of([two[i][m] * back[m][j] for m in range(i + 1)]) for j in range(4)] for i in range(4)]
    return one + [corner[i] + two[i] for i in range(4)]


def inverse_factor(strips):
    lane = lax.broadcasted_iota(jnp.int32, (STRIP, LANES), 1)
    level = lax.broadcasted_iota(jnp.int32, (STRIP, LANES), 0)
    strips = list(strips)
    result = [None] * len(strips)
    waiting = []

    def factor_columns(r, start, t):
        columns = [column(strips[r], start + j) for j in range(STRIP)]
        return [total_of([columns[j] * t[k][j] for j in range(k + 1)]) for k in range(STRIP)]

    def finish(p, t, found):
        start = p * STRIP
        own = (lane >= start) & (lane < start + STRIP)
        rows = []

        def scaled():
            entered = jnp.where(own, jnp.where(lane - start == level, 1.0, 0.0), strips[p])
            terms = []
            for k in range(STRIP):
                t_column = t[STRIP - 1][k]
                for i in range(STRIP - 2, k - 1, -1):
                    t_column = jnp.where(level == i, t[i][k], t_column)
                if k:
                    t_column = jnp.where(level < k, 0.0, t_column)
                terms.append(t_column * row(entered, k))
            done = total_of(terms)
            result[p] = jnp.where(lane < start + STRIP, done, 0.0)
            rows.extend(row(done, k) for k in range(STRIP))

        def updated(r):
            l_columns = found if r == p + 1 else factor_columns(r, start, t)
            update = total_of([l_columns[k] * rows[k] for k in range(STRIP)])
            strips[r] = jnp.where(own, 0.0, strips[r]) - update

        return [scaled] + [functools.partial(updated, r) for r in range(p + 1, len(strips))]

    columns = [column(strips[0], k) for k in range(STRIP)]
    for p in range(len(strips)):
        steps = small_inverse(columns)
        while True:
            try:
                next(steps)
            except StopIteration as ended:
                t = ended.value
                break
            for _ in range(2):
                if waiting:
                    waiting.pop(0)()
        while waiting:
            waiting.pop(0)()
        found = None
        if p + 1 < len(strips):
            start = p * STRIP
            found = factor_columns(p + 1, start, t)
            columns = [
                column(strips[p + 1], start + STRIP + j) - total_of([found[k] * row(found[k], j) for k in range(STRIP)])
                for j in range(STRIP)
            ]
        waiting = finish(p, t, found)
    while waiting:
        waiting.pop(0)()
    return result


def probe_kernel(pivot_ref, point_ref, coeff_ref, noise_ref, *refs):
    inverse_ref, probe_ref, sent_ref, high_ref, middle_ref, little_ref = refs[-6:]
    hp = lax.Precision.HIGHEST
    size = pivot_ref.shape[1]
    half = size // 2
    pivots = extended(pivot_ref[...], True).astype(jnp.bfloat16)
    others = extended(pivot_ref[...], False).astype(jnp.bfloat16)
    points = extended(point_ref[...], False).astype(jnp.bfloat16)
    cols = kernel_of(product(pivots, points, ((0,), (0,))))
    high_ref[...], middle_ref[...], little_ref[...] = thirds(cols)

    gram = kernel_of(product(pivots, others, ((0,), (0,))))
    equal = lax.broadcasted_iota(jnp.int32, gram.shape, 0) == lax.broadcasted_iota(jnp.int32, gram.shape, 1)
    gram = gram + jnp.where(equal, jitter, 0.0)

    def inverted(block):
        strips = [block[s:s + STRIP, :] for s in range(0, half, STRIP)]
        return jnp.concatenate(inverse_factor(strips), axis=0)

    one = inverted(gram[:half, :half])
    below = product(gram[half:, :half], one, ((1,), (1,)), hp)
    back = product(below, one, ((1,), (0,)), hp)
    two = inverted(gram[half:, half:] - product(below, below, ((1,), (1,)), hp))
    coeffs = coeff_ref[...]
    start = product(coeffs[:, :half], one, ((1,), (0,)), hp)
    later = product(coeffs[:, half:], two, ((1,), (0,)), hp)
    weights = jnp.concatenate([start - product(later, back, ((1,), (0,)), hp), later], axis=1)

    rows = weights.shape[0]
    stacked = jnp.concatenate(thirds(weights), axis=0)
    by_high = product(stacked, high_ref[...], ((1,), (0,)))
    by_middle = product(stacked[:2 * rows], middle_ref[...], ((1,), (0,)))
    by_little = product(stacked[:rows], little_ref[...], ((1,), (0,)))
    small = by_high[2 * rows:] + by_middle[rows:] + by_little
    probes = by_high[:rows] + (by_high[rows:2 * rows] + by_middle[:rows] + small) + noise_ref[...]
    probe_ref[...] = probes
    sent_ref[...] = probes.astype(jnp.bfloat16)

    inverse_ref[:half, :half] = one
    inverse_ref[:half, half:] = jnp.zeros((half, half), jnp.float32)
    inverse_ref[half:, :half] = -product(two, back, ((1,), (0,)), hp)
    inverse_ref[half:, half:] = two


def probes_of(pivots_t, points_t, coeffs_t, noise_t, awaited):
    size = pivots_t.shape[1]
    count = points_t.shape[1]
    return pl.pallas_call(
        probe_kernel,
        out_shape=(
            jax.ShapeDtypeStruct((size, size), jnp.float32),
            jax.ShapeDtypeStruct(noise_t.shape, jnp.float32),
            pltpu.VMEM(noise_t.shape, jnp.bfloat16),
        ),
        in_specs=in_vmem(4) + [pl.BlockSpec(memory_space=pl.ANY)] * len(awaited),
        out_specs=tuple(in_vmem(3)),
        scratch_shapes=[pltpu.VMEM((size, count), jnp.bfloat16)] * 3,
        compiler_params=pltpu.CompilerParams(vmem_limit_bytes=32 * 1024 * 1024),
        name="probes",
    )(pivots_t, points_t, coeffs_t, noise_t, *awaited)


def padded(value):
    return jnp.concatenate([value, jnp.zeros((LANES - value.shape[0], value.shape[1]), value.dtype)], axis=0)


def tile_terms(own, other, probes):
    return product(kernel_of(product(own, other, ((1,), (0,)))).astype(jnp.bfloat16), probes, ((1,), (1,)))


def factor_kernel(pivot_ref, point_ref, inverse_ref, awaited_ref, factor_ref, zero_ref):
    count = point_ref.shape[1]
    own = jnp.transpose(padded(extended(point_ref[...], True))).astype(jnp.bfloat16)
    pivots = padded(extended(pivot_ref[...], False)).astype(jnp.bfloat16)
    high, middle, _ = thirds(inverse_ref[...])
    for s in range(0, count, CHUNK):
        rows = own[s:s + CHUNK, :]
        cols_high, cols_middle, _ = thirds(kernel_of(product(rows, pivots, ((1,), (0,)))))
        factor_ref[s:s + CHUNK, :] = (
            product(cols_high, middle, ((1,), (1,))) + product(cols_middle, high, ((1,), (1,)))
        ) + product(cols_high, high, ((1,), (1,)))
    zero_ref[...] = jnp.zeros_like(zero_ref)


def factor_of(pivots_t, points_t, inverse, awaited):
    size = pivots_t.shape[1]
    depth, count = points_t.shape
    return pl.pallas_call(
        factor_kernel,
        out_shape=(
            jax.ShapeDtypeStruct((count, size), jnp.float32),
            pltpu.VMEM((depth, count), jnp.bfloat16),
        ),
        in_specs=in_vmem(3) + [pl.BlockSpec(memory_space=pl.ANY)],
        out_specs=tuple(in_vmem(2)),
        compiler_params=pltpu.CompilerParams(vmem_limit_bytes=32 * 1024 * 1024),
        cost_estimate=pl.CostEstimate(
            flops=6 * count * size * size,
            bytes_accessed=6 * count * size,
            transcendentals=count * size,
        ),
        name="factor",
    )(pivots_t, points_t, inverse, awaited)


def band_kernel(pieces, first, last, *refs):
    own_ref = refs[0]
    depth, count = own_ref.shape
    rest = list(refs[1 + max(place for piece in pieces for place, _ in piece):])
    before_ref = None if first else rest.pop(0)
    own = jnp.transpose(padded(extended(own_ref[...], True))).astype(jnp.bfloat16)
    blocks = []
    for (point_at, point_row), (probe_at, probe_row) in pieces:
        points = refs[point_at][point_row:point_row + depth, :]
        blocks.append((padded(extended(points, False)).astype(jnp.bfloat16), refs[probe_at], probe_row))
    for s in range(0, count, CHUNK):
        total = None if first else before_ref[s:s + CHUNK, :]
        for other, probe_ref, probe_row in blocks:
            term = tile_terms(own[s:s + CHUNK, :], other, probe_ref[probe_row:, :])
            total = term if total is None else total + term
        if last:
            probe_ref, out_ref = rest
            scale = 1.0 / (count ** 0.5)
            out_ref[:, s:s + CHUNK] = jnp.transpose(total) * scale + noise_weight * probe_ref[:, s:s + CHUNK]
        else:
            rest[0][s:s + CHUNK, :] = total
    if not last:
        rest[1][...] = jnp.zeros_like(rest[1])


def band_sum(own, pieces, before=None, probes=None):
    depth, count = own.shape
    first, last = before is None, probes is not None
    operands = [own]
    places = []
    for piece in pieces:
        place = []
        for array, start in piece:
            known = [i for i, operand in enumerate(operands) if operand is array]
            if not known:
                operands.append(array)
            place.append((known[0] if known else len(operands) - 1, start))
        places.append(tuple(place))
    array, start = pieces[0][1]
    width = array.shape[0] - start
    operands += ([] if first else [before]) + ([probes] if last else [])
    if last:
        out_shape = jax.ShapeDtypeStruct((width, count), jnp.float32)
    else:
        out_shape = (jax.ShapeDtypeStruct((count, width), jnp.float32), pltpu.VMEM((width, count), jnp.bfloat16))
    return pl.pallas_call(
        functools.partial(band_kernel, tuple(places), first, last),
        out_shape=out_shape,
        in_specs=in_vmem(len(operands)),
        out_specs=in_vmem(1)[0] if last else tuple(in_vmem(2)),
        compiler_params=pltpu.CompilerParams(vmem_limit_bytes=32 * 1024 * 1024),
        cost_estimate=pl.CostEstimate(
            flops=len(pieces) * 4 * count * count * LANES,
            bytes_accessed=4 * count * width * len(operands),
            transcendentals=len(pieces) * count * count,
        ),
        name="band_sum",
    )(*operands)


def shards(points, pivots, owners, coeffs, noise):
    tall = lax.axis_size("gy") == BAND + 1
    points = points.T
    depth = points.shape[0]
    pivot_points = spread(pick(owners, pivots, points))
    if tall:
        far = swapped(points, "gy", 2)
        pair = swapped(jnp.concatenate([points, far], axis=0), "gy", 1)
        near = [far, pair]
    else:
        near = direct_blocks(points)

    inverse, probes, sent = probes_of(pivot_points, points, coeffs.T, noise.T, near)
    total, zeros = band_sum(points, [((points, 0), (sent, 0))])
    if tall:
        two = swapped(sent, "gy", 2)
        one = swapped(sent, "gy", 1) + zeros
        factor, zeros = factor_of(pivot_points, points, inverse, one)
        two = two + zeros
        cross_one = cross(jnp.concatenate([pair[:depth], one], axis=0), 1)
        three = swapped(two, "gy", 1)
        cross_two = cross(jnp.concatenate([far, two], axis=0), 2)
        total, zeros = band_sum(points, [((pair, 0), (one, 0)), ((far, 0), (two, 0))], total)
        cross_three = cross(jnp.concatenate([pair[depth:], three + zeros], axis=0), 3)
        crossed = [((stacked, 0), (stacked, depth)) for stacked in (cross_one, cross_two, cross_three)]
        total, _ = band_sum(points, crossed[:2] + [((pair, depth), (three, 0))], total)
        kernel_probes = band_sum(points, crossed[2:], total, probes)
    else:
        factor, _ = factor_of(pivot_points, points, inverse, zeros)
        pieces = [((block, 0), (probe, 0)) for block, probe in zip(near, direct_blocks(sent))]
        total, _ = band_sum(points, pieces[:3], total)
        kernel_probes = band_sum(points, pieces[3:], total, probes)
    return (kernel_probes.T, factor)


def solution(mesh):
    in_specs = (P(("gx", "gy"), None), P(), P(), P(), P(("gx", "gy"), None))
    out_specs = (P(("gx", "gy"), None), P(("gx", "gy"), None))
    return jax.shard_map(shards, mesh=mesh, in_specs=in_specs, out_specs=out_specs, check_vma=False)
```

```python
import functools
import math

import jax
import jax.numpy as jnp
from jax import lax
from jax.experimental import pallas as pl
from jax.experimental.pallas import tpu as pltpu
from jax.sharding import PartitionSpec as P

PIVOTS = 128
KERNEL_SCALE = 32
BAND = 3
STRIP = 8
LANES = 128
EXTRA = 16
CHUNK = 256
SHORT = pl.CostEstimate(flops=1, bytes_accessed=1, transcendentals=0)
LONG = pl.CostEstimate(flops=1 << 34, bytes_accessed=1, transcendentals=0)


jitter = 0.1
noise_weight = 0.5


def shifted(value, axis, steps):
    count = lax.axis_size(axis)
    return lax.ppermute(value, axis, [((i + steps) % count, i) for i in range(count)])


def swapped(value, axis, bit):
    return lax.ppermute(value, axis, [(i ^ bit, i) for i in range(lax.axis_size(axis))])


def spread(value):
    for axis in ("gy", "gx"):
        count = lax.axis_size(axis)
        bit = 1
        while bit < count:
            wide = 2 if (count // bit).bit_length() % 2 == 0 else 4
            value = sum((swapped(value, axis, bit * k) for k in range(1, wide)), value)
            bit *= wide
    return value


def zero_like(value):
    return jnp.minimum(jnp.abs(value), 0)


def cross(piece, bits):
    outer, inner = lax.axis_size("gx"), lax.axis_size("gy")
    pairs = []
    for x in range(outer):
        for z in range(inner):
            source = (x - 1 if z ^ bits > z else x + 1) % outer
            pairs.append((source * inner + z, x * inner + z))
    return lax.ppermute(piece, ("gx", "gy"), pairs)


def direct_blocks(value):
    return [shifted(value, ("gx", "gy"), k) for k in range(-BAND, BAND + 1) if k != 0]


def in_vmem(count):
    return [pl.BlockSpec(memory_space=pltpu.VMEM)] * count


def thirds(value):
    high = value.astype(jnp.bfloat16)
    rest = value - high.astype(jnp.float32)
    middle = rest.astype(jnp.bfloat16)
    return high, middle, (rest - middle.astype(jnp.float32)).astype(jnp.bfloat16)


def product(left, right, contract, precision=None):
    return lax.dot_general(
        left, right, (contract, ((), ())), precision=precision, preferred_element_type=jnp.float32
    )


def extended(columns, ones_first):
    wide = columns.astype(jnp.float32)
    half = -0.5 * jnp.sum(wide * wide, axis=0, keepdims=True)
    terms = [term.astype(jnp.float32) for term in thirds(half)]
    shape = (EXTRA, columns.shape[1])
    level = lax.broadcasted_iota(jnp.int32, shape, 0)
    first = 0 if ones_first else 3
    below = jnp.where((level >= first) & (level < first + 3), 1.0, 0.0)
    for i, term in enumerate(terms):
        below = jnp.where(level == 3 - first + i, jnp.broadcast_to(term, shape), below)
    return jnp.concatenate([wide, below], axis=0)


def kernel_of(product_of_extended):
    return jnp.exp2(product_of_extended * (2.0 / KERNEL_SCALE * math.log2(math.e)))


def pick_kernel(owner_ref, pivot_ref, point_ref, out_ref):
    count = point_ref.shape[1]
    me = lax.axis_index(("gx", "gy"))
    wanted = [jnp.where(owner_ref[r] == me, pivot_ref[r:r + 1, :], -1) for r in range(2)]
    wanted = jnp.concatenate(wanted, axis=1)
    place = lax.broadcasted_iota(jnp.int32, (count, wanted.shape[1]), 0)
    chosen = jnp.where(place == wanted, 1.0, 0.0).astype(jnp.bfloat16)
    out_ref[...] = product(point_ref[...], chosen, ((1,), (0,))).astype(jnp.bfloat16)


def pick(owners, pivots, points_t):
    return pl.pallas_call(
        pick_kernel,
        out_shape=pltpu.VMEM((points_t.shape[0], 2 * PIVOTS), jnp.bfloat16),
        in_specs=[pl.BlockSpec(memory_space=pltpu.SMEM)] + in_vmem(2),
        out_specs=in_vmem(1)[0],
        name="pick",
    )(owners, pivots, points_t)


def column(strip, lane):
    return jnp.broadcast_to(strip[:, lane:lane + 1], strip.shape)


def row(strip, i):
    return jnp.broadcast_to(strip[i:i + 1, :], strip.shape)


def total_of(terms):
    while len(terms) > 1:
        terms = [terms[i] + terms[i + 1] if i + 1 < len(terms) else terms[i] for i in range(0, len(terms), 2)]
    return terms[0]


def four_pivots(a):
    rows = len(a)
    x = [[None] * 4 for _ in range(4)]
    scale = [None] * 4
    product_so_far = None
    for k in range(4):
        pivot = a[k][k]
        x[k][k] = product_so_far
        product_so_far = pivot if k == 0 else product_so_far * pivot
        scale[k] = lax.rsqrt(product_so_far)
        for i in range(k + 1, rows):
            for j in range(k + 1, min(i, 3) + 1):
                a[i][j] = pivot * a[i][j] - a[i][k] * a[j][k]
        for i in range(k + 1, 4):
            for j in range(k):
                x[i][j] = pivot * x[i][j] - a[i][k] * x[k][j]
            x[i][k] = -a[i][k] if k == 0 else -a[i][k] * x[k][k]
        yield
    factor = [[a[i][k] * scale[k] for k in range(4)] for i in range(4, rows)]
    inverse = [[scale[i] if x[i][j] is None else x[i][j] * scale[i] for j in range(i + 1)] for i in range(4)]
    return factor, inverse


def small_inverse(columns):
    a = [[row(columns[k], i) for k in range(i + 1)] for i in range(STRIP)]
    yield
    below, one = yield from four_pivots([list(entries) for entries in a])
    rest = [
        [a[4 + i][4 + j] - total_of([below[i][k] * below[j][k] for k in range(4)]) for j in range(i + 1)]
        for i in range(4)
    ]
    back = [[total_of([below[i][k] * one[k][j] for k in range(j, 4)]) for j in range(4)] for i in range(4)]
    _, two = yield from four_pivots(rest)
    corner = [[-total_of([two[i][m] * back[m][j] for m in range(i + 1)]) for j in range(4)] for i in range(4)]
    return one + [corner[i] + two[i] for i in range(4)]


def inverse_factor(strips):
    lane = lax.broadcasted_iota(jnp.int32, (STRIP, LANES), 1)
    level = lax.broadcasted_iota(jnp.int32, (STRIP, LANES), 0)
    strips = list(strips)
    result = [None] * len(strips)
    waiting = []

    def factor_columns(r, start, t):
        columns = [column(strips[r], start + j) for j in range(STRIP)]
        return [total_of([columns[j] * t[k][j] for j in range(k + 1)]) for k in range(STRIP)]

    def finish(p, t, found):
        start = p * STRIP
        own = (lane >= start) & (lane < start + STRIP)
        rows = []

        def scaled():
            entered = jnp.where(own, jnp.where(lane - start == level, 1.0, 0.0), strips[p])
            terms = []
            for k in range(STRIP):
                t_column = t[STRIP - 1][k]
                for i in range(STRIP - 2, k - 1, -1):
                    t_column = jnp.where(level == i, t[i][k], t_column)
                if k:
                    t_column = jnp.where(level < k, 0.0, t_column)
                terms.append(t_column * row(entered, k))
            done = total_of(terms)
            result[p] = jnp.where(lane < start + STRIP, done, 0.0)
            rows.extend(row(done, k) for k in range(STRIP))

        def updated(r):
            l_columns = found if r == p + 1 else factor_columns(r, start, t)
            update = total_of([l_columns[k] * rows[k] for k in range(STRIP)])
            strips[r] = jnp.where(own, 0.0, strips[r]) - update

        return [scaled] + [functools.partial(updated, r) for r in range(p + 1, len(strips))]

    columns = [column(strips[0], k) for k in range(STRIP)]
    for p in range(len(strips)):
        steps = small_inverse(columns)
        while True:
            try:
                next(steps)
            except StopIteration as ended:
                t = ended.value
                break
            for _ in range(2):
                if waiting:
                    waiting.pop(0)()
        while waiting:
            waiting.pop(0)()
        found = None
        if p + 1 < len(strips):
            start = p * STRIP
            found = factor_columns(p + 1, start, t)
            columns = [
                column(strips[p + 1], start + STRIP + j) - total_of([found[k] * row(found[k], j) for k in range(STRIP)])
                for j in range(STRIP)
            ]
        waiting = finish(p, t, found)
    while waiting:
        waiting.pop(0)()
    return result


def probe_kernel(pivot_ref, point_ref, coeff_ref, noise_ref, *refs):
    inverse_ref, probe_ref, sent_ref, high_ref, middle_ref, little_ref = refs[-6:]
    hp = lax.Precision.HIGHEST
    size = pivot_ref.shape[1]
    half = size // 2
    pivots = extended(pivot_ref[...], True).astype(jnp.bfloat16)
    others = extended(pivot_ref[...], False).astype(jnp.bfloat16)
    points = extended(point_ref[...], False).astype(jnp.bfloat16)
    cols = kernel_of(product(pivots, points, ((0,), (0,))))
    high_ref[...], middle_ref[...], little_ref[...] = thirds(cols)

    gram = kernel_of(product(pivots, others, ((0,), (0,))))
    equal = lax.broadcasted_iota(jnp.int32, gram.shape, 0) == lax.broadcasted_iota(jnp.int32, gram.shape, 1)
    gram = gram + jnp.where(equal, jitter, 0.0)

    def inverted(block):
        strips = [block[s:s + STRIP, :] for s in range(0, half, STRIP)]
        return jnp.concatenate(inverse_factor(strips), axis=0)

    one = inverted(gram[:half, :half])
    below = product(gram[half:, :half], one, ((1,), (1,)), hp)
    back = product(below, one, ((1,), (0,)), hp)
    two = inverted(gram[half:, half:] - product(below, below, ((1,), (1,)), hp))
    coeffs = coeff_ref[...]
    start = product(coeffs[:, :half], one, ((1,), (0,)), hp)
    later = product(coeffs[:, half:], two, ((1,), (0,)), hp)
    weights = jnp.concatenate([start - product(later, back, ((1,), (0,)), hp), later], axis=1)

    rows = weights.shape[0]
    stacked = jnp.concatenate(thirds(weights), axis=0)
    by_high = product(stacked, high_ref[...], ((1,), (0,)))
    by_middle = product(stacked[:2 * rows], middle_ref[...], ((1,), (0,)))
    by_little = product(stacked[:rows], little_ref[...], ((1,), (0,)))
    small = by_high[2 * rows:] + by_middle[rows:] + by_little
    probes = by_high[:rows] + (by_high[rows:2 * rows] + by_middle[:rows] + small) + noise_ref[...]
    probe_ref[...] = probes
    sent_ref[...] = probes.astype(jnp.bfloat16)

    inverse_ref[:half, :half] = one
    inverse_ref[:half, half:] = jnp.zeros((half, half), jnp.float32)
    inverse_ref[half:, :half] = -product(two, back, ((1,), (0,)), hp)
    inverse_ref[half:, half:] = two


def probes_of(pivots_t, points_t, coeffs_t, noise_t, awaited):
    size = pivots_t.shape[1]
    count = points_t.shape[1]
    return pl.pallas_call(
        probe_kernel,
        out_shape=(
            jax.ShapeDtypeStruct((size, size), jnp.float32),
            jax.ShapeDtypeStruct(noise_t.shape, jnp.float32),
            pltpu.VMEM(noise_t.shape, jnp.bfloat16),
        ),
        in_specs=in_vmem(4) + [pl.BlockSpec(memory_space=pl.ANY)] * len(awaited),
        out_specs=tuple(in_vmem(3)),
        scratch_shapes=[pltpu.VMEM((size, count), jnp.bfloat16)] * 3,
        cost_estimate=LONG,
        compiler_params=pltpu.CompilerParams(vmem_limit_bytes=32 * 1024 * 1024),
        name="probes",
    )(pivots_t, points_t, coeffs_t, noise_t, *awaited)


def padded(value):
    return jnp.concatenate([value, jnp.zeros((LANES - value.shape[0], value.shape[1]), value.dtype)], axis=0)


def tile_terms(own, other, probes):
    return product(kernel_of(product(own, other, ((1,), (0,)))).astype(jnp.bfloat16), probes, ((1,), (1,)))


def factor_kernel(pivot_ref, point_ref, inverse_ref, awaited_ref, factor_ref, zero_ref):
    count = point_ref.shape[1]
    own = jnp.transpose(padded(extended(point_ref[...], True))).astype(jnp.bfloat16)
    pivots = padded(extended(pivot_ref[...], False)).astype(jnp.bfloat16)
    high, middle, _ = thirds(inverse_ref[...])
    for s in range(0, count, CHUNK):
        rows = own[s:s + CHUNK, :]
        cols_high, cols_middle, _ = thirds(kernel_of(product(rows, pivots, ((1,), (0,)))))
        factor_ref[s:s + CHUNK, :] = (
            product(cols_high, middle, ((1,), (1,))) + product(cols_middle, high, ((1,), (1,)))
        ) + product(cols_high, high, ((1,), (1,)))
    zero_ref[...] = jnp.zeros_like(zero_ref)


def factor_of(pivots_t, points_t, inverse, awaited):
    size = pivots_t.shape[1]
    depth, count = points_t.shape
    return pl.pallas_call(
        factor_kernel,
        out_shape=(
            jax.ShapeDtypeStruct((count, size), jnp.float32),
            pltpu.VMEM((depth, count), jnp.bfloat16),
        ),
        in_specs=in_vmem(3) + [pl.BlockSpec(memory_space=pl.ANY)],
        out_specs=tuple(in_vmem(2)),
        compiler_params=pltpu.CompilerParams(vmem_limit_bytes=32 * 1024 * 1024),
        cost_estimate=SHORT,
        name="factor",
    )(pivots_t, points_t, inverse, awaited)


def band_kernel(pieces, first, last, *refs):
    own_ref = refs[0]
    depth, count = own_ref.shape
    rest = list(refs[1 + max(place for piece in pieces for place, _ in piece):])
    before_ref = None if first else rest.pop(0)
    own = jnp.transpose(padded(extended(own_ref[...], True))).astype(jnp.bfloat16)
    blocks = []
    for (point_at, point_row), (probe_at, probe_row) in pieces:
        points = refs[point_at][point_row:point_row + depth, :]
        blocks.append((padded(extended(points, False)).astype(jnp.bfloat16), refs[probe_at], probe_row))
    for s in range(0, count, CHUNK):
        total = None if first else before_ref[s:s + CHUNK, :]
        for other, probe_ref, probe_row in blocks:
            term = tile_terms(own[s:s + CHUNK, :], other, probe_ref[probe_row:, :])
            total = term if total is None else total + term
        if last:
            probe_ref, out_ref = rest
            scale = 1.0 / (count ** 0.5)
            out_ref[:, s:s + CHUNK] = jnp.transpose(total) * scale + noise_weight * probe_ref[:, s:s + CHUNK]
        else:
            rest[0][s:s + CHUNK, :] = total
    if not last:
        rest[1][...] = jnp.zeros_like(rest[1])


def band_sum(own, pieces, before=None, probes=None):
    depth, count = own.shape
    first, last = before is None, probes is not None
    operands = [own]
    places = []
    for piece in pieces:
        place = []
        for array, start in piece:
            known = [i for i, operand in enumerate(operands) if operand is array]
            if not known:
                operands.append(array)
            place.append((known[0] if known else len(operands) - 1, start))
        places.append(tuple(place))
    array, start = pieces[0][1]
    width = array.shape[0] - start
    operands += ([] if first else [before]) + ([probes] if last else [])
    if last:
        out_shape = jax.ShapeDtypeStruct((width, count), jnp.float32)
    else:
        out_shape = (jax.ShapeDtypeStruct((count, width), jnp.float32), pltpu.VMEM((width, count), jnp.bfloat16))
    return pl.pallas_call(
        functools.partial(band_kernel, tuple(places), first, last),
        out_shape=out_shape,
        in_specs=in_vmem(len(operands)),
        out_specs=in_vmem(1)[0] if last else tuple(in_vmem(2)),
        compiler_params=pltpu.CompilerParams(vmem_limit_bytes=32 * 1024 * 1024),
        cost_estimate=SHORT,
        name="band_sum",
    )(*operands)


def shards(points, pivots, owners, coeffs, noise):
    tall = lax.axis_size("gy") == BAND + 1
    points = points.T
    depth = points.shape[0]
    pivot_points = spread(pick(owners, pivots, points))
    if tall:
        far = swapped(points, "gy", 2)
        pair = swapped(jnp.concatenate([points, far], axis=0), "gy", 1)
        crossing_one = cross(pair[:depth], 1)
        crossing_pair = cross(jnp.concatenate([far, pair[depth:]], axis=0), 2)
        near = [far, pair]
    else:
        near = direct_blocks(points)

    inverse, probes, sent = probes_of(pivot_points, points, coeffs.T, noise.T, near)
    total, zeros = band_sum(points, [((points, 0), (sent, 0))])
    if tall:
        leaving = sent + zero_like(crossing_one) + zero_like(crossing_pair[:depth])
        two = swapped(leaving, "gy", 2)
        one = swapped(leaving, "gy", 1) + zeros
        factor, zeros = factor_of(pivot_points, points, inverse, one)
        two = two + zeros
        three = swapped(two, "gy", 1)
        cross_one, cross_two = cross(one, 1), cross(two, 2)
        total, zeros = band_sum(points, [((pair, 0), (one, 0)), ((far, 0), (two, 0))], total)
        three = three + zeros
        cross_three = cross(three, 3)
        pieces = [((crossing_one, 0), (cross_one, 0)), ((crossing_pair, 0), (cross_two, 0)), ((pair, depth), (three, 0))]
        total, _ = band_sum(points, pieces, total)
        kernel_probes = band_sum(points, [((crossing_pair, depth), (cross_three, 0))], total, probes)
    else:
        factor, _ = factor_of(pivot_points, points, inverse, zeros)
        pieces = [((block, 0), (probe, 0)) for block, probe in zip(near, direct_blocks(sent))]
        total, _ = band_sum(points, pieces[:3], total)
        kernel_probes = band_sum(points, pieces[3:], total, probes)
    return (kernel_probes.T, factor)


def solution(mesh):
    in_specs = (P(("gx", "gy"), None), P(), P(), P(), P(("gx", "gy"), None))
    out_specs = (P(("gx", "gy"), None), P(("gx", "gy"), None))
    return jax.shard_map(shards, mesh=mesh, in_specs=in_specs, out_specs=out_specs, check_vma=False)
```

```python
import functools
import math

import jax
import jax.numpy as jnp
from jax import lax
from jax.experimental import pallas as pl
from jax.experimental.pallas import tpu as pltpu
from jax.sharding import PartitionSpec as P

PIVOTS = 128
KERNEL_SCALE = 32
BAND = 3
STRIP = 8
LANES = 128
EXTRA = 16
CHUNK = 256
SHORT = pl.CostEstimate(flops=1, bytes_accessed=1, transcendentals=0)
LONG = pl.CostEstimate(flops=1 << 34, bytes_accessed=1, transcendentals=0)


jitter = 0.1
noise_weight = 0.5


def shifted(value, axis, steps):
    count = lax.axis_size(axis)
    return lax.ppermute(value, axis, [((i + steps) % count, i) for i in range(count)])


def swapped(value, axis, bit):
    return lax.ppermute(value, axis, [(i ^ bit, i) for i in range(lax.axis_size(axis))])


def spread(value, axis):
    count = lax.axis_size(axis)
    bit = 1
    while bit < count:
        wide = 2 if (count // bit).bit_length() % 2 == 0 else 4
        value = sum((swapped(value, axis, bit * k) for k in range(1, wide)), value)
        bit *= wide
    return value


def zero_like(value):
    return jnp.minimum(jnp.abs(value), 0)


def cross(piece, bits):
    outer, inner = lax.axis_size("gx"), lax.axis_size("gy")
    pairs = []
    for x in range(outer):
        for z in range(inner):
            source = (x - 1 if z ^ bits > z else x + 1) % outer
            pairs.append((source * inner + z, x * inner + z))
    return lax.ppermute(piece, ("gx", "gy"), pairs)


def direct_blocks(value):
    return [shifted(value, ("gx", "gy"), k) for k in range(-BAND, BAND + 1) if k != 0]


def in_vmem(count):
    return [pl.BlockSpec(memory_space=pltpu.VMEM)] * count


def thirds(value):
    high = value.astype(jnp.bfloat16)
    rest = value - high.astype(jnp.float32)
    middle = rest.astype(jnp.bfloat16)
    return high, middle, (rest - middle.astype(jnp.float32)).astype(jnp.bfloat16)


def product(left, right, contract, precision=None):
    return lax.dot_general(
        left, right, (contract, ((), ())), precision=precision, preferred_element_type=jnp.float32
    )


def extended(columns, ones_first):
    wide = columns.astype(jnp.float32)
    half = -0.5 * jnp.sum(wide * wide, axis=0, keepdims=True)
    terms = [term.astype(jnp.float32) for term in thirds(half)]
    shape = (EXTRA, columns.shape[1])
    level = lax.broadcasted_iota(jnp.int32, shape, 0)
    first = 0 if ones_first else 3
    below = jnp.where((level >= first) & (level < first + 3), 1.0, 0.0)
    for i, term in enumerate(terms):
        below = jnp.where(level == 3 - first + i, jnp.broadcast_to(term, shape), below)
    return jnp.concatenate([wide, below], axis=0)


def kernel_of(product_of_extended):
    return jnp.exp2(product_of_extended * (2.0 / KERNEL_SCALE * math.log2(math.e)))


def pick_kernel(owner_ref, pivot_ref, point_ref, out_ref):
    count = point_ref.shape[1]
    me = lax.axis_index(("gx", "gy"))
    wanted = [jnp.where(owner_ref[r] == me, pivot_ref[r:r + 1, :], -1) for r in range(2)]
    wanted = jnp.concatenate(wanted, axis=1)
    place = lax.broadcasted_iota(jnp.int32, (count, wanted.shape[1]), 0)
    chosen = jnp.where(place == wanted, 1.0, 0.0).astype(jnp.bfloat16)
    out_ref[...] = product(point_ref[...], chosen, ((1,), (0,))).astype(jnp.bfloat16)


def pick(owners, pivots, points_t):
    return pl.pallas_call(
        pick_kernel,
        out_shape=pltpu.VMEM((points_t.shape[0], 2 * PIVOTS), jnp.bfloat16),
        in_specs=[pl.BlockSpec(memory_space=pltpu.SMEM)] + in_vmem(2),
        out_specs=in_vmem(1)[0],
        name="pick",
    )(owners, pivots, points_t)


def column(strip, lane):
    return jnp.broadcast_to(strip[:, lane:lane + 1], strip.shape)


def row(strip, i):
    return jnp.broadcast_to(strip[i:i + 1, :], strip.shape)


def total_of(terms):
    while len(terms) > 1:
        terms = [terms[i] + terms[i + 1] if i + 1 < len(terms) else terms[i] for i in range(0, len(terms), 2)]
    return terms[0]


def four_pivots(a):
    rows = len(a)
    x = [[None] * 4 for _ in range(4)]
    scale = [None] * 4
    product_so_far = None
    for k in range(4):
        pivot = a[k][k]
        x[k][k] = product_so_far
        product_so_far = pivot if k == 0 else product_so_far * pivot
        scale[k] = lax.rsqrt(product_so_far)
        for i in range(k + 1, rows):
            for j in range(k + 1, min(i, 3) + 1):
                a[i][j] = pivot * a[i][j] - a[i][k] * a[j][k]
        for i in range(k + 1, 4):
            for j in range(k):
                x[i][j] = pivot * x[i][j] - a[i][k] * x[k][j]
            x[i][k] = -a[i][k] if k == 0 else -a[i][k] * x[k][k]
        yield
    factor = [[a[i][k] * scale[k] for k in range(4)] for i in range(4, rows)]
    inverse = [[scale[i] if x[i][j] is None else x[i][j] * scale[i] for j in range(i + 1)] for i in range(4)]
    return factor, inverse


def small_inverse(columns):
    a = [[row(columns[k], i) for k in range(i + 1)] for i in range(STRIP)]
    yield
    below, one = yield from four_pivots([list(entries) for entries in a])
    rest = [
        [a[4 + i][4 + j] - total_of([below[i][k] * below[j][k] for k in range(4)]) for j in range(i + 1)]
        for i in range(4)
    ]
    back = [[total_of([below[i][k] * one[k][j] for k in range(j, 4)]) for j in range(4)] for i in range(4)]
    _, two = yield from four_pivots(rest)
    corner = [[-total_of([two[i][m] * back[m][j] for m in range(i + 1)]) for j in range(4)] for i in range(4)]
    return one + [corner[i] + two[i] for i in range(4)]


def inverse_factor(strips, beside):
    lane = lax.broadcasted_iota(jnp.int32, (STRIP, LANES), 1)
    level = lax.broadcasted_iota(jnp.int32, (STRIP, LANES), 0)
    strips = list(strips)
    result = [None] * len(strips)
    waiting = []

    def factor_columns(r, start, t):
        columns = [column(strips[r], start + j) for j in range(STRIP)]
        return [total_of([columns[j] * t[k][j] for j in range(k + 1)]) for k in range(STRIP)]

    def finish(p, t, found):
        start = p * STRIP
        own = (lane >= start) & (lane < start + STRIP)
        rows = []

        def scaled():
            entered = jnp.where(own, jnp.where(lane - start == level, 1.0, 0.0), strips[p])
            terms = []
            for k in range(STRIP):
                t_column = t[STRIP - 1][k]
                for i in range(STRIP - 2, k - 1, -1):
                    t_column = jnp.where(level == i, t[i][k], t_column)
                if k:
                    t_column = jnp.where(level < k, 0.0, t_column)
                terms.append(t_column * row(entered, k))
            done = total_of(terms)
            result[p] = jnp.where(lane < start + STRIP, done, 0.0)
            rows.extend(row(done, k) for k in range(STRIP))

        def updated(r):
            l_columns = found if r == p + 1 else factor_columns(r, start, t)
            update = total_of([l_columns[k] * rows[k] for k in range(STRIP)])
            strips[r] = jnp.where(own, 0.0, strips[r]) - update

        return [scaled] + [functools.partial(updated, r) for r in range(p + 1, len(strips))]

    columns = [column(strips[0], k) for k in range(STRIP)]
    for p in range(len(strips)):
        if beside:
            waiting.append(beside.pop(0))
        steps = small_inverse(columns)
        while True:
            try:
                next(steps)
            except StopIteration as ended:
                t = ended.value
                break
            for _ in range(2):
                if waiting:
                    waiting.pop(0)()
        while waiting:
            waiting.pop(0)()
        found = None
        if p + 1 < len(strips):
            start = p * STRIP
            found = factor_columns(p + 1, start, t)
            columns = [
                column(strips[p + 1], start + STRIP + j) - total_of([found[k] * row(found[k], j) for k in range(STRIP)])
                for j in range(STRIP)
            ]
        waiting = finish(p, t, found)
    while waiting:
        waiting.pop(0)()
    return result


def probe_kernel(
    pivot_ref, point_ref, coeff_ref, noise_ref, inverse_ref, probe_ref, sent_ref, high_ref, middle_ref, little_ref
):
    hp = lax.Precision.HIGHEST
    size = pivot_ref.shape[1]
    half = size // 2
    pivots = jnp.transpose(padded(extended(pivot_ref[...], True))).astype(jnp.bfloat16)
    others = padded(extended(pivot_ref[...], False)).astype(jnp.bfloat16)
    points = padded(extended(point_ref[...], False)).astype(jnp.bfloat16)

    def columns_at(start):
        at = slice(start, start + LANES)
        cols = kernel_of(product(pivots, points[:, at], ((1,), (0,))))
        high_ref[:, at], middle_ref[:, at], little_ref[:, at] = thirds(cols)

    gram = kernel_of(product(pivots, others, ((1,), (0,))))
    equal = lax.broadcasted_iota(jnp.int32, gram.shape, 0) == lax.broadcasted_iota(jnp.int32, gram.shape, 1)
    gram = gram + jnp.where(equal, jitter, 0.0)

    def inverted(block, beside):
        strips = [block[s:s + STRIP, :] for s in range(0, half, STRIP)]
        return jnp.concatenate(inverse_factor(strips, beside), axis=0)

    beside = [functools.partial(columns_at, start) for start in range(0, points.shape[1], LANES)]
    one = inverted(gram[:half, :half], beside)
    below = product(gram[half:, :half], one, ((1,), (1,)), hp)
    back = product(below, one, ((1,), (0,)), hp)
    two = inverted(gram[half:, half:] - product(below, below, ((1,), (1,)), hp), beside)
    coeffs = coeff_ref[...]
    start = product(coeffs[:, :half], one, ((1,), (0,)), hp)
    later = product(coeffs[:, half:], two, ((1,), (0,)), hp)
    weights = jnp.concatenate([start - product(later, back, ((1,), (0,)), hp), later], axis=1)

    rows = weights.shape[0]
    stacked = jnp.concatenate(thirds(weights), axis=0)
    by_high = product(stacked, high_ref[...], ((1,), (0,)))
    by_middle = product(stacked[:2 * rows], middle_ref[...], ((1,), (0,)))
    by_little = product(stacked[:rows], little_ref[...], ((1,), (0,)))
    small = by_high[2 * rows:] + by_middle[rows:] + by_little
    probes = by_high[:rows] + (by_high[rows:2 * rows] + by_middle[:rows] + small) + noise_ref[...]
    probe_ref[...] = probes
    sent_ref[...] = probes.astype(jnp.bfloat16)

    inverse_ref[:half, :half] = one
    inverse_ref[:half, half:] = jnp.zeros((half, half), jnp.float32)
    inverse_ref[half:, :half] = -product(two, back, ((1,), (0,)), hp)
    inverse_ref[half:, half:] = two


def probes_of(pivots_t, points_t, coeffs_t, noise_t):
    size = pivots_t.shape[1]
    count = points_t.shape[1]
    return pl.pallas_call(
        probe_kernel,
        out_shape=(
            pltpu.VMEM((size, size), jnp.float32),
            pltpu.VMEM(noise_t.shape, jnp.float32),
            pltpu.VMEM(noise_t.shape, jnp.bfloat16),
        ),
        in_specs=in_vmem(4),
        out_specs=tuple(in_vmem(3)),
        scratch_shapes=[pltpu.VMEM((size, count), jnp.bfloat16)] * 3,
        cost_estimate=LONG,
        compiler_params=pltpu.CompilerParams(vmem_limit_bytes=32 * 1024 * 1024),
        name="probes",
    )(pivots_t, points_t, coeffs_t, noise_t)


def padded(value):
    return jnp.concatenate([value, jnp.zeros((LANES - value.shape[0], value.shape[1]), value.dtype)], axis=0)


def tile_terms(own, other, probes):
    return product(kernel_of(product(own, other, ((1,), (0,)))).astype(jnp.bfloat16), probes, ((1,), (1,)))


def factor_kernel(pivot_ref, point_ref, inverse_ref, awaited_ref, factor_ref, zero_ref):
    count = point_ref.shape[1]
    own = jnp.transpose(padded(extended(point_ref[...], True))).astype(jnp.bfloat16)
    pivots = padded(extended(pivot_ref[...], False)).astype(jnp.bfloat16)
    high, middle, _ = thirds(inverse_ref[...])
    for s in range(0, count, CHUNK):
        rows = own[s:s + CHUNK, :]
        cols_high, cols_middle, _ = thirds(kernel_of(product(rows, pivots, ((1,), (0,)))))
        factor_ref[s:s + CHUNK, :] = (
            product(cols_high, middle, ((1,), (1,))) + product(cols_middle, high, ((1,), (1,)))
        ) + product(cols_high, high, ((1,), (1,)))
    zero_ref[...] = jnp.zeros_like(zero_ref)


def factor_of(pivots_t, points_t, inverse, awaited):
    size = pivots_t.shape[1]
    depth, count = points_t.shape
    return pl.pallas_call(
        factor_kernel,
        out_shape=(
            jax.ShapeDtypeStruct((count, size), jnp.float32),
            pltpu.VMEM((depth, count), jnp.bfloat16),
        ),
        in_specs=in_vmem(3) + [pl.BlockSpec(memory_space=pl.ANY)],
        out_specs=tuple(in_vmem(2)),
        compiler_params=pltpu.CompilerParams(vmem_limit_bytes=32 * 1024 * 1024),
        cost_estimate=SHORT,
        name="factor",
    )(pivots_t, points_t, inverse, awaited)


def band_kernel(pieces, first, last, *refs):
    own_ref = refs[0]
    depth, count = own_ref.shape
    rest = list(refs[1 + max(place for piece in pieces for place, _ in piece):])
    before_ref = None if first else rest.pop(0)
    own = jnp.transpose(padded(extended(own_ref[...], True))).astype(jnp.bfloat16)
    blocks = []
    for (point_at, point_row), (probe_at, probe_row) in pieces:
        points = refs[point_at][point_row:point_row + depth, :]
        blocks.append((padded(extended(points, False)).astype(jnp.bfloat16), refs[probe_at], probe_row))
    for s in range(0, count, CHUNK):
        total = None if first else before_ref[s:s + CHUNK, :]
        for other, probe_ref, probe_row in blocks:
            term = tile_terms(own[s:s + CHUNK, :], other, probe_ref[probe_row:, :])
            total = term if total is None else total + term
        if last:
            probe_ref, out_ref = rest
            scale = 1.0 / (count ** 0.5)
            out_ref[:, s:s + CHUNK] = jnp.transpose(total) * scale + noise_weight * probe_ref[:, s:s + CHUNK]
        else:
            rest[0][s:s + CHUNK, :] = total
    if not last:
        rest[1][...] = jnp.zeros_like(rest[1])


def band_sum(own, pieces, before=None, probes=None):
    depth, count = own.shape
    first, last = before is None, probes is not None
    operands = [own]
    places = []
    for piece in pieces:
        place = []
        for array, start in piece:
            known = [i for i, operand in enumerate(operands) if operand is array]
            if not known:
                operands.append(array)
            place.append((known[0] if known else len(operands) - 1, start))
        places.append(tuple(place))
    array, start = pieces[0][1]
    width = array.shape[0] - start
    operands += ([] if first else [before]) + ([probes] if last else [])
    if last:
        out_shape = jax.ShapeDtypeStruct((width, count), jnp.float32)
    else:
        out_shape = (pltpu.VMEM((count, width), jnp.float32), pltpu.VMEM((width, count), jnp.bfloat16))
    return pl.pallas_call(
        functools.partial(band_kernel, tuple(places), first, last),
        out_shape=out_shape,
        in_specs=in_vmem(len(operands)),
        out_specs=in_vmem(1)[0] if last else tuple(in_vmem(2)),
        compiler_params=pltpu.CompilerParams(vmem_limit_bytes=32 * 1024 * 1024),
        cost_estimate=SHORT,
        name="band_sum",
    )(*operands)


def shards(points, pivots, owners, coeffs, noise):
    tall = lax.axis_size("gy") == BAND + 1
    points = points.T
    depth = points.shape[0]
    row_sum = spread(pick(owners, pivots, points), "gx")
    if tall:
        far = swapped(points, "gy", 2)
        row_sum = row_sum + zero_like(far[:, :row_sum.shape[1]])
        pair = swapped(jnp.concatenate([points, far], axis=0), "gy", 1)
    else:
        near = direct_blocks(points)
    pivot_points = spread(row_sum, "gy")

    inverse, probes, sent = probes_of(pivot_points, points, coeffs.T, noise.T)
    total, zeros = band_sum(points, [((points, 0), (sent, 0))])
    if tall:
        leaving = sent + zero_like(pair[:depth])
        two = swapped(leaving, "gy", 2)
        one = swapped(leaving, "gy", 1) + zeros
        factor, zeros = factor_of(pivot_points, points, inverse, one)
        two = two + zeros
        cross_one = cross(jnp.concatenate([pair[:depth], one], axis=0), 1)
        three = swapped(two, "gy", 1)
        cross_two = cross(jnp.concatenate([far, two], axis=0), 2)
        total, zeros = band_sum(points, [((pair, 0), (one, 0)), ((far, 0), (two, 0))], total)
        cross_three = cross(jnp.concatenate([pair[depth:], three + zeros], axis=0), 3)
        crossed = [((stacked, 0), (stacked, depth)) for stacked in (cross_one, cross_two, cross_three)]
        total, _ = band_sum(points, crossed[:2] + [((pair, depth), (three, 0))], total)
        kernel_probes = band_sum(points, crossed[2:], total, probes)
    else:
        factor, _ = factor_of(pivot_points, points, inverse, zeros)
        pieces = [((block, 0), (probe, 0)) for block, probe in zip(near, direct_blocks(sent))]
        total, _ = band_sum(points, pieces[:3], total)
        kernel_probes = band_sum(points, pieces[3:], total, probes)
    return (kernel_probes.T, factor)


def solution(mesh):
    in_specs = (P(("gx", "gy"), None), P(), P(), P(), P(("gx", "gy"), None))
    out_specs = (P(("gx", "gy"), None), P(("gx", "gy"), None))
    return jax.shard_map(shards, mesh=mesh, in_specs=in_specs, out_specs=out_specs, check_vma=False)
```

```python
import functools
import math

import jax
import jax.numpy as jnp
from jax import lax
from jax.experimental import pallas as pl
from jax.experimental.pallas import tpu as pltpu
from jax.sharding import PartitionSpec as P

PIVOTS = 128
KERNEL_SCALE = 32
BAND = 3
STRIP = 8
LANES = 128
EXTRA = 16
CHUNK = 256
LONG = pl.CostEstimate(flops=1 << 34, bytes_accessed=1, transcendentals=0)


jitter = 0.1
noise_weight = 0.5


def shifted(value, axis, steps):
    count = lax.axis_size(axis)
    return lax.ppermute(value, axis, [((i + steps) % count, i) for i in range(count)])


def swapped(value, axis, bit):
    return lax.ppermute(value, axis, [(i ^ bit, i) for i in range(lax.axis_size(axis))])


def spread(value, axis):
    count = lax.axis_size(axis)
    bit = 1
    while bit < count:
        wide = 2 if (count // bit).bit_length() % 2 == 0 else 4
        value = sum((swapped(value, axis, bit * k) for k in range(1, wide)), value)
        bit *= wide
    return value


def zero_like(value):
    return jnp.minimum(jnp.abs(value), 0)


def cross(piece, bits):
    outer, inner = lax.axis_size("gx"), lax.axis_size("gy")
    pairs = []
    for x in range(outer):
        for z in range(inner):
            source = (x - 1 if z ^ bits > z else x + 1) % outer
            pairs.append((source * inner + z, x * inner + z))
    return lax.ppermute(piece, ("gx", "gy"), pairs)


def direct_blocks(value):
    return [shifted(value, ("gx", "gy"), k) for k in range(-BAND, BAND + 1) if k != 0]


def in_vmem(count):
    return [pl.BlockSpec(memory_space=pltpu.VMEM)] * count


def thirds(value):
    high = value.astype(jnp.bfloat16)
    rest = value - high.astype(jnp.float32)
    middle = rest.astype(jnp.bfloat16)
    return high, middle, (rest - middle.astype(jnp.float32)).astype(jnp.bfloat16)


def product(left, right, contract, precision=None):
    return lax.dot_general(
        left, right, (contract, ((), ())), precision=precision, preferred_element_type=jnp.float32
    )


def extended(columns, ones_first):
    wide = columns.astype(jnp.float32)
    half = -0.5 * jnp.sum(wide * wide, axis=0, keepdims=True)
    terms = [term.astype(jnp.float32) for term in thirds(half)]
    shape = (EXTRA, columns.shape[1])
    level = lax.broadcasted_iota(jnp.int32, shape, 0)
    first = 0 if ones_first else 3
    below = jnp.where((level >= first) & (level < first + 3), 1.0, 0.0)
    for i, term in enumerate(terms):
        below = jnp.where(level == 3 - first + i, jnp.broadcast_to(term, shape), below)
    return jnp.concatenate([wide, below], axis=0)


def kernel_of(product_of_extended):
    return jnp.exp2(product_of_extended * (2.0 / KERNEL_SCALE * math.log2(math.e)))


def pick_kernel(owner_ref, pivot_ref, point_ref, out_ref):
    count = point_ref.shape[1]
    me = lax.axis_index(("gx", "gy"))
    wanted = [jnp.where(owner_ref[r] == me, pivot_ref[r:r + 1, :], -1) for r in range(2)]
    wanted = jnp.concatenate(wanted, axis=1)
    place = lax.broadcasted_iota(jnp.int32, (count, wanted.shape[1]), 0)
    chosen = jnp.where(place == wanted, 1.0, 0.0).astype(jnp.bfloat16)
    out_ref[...] = product(point_ref[...], chosen, ((1,), (0,))).astype(jnp.bfloat16)


def pick(owners, pivots, points_t):
    return pl.pallas_call(
        pick_kernel,
        out_shape=pltpu.VMEM((points_t.shape[0], 2 * PIVOTS), jnp.bfloat16),
        in_specs=[pl.BlockSpec(memory_space=pltpu.SMEM)] + in_vmem(2),
        out_specs=in_vmem(1)[0],
        name="pick",
    )(owners, pivots, points_t)


def column(strip, lane):
    return jnp.broadcast_to(strip[:, lane:lane + 1], strip.shape)


def row(strip, i):
    return jnp.broadcast_to(strip[i:i + 1, :], strip.shape)


def total_of(terms):
    while len(terms) > 1:
        terms = [terms[i] + terms[i + 1] if i + 1 < len(terms) else terms[i] for i in range(0, len(terms), 2)]
    return terms[0]


def four_pivots(a):
    rows = len(a)
    x = [[None] * (i + 1) for i in range(4)]
    scale = [None] * 4
    product_so_far = None
    for k in range(4):
        pivot = a[k][k]
        x[k][k] = product_so_far
        product_so_far = pivot if k == 0 else product_so_far * pivot
        scale[k] = lax.rsqrt(product_so_far)
        for i in range(k + 1, rows):
            for j in range(k + 1, min(i, 3) + 1):
                a[i][j] = pivot * a[i][j] - a[i][k] * a[j][k]
        for i in range(k + 1, 4):
            for j in range(k):
                x[i][j] = pivot * x[i][j] - a[i][k] * x[k][j]
            x[i][k] = -a[i][k] if k == 0 else -a[i][k] * x[k][k]
        yield
    factor = [[a[i][k] * scale[k] for k in range(4)] for i in range(4, rows)]
    return factor, x, scale


def combined(entries, columns):
    return total_of([column if entry is None else entry * column for entry, column in zip(entries, columns)])


def small_inverse(columns, fetch):
    a = [[row(columns[k], i) for k in range(i + 1)] for i in range(STRIP)]
    yield
    below, x, scale = yield from four_pivots([list(entries) for entries in a])
    one = [[scale[i] if entry is None else entry * scale[i] for entry in x[i]] for i in range(4)]
    rest = [
        [a[4 + i][4 + j] - total_of([below[i][k] * below[j][k] for k in range(4)]) for j in range(i + 1)]
        for i in range(4)
    ]
    back = [[total_of([below[i][k] * one[k][j] for k in range(j, 4)]) for j in range(4)] for i in range(4)]
    coming = fetch()
    if coming is not None:
        lower, diagonal = coming
        found = [combined(one[k], lower[:k + 1]) for k in range(4)]
        diagonal = [
            diagonal[j] - total_of([found[k] * row(found[k], j) for k in range(4)]) for j in range(STRIP)
        ]
        lower = [lower[4 + m] - total_of([found[j] * below[m][j] for j in range(4)]) for m in range(4)]
    _, x, scale = yield from four_pivots(rest)
    if coming is not None:
        plain = [combined(x[k], lower[:k + 1]) for k in range(4)]
        squares = [scale[k] * scale[k] for k in range(4)]
        diagonal = [
            diagonal[j] - total_of([plain[k] * row(plain[k], j) * squares[k] for k in range(4)])
            for j in range(STRIP)
        ]
        coming = found + [plain[k] * scale[k] for k in range(4)], diagonal
    two = [[scale[i] if entry is None else entry * scale[i] for entry in x[i]] for i in range(4)]
    corner = [[-total_of([two[i][m] * back[m][j] for m in range(i + 1)]) for j in range(4)] for i in range(4)]
    return one + [corner[i] + two[i] for i in range(4)], coming


def inverse_factor(strips, beside):
    lane = lax.broadcasted_iota(jnp.int32, (STRIP, LANES), 1)
    level = lax.broadcasted_iota(jnp.int32, (STRIP, LANES), 0)
    strips = list(strips)
    result = [None] * len(strips)
    waiting = []

    def factor_columns(r, start, t):
        columns = [column(strips[r], start + j) for j in range(STRIP)]
        return [total_of([columns[j] * t[k][j] for j in range(k + 1)]) for k in range(STRIP)]

    def finish(p, t, found):
        start = p * STRIP
        own = (lane >= start) & (lane < start + STRIP)
        rows = []

        def scaled():
            entered = jnp.where(own, jnp.where(lane - start == level, 1.0, 0.0), strips[p])
            terms = []
            for k in range(STRIP):
                t_column = t[STRIP - 1][k]
                for i in range(STRIP - 2, k - 1, -1):
                    t_column = jnp.where(level == i, t[i][k], t_column)
                if k:
                    t_column = jnp.where(level < k, 0.0, t_column)
                terms.append(t_column * row(entered, k))
            done = total_of(terms)
            result[p] = jnp.where(lane < start + STRIP, done, 0.0)
            rows.extend(row(done, k) for k in range(STRIP))

        def updated(r):
            l_columns = found if r == p + 1 else factor_columns(r, start, t)
            update = total_of([l_columns[k] * rows[k] for k in range(STRIP)])
            strips[r] = jnp.where(own, 0.0, strips[r]) - update

        return [scaled] + [functools.partial(updated, r) for r in range(p + 1, len(strips))]

    def coming_to(p):
        if p + 1 == len(strips):
            return None
        start = p * STRIP
        return tuple([column(strips[p + 1], first + j) for j in range(STRIP)] for first in (start, start + STRIP))

    columns = [column(strips[0], k) for k in range(STRIP)]
    for p in range(len(strips)):
        if beside:
            waiting.append(beside.pop(0))
        steps = small_inverse(columns, functools.partial(coming_to, p))
        while True:
            try:
                next(steps)
            except StopIteration as ended:
                t, coming = ended.value
                break
            for _ in range(2):
                if waiting:
                    waiting.pop(0)()
        while waiting:
            waiting.pop(0)()
        found = None
        if coming is not None:
            found, columns = coming
        waiting = finish(p, t, found)
    while waiting:
        waiting.pop(0)()
    return result


def probe_kernel(
    pivot_ref, point_ref, coeff_ref, noise_ref, inverse_ref, probe_ref, sent_ref, high_ref, middle_ref, little_ref
):
    hp = lax.Precision.HIGHEST
    size = pivot_ref.shape[1]
    half = size // 2
    pivots = jnp.transpose(padded(extended(pivot_ref[...], True))).astype(jnp.bfloat16)
    others = padded(extended(pivot_ref[...], False)).astype(jnp.bfloat16)
    points = padded(extended(point_ref[...], False)).astype(jnp.bfloat16)

    def columns_at(start):
        at = slice(start, start + LANES)
        cols = kernel_of(product(pivots, points[:, at], ((1,), (0,))))
        high_ref[:, at], middle_ref[:, at], little_ref[:, at] = thirds(cols)

    gram = kernel_of(product(pivots, others, ((1,), (0,))))
    equal = lax.broadcasted_iota(jnp.int32, gram.shape, 0) == lax.broadcasted_iota(jnp.int32, gram.shape, 1)
    gram = gram + jnp.where(equal, jitter, 0.0)

    def inverted(block, beside):
        strips = [block[s:s + STRIP, :] for s in range(0, half, STRIP)]
        return jnp.concatenate(inverse_factor(strips, beside), axis=0)

    beside = [functools.partial(columns_at, start) for start in range(0, points.shape[1], LANES)]
    one = inverted(gram[:half, :half], beside)
    below = product(gram[half:, :half], one, ((1,), (1,)), hp)
    back = product(below, one, ((1,), (0,)), hp)
    two = inverted(gram[half:, half:] - product(below, below, ((1,), (1,)), hp), beside)
    coeffs = coeff_ref[...]
    start = product(coeffs[:, :half], one, ((1,), (0,)), hp)
    later = product(coeffs[:, half:], two, ((1,), (0,)), hp)
    weights = jnp.concatenate([start - product(later, back, ((1,), (0,)), hp), later], axis=1)

    rows = weights.shape[0]
    stacked = jnp.concatenate(thirds(weights), axis=0)
    by_high = product(stacked, high_ref[...], ((1,), (0,)))
    by_middle = product(stacked[:2 * rows], middle_ref[...], ((1,), (0,)))
    by_little = product(stacked[:rows], little_ref[...], ((1,), (0,)))
    small = by_high[2 * rows:] + by_middle[rows:] + by_little
    probes = by_high[:rows] + (by_high[rows:2 * rows] + by_middle[:rows] + small) + noise_ref[...]
    probe_ref[...] = probes
    sent_ref[...] = probes.astype(jnp.bfloat16)

    inverse_ref[:half, :half] = one
    inverse_ref[:half, half:] = jnp.zeros((half, half), jnp.float32)
    inverse_ref[half:, :half] = -product(two, back, ((1,), (0,)), hp)
    inverse_ref[half:, half:] = two


def probes_of(pivots_t, points_t, coeffs_t, noise_t):
    size = pivots_t.shape[1]
    count = points_t.shape[1]
    return pl.pallas_call(
        probe_kernel,
        out_shape=(
            pltpu.VMEM((size, size), jnp.float32),
            pltpu.VMEM(noise_t.shape, jnp.float32),
            pltpu.VMEM(noise_t.shape, jnp.bfloat16),
        ),
        in_specs=in_vmem(4),
        out_specs=tuple(in_vmem(3)),
        scratch_shapes=[pltpu.VMEM((size, count), jnp.bfloat16)] * 3,
        cost_estimate=LONG,
        compiler_params=pltpu.CompilerParams(vmem_limit_bytes=32 * 1024 * 1024),
        name="probes",
    )(pivots_t, points_t, coeffs_t, noise_t)


def padded(value):
    return jnp.concatenate([value, jnp.zeros((LANES - value.shape[0], value.shape[1]), value.dtype)], axis=0)


def tile_terms(own, other, probes):
    return product(kernel_of(product(own, other, ((1,), (0,)))).astype(jnp.bfloat16), probes, ((1,), (1,)))


def factor_kernel(pivot_ref, point_ref, inverse_ref, awaited_ref, factor_ref, zero_ref):
    count = point_ref.shape[1]
    own = jnp.transpose(padded(extended(point_ref[...], True))).astype(jnp.bfloat16)
    pivots = padded(extended(pivot_ref[...], False)).astype(jnp.bfloat16)
    high, middle, _ = thirds(inverse_ref[...])
    for s in range(0, count, CHUNK):
        rows = own[s:s + CHUNK, :]
        cols_high, cols_middle, _ = thirds(kernel_of(product(rows, pivots, ((1,), (0,)))))
        factor_ref[s:s + CHUNK, :] = (
            product(cols_high, middle, ((1,), (1,))) + product(cols_middle, high, ((1,), (1,)))
        ) + product(cols_high, high, ((1,), (1,)))
    zero_ref[...] = jnp.zeros_like(zero_ref)


def factor_of(pivots_t, points_t, inverse, awaited):
    size = pivots_t.shape[1]
    depth, count = points_t.shape
    return pl.pallas_call(
        factor_kernel,
        out_shape=(
            jax.ShapeDtypeStruct((count, size), jnp.float32),
            pltpu.VMEM((depth, count), jnp.bfloat16),
        ),
        in_specs=in_vmem(3) + [pl.BlockSpec(memory_space=pl.ANY)],
        out_specs=tuple(in_vmem(2)),
        compiler_params=pltpu.CompilerParams(vmem_limit_bytes=32 * 1024 * 1024),
        cost_estimate=pl.CostEstimate(
            flops=6 * count * size * size // 8,
            bytes_accessed=6 * count * size // 8,
            transcendentals=count * size // 8,
        ),
        name="factor",
    )(pivots_t, points_t, inverse, awaited)


def band_kernel(pieces, first, last, *refs):
    own_ref = refs[0]
    depth, count = own_ref.shape
    rest = list(refs[1 + max(place for piece in pieces for place, _ in piece):])
    before_ref = None if first else rest.pop(0)
    own = jnp.transpose(padded(extended(own_ref[...], True))).astype(jnp.bfloat16)
    blocks = []
    for (point_at, point_row), (probe_at, probe_row) in pieces:
        points = refs[point_at][point_row:point_row + depth, :]
        blocks.append((padded(extended(points, False)).astype(jnp.bfloat16), refs[probe_at], probe_row))
    for s in range(0, count, CHUNK):
        total = None if first else before_ref[s:s + CHUNK, :]
        for other, probe_ref, probe_row in blocks:
            term = tile_terms(own[s:s + CHUNK, :], other, probe_ref[probe_row:, :])
            total = term if total is None else total + term
        if last:
            probe_ref, out_ref = rest
            scale = 1.0 / (count ** 0.5)
            out_ref[:, s:s + CHUNK] = jnp.transpose(total) * scale + noise_weight * probe_ref[:, s:s + CHUNK]
        else:
            rest[0][s:s + CHUNK, :] = total
    if not last:
        rest[1][...] = jnp.zeros_like(rest[1])


def band_sum(own, pieces, before=None, probes=None):
    depth, count = own.shape
    first, last = before is None, probes is not None
    operands = [own]
    places = []
    for piece in pieces:
        place = []
        for array, start in piece:
            known = [i for i, operand in enumerate(operands) if operand is array]
            if not known:
                operands.append(array)
            place.append((known[0] if known else len(operands) - 1, start))
        places.append(tuple(place))
    array, start = pieces[0][1]
    width = array.shape[0] - start
    operands += ([] if first else [before]) + ([probes] if last else [])
    if last:
        out_shape = jax.ShapeDtypeStruct((width, count), jnp.float32)
    else:
        out_shape = (pltpu.VMEM((count, width), jnp.float32), pltpu.VMEM((width, count), jnp.bfloat16))
    return pl.pallas_call(
        functools.partial(band_kernel, tuple(places), first, last),
        out_shape=out_shape,
        in_specs=in_vmem(len(operands)),
        out_specs=in_vmem(1)[0] if last else tuple(in_vmem(2)),
        compiler_params=pltpu.CompilerParams(vmem_limit_bytes=32 * 1024 * 1024),
        cost_estimate=pl.CostEstimate(
            flops=1 if first else len(pieces) * 4 * count * count * LANES,
            bytes_accessed=1 if first else 4 * count * width * len(operands),
            transcendentals=0 if first else len(pieces) * count * count,
        ),
        name="band_sum",
    )(*operands)


def shards(points, pivots, owners, coeffs, noise):
    tall = lax.axis_size("gy") == BAND + 1
    points = points.T
    depth = points.shape[0]
    row_sum = spread(pick(owners, pivots, points), "gx")
    if tall:
        far = swapped(points, "gy", 2)
        row_sum = row_sum + zero_like(far[:, :row_sum.shape[1]])
        pair = swapped(jnp.concatenate([points, far], axis=0), "gy", 1)
    else:
        near = direct_blocks(points)
    pivot_points = spread(row_sum, "gy")

    inverse, probes, sent = probes_of(pivot_points, points, coeffs.T, noise.T)
    total, zeros = band_sum(points, [((points, 0), (sent, 0))])
    if tall:
        leaving = sent + zero_like(pair[:depth])
        two = swapped(leaving, "gy", 2)
        one = swapped(leaving, "gy", 1) + zeros
        factor, zeros = factor_of(pivot_points, points, inverse, one)
        two = two + zeros
        cross_one = cross(jnp.concatenate([pair[:depth], one], axis=0), 1)
        three = swapped(two, "gy", 1)
        cross_two = cross(jnp.concatenate([far, two], axis=0), 2)
        total, zeros = band_sum(points, [((pair, 0), (one, 0)), ((far, 0), (two, 0))], total)
        cross_three = cross(jnp.concatenate([pair[depth:], three + zeros], axis=0), 3)
        crossed = [((stacked, 0), (stacked, depth)) for stacked in (cross_one, cross_two, cross_three)]
        total, _ = band_sum(points, [((pair, depth), (three, 0)), crossed[0]], total)
        total, _ = band_sum(points, crossed[1:2], total)
        kernel_probes = band_sum(points, crossed[2:], total, probes)
    else:
        factor, _ = factor_of(pivot_points, points, inverse, zeros)
        pieces = [((block, 0), (probe, 0)) for block, probe in zip(near, direct_blocks(sent))]
        total, _ = band_sum(points, pieces[:3], total)
        kernel_probes = band_sum(points, pieces[3:], total, probes)
    return (kernel_probes.T, factor)


def solution(mesh):
    in_specs = (P(("gx", "gy"), None), P(), P(), P(), P(("gx", "gy"), None))
    out_specs = (P(("gx", "gy"), None), P(("gx", "gy"), None))
    return jax.shard_map(shards, mesh=mesh, in_specs=in_specs, out_specs=out_specs, check_vma=False)
```

```python
import functools
import math

import jax
import jax.numpy as jnp
from jax import lax
from jax.experimental import pallas as pl
from jax.experimental.pallas import tpu as pltpu
from jax.sharding import PartitionSpec as P

PIVOTS = 128
KERNEL_SCALE = 32
BAND = 3
STRIP = 8
LANES = 128
EXTRA = 16
CHUNK = 256
LONG = pl.CostEstimate(flops=1 << 34, bytes_accessed=1, transcendentals=0)


jitter = 0.1
noise_weight = 0.5


def shifted(value, axis, steps):
    count = lax.axis_size(axis)
    return lax.ppermute(value, axis, [((i + steps) % count, i) for i in range(count)])


def swapped(value, axis, bit):
    return lax.ppermute(value, axis, [(i ^ bit, i) for i in range(lax.axis_size(axis))])


def spread(value, axis):
    count = lax.axis_size(axis)
    bit = 1
    while bit < count:
        wide = 2 if (count // bit).bit_length() % 2 == 0 else 4
        value = sum((swapped(value, axis, bit * k) for k in range(1, wide)), value)
        bit *= wide
    return value


def zero_like(value):
    return jnp.minimum(jnp.abs(value), 0)


def cross(piece, bits):
    outer, inner = lax.axis_size("gx"), lax.axis_size("gy")
    pairs = []
    for x in range(outer):
        for z in range(inner):
            source = (x - 1 if z ^ bits > z else x + 1) % outer
            pairs.append((source * inner + z, x * inner + z))
    return lax.ppermute(piece, ("gx", "gy"), pairs)


def direct_blocks(value):
    return [shifted(value, ("gx", "gy"), k) for k in range(-BAND, BAND + 1) if k != 0]


def in_vmem(count):
    return [pl.BlockSpec(memory_space=pltpu.VMEM)] * count


def thirds(value):
    high = value.astype(jnp.bfloat16)
    rest = value - high.astype(jnp.float32)
    middle = rest.astype(jnp.bfloat16)
    return high, middle, (rest - middle.astype(jnp.float32)).astype(jnp.bfloat16)


def product(left, right, contract, precision=None):
    return lax.dot_general(
        left, right, (contract, ((), ())), precision=precision, preferred_element_type=jnp.float32
    )


def extended(columns, ones_first):
    wide = columns.astype(jnp.float32)
    half = -0.5 * jnp.sum(wide * wide, axis=0, keepdims=True)
    terms = [term.astype(jnp.float32) for term in thirds(half)]
    shape = (EXTRA, columns.shape[1])
    level = lax.broadcasted_iota(jnp.int32, shape, 0)
    first = 0 if ones_first else 3
    below = jnp.where((level >= first) & (level < first + 3), 1.0, 0.0)
    for i, term in enumerate(terms):
        below = jnp.where(level == 3 - first + i, jnp.broadcast_to(term, shape), below)
    return jnp.concatenate([wide, below], axis=0)


def kernel_of(product_of_extended):
    return jnp.exp2(product_of_extended * (2.0 / KERNEL_SCALE * math.log2(math.e)))


def pick_kernel(owner_ref, pivot_ref, point_ref, out_ref):
    count = point_ref.shape[1]
    me = lax.axis_index(("gx", "gy"))
    wanted = [jnp.where(owner_ref[r] == me, pivot_ref[r:r + 1, :], -1) for r in range(2)]
    wanted = jnp.concatenate(wanted, axis=1)
    place = lax.broadcasted_iota(jnp.int32, (count, wanted.shape[1]), 0)
    chosen = jnp.where(place == wanted, 1.0, 0.0).astype(jnp.bfloat16)
    out_ref[...] = product(point_ref[...], chosen, ((1,), (0,))).astype(jnp.bfloat16)


def pick(owners, pivots, points_t):
    return pl.pallas_call(
        pick_kernel,
        out_shape=pltpu.VMEM((points_t.shape[0], 2 * PIVOTS), jnp.bfloat16),
        in_specs=[pl.BlockSpec(memory_space=pltpu.SMEM)] + in_vmem(2),
        out_specs=in_vmem(1)[0],
        name="pick",
    )(owners, pivots, points_t)


def column(strip, lane):
    return jnp.broadcast_to(strip[:, lane:lane + 1], strip.shape)


def column_of(square, lane):
    return jnp.broadcast_to(square[:, lane:lane + 1], (STRIP, LANES))


def row(strip, i):
    return jnp.broadcast_to(strip[i:i + 1, :], strip.shape)


def total_of(terms):
    while len(terms) > 1:
        terms = [terms[i] + terms[i + 1] if i + 1 < len(terms) else terms[i] for i in range(0, len(terms), 2)]
    return terms[0]


def four_pivots(a):
    rows = len(a)
    x = [[None] * (i + 1) for i in range(4)]
    scale = [None] * 4
    product_so_far = None
    for k in range(4):
        pivot = a[k][k]
        x[k][k] = product_so_far
        product_so_far = pivot if k == 0 else product_so_far * pivot
        scale[k] = lax.rsqrt(product_so_far)
        for i in range(k + 1, rows):
            for j in range(k + 1, min(i, 3) + 1):
                a[i][j] = pivot * a[i][j] - a[i][k] * a[j][k]
        for i in range(k + 1, 4):
            for j in range(k):
                x[i][j] = pivot * x[i][j] - a[i][k] * x[k][j]
            x[i][k] = -a[i][k] if k == 0 else -a[i][k] * x[k][k]
        yield
    factor = [[a[i][k] * scale[k] for k in range(4)] for i in range(4, rows)]
    return factor, x, scale


def combined(entries, columns):
    return total_of([column if entry is None else entry * column for entry, column in zip(entries, columns)])


def block_rows(columns, entered, fetch):
    a = [[row(columns[k], i) for k in range(i + 1)] for i in range(STRIP)]
    yield
    below, x, scale = yield from four_pivots([list(entries) for entries in a])
    one = [[scale[i] if entry is None else entry * scale[i] for entry in x[i]] for i in range(4)]
    rest = [
        [a[4 + i][4 + j] - total_of([below[i][k] * below[j][k] for k in range(4)]) for j in range(i + 1)]
        for i in range(4)
    ]

    def halfway(values):
        upper = [combined(one[k], values[:k + 1]) for k in range(4)]
        return upper, [values[4 + m] - total_of([below[m][j] * upper[j] for j in range(4)]) for m in range(4)]

    sides = [halfway(values) for values in (entered, fetch()) if values is not None]
    _, x, scale = yield from four_pivots(rest)
    two = [[scale[i] if entry is None else entry * scale[i] for entry in x[i]] for i in range(4)]
    solved = [upper + [combined(two[k], lower[:k + 1]) for k in range(4)] for upper, lower in sides]
    return solved[0], solved[1] if len(solved) > 1 else None


def inverse_factor(strips, beside):
    lane = lax.broadcasted_iota(jnp.int32, (STRIP, LANES), 1)
    level = lax.broadcasted_iota(jnp.int32, (STRIP, LANES), 0)
    strips = list(strips)
    result = []
    waiting = []

    def finish(p, own, rows):
        turned = []

        def turn():
            turned.append(jnp.transpose(result[p]))

        def update(r):
            factors = turned[0][r * STRIP:(r + 1) * STRIP, :]
            terms = [column_of(factors, k) * rows[k] for k in range(STRIP)]
            strips[r] = jnp.where(own, 0.0, strips[r]) - total_of(terms)

        return [turn] + [functools.partial(update, r) for r in range(p + 2, len(strips))]

    columns = [column(strips[0], k) for k in range(STRIP)]
    for p in range(len(strips)):
        start = p * STRIP
        own = (lane >= start) & (lane < start + STRIP)
        if beside:
            waiting.append(beside.pop(0))
        entered = jnp.where(own, jnp.where(lane - start == level, 1.0, 0.0), strips[p])

        def fetch():
            if p + 1 == len(strips):
                return None
            return [column(strips[p + 1], start + j) for j in range(STRIP)]

        steps = block_rows(columns, [row(entered, k) for k in range(STRIP)], fetch)
        while True:
            try:
                next(steps)
            except StopIteration as ended:
                rows, found = ended.value
                break
            for _ in range(2):
                if waiting:
                    waiting.pop(0)()
        while waiting:
            waiting.pop(0)()
        done = rows[0]
        for k in range(1, STRIP):
            done = jnp.where(level == k, rows[k], done)
        result.append(done)
        if found is not None:
            update = total_of([found[k] * rows[k] for k in range(STRIP)])
            strips[p + 1] = jnp.where(own, 0.0, strips[p + 1]) - update
            columns = [column(strips[p + 1], start + STRIP + k) for k in range(STRIP)]
            waiting = finish(p, own, rows)
    return [jnp.where(lane < (p + 1) * STRIP, done, 0.0) for p, done in enumerate(result)]


def probe_kernel(
    pivot_ref, point_ref, coeff_ref, noise_ref, inverse_ref, probe_ref, sent_ref, high_ref, middle_ref, little_ref
):
    hp = lax.Precision.HIGHEST
    size = pivot_ref.shape[1]
    half = size // 2
    pivots = jnp.transpose(padded(extended(pivot_ref[...], True))).astype(jnp.bfloat16)
    others = padded(extended(pivot_ref[...], False)).astype(jnp.bfloat16)
    points = padded(extended(point_ref[...], False)).astype(jnp.bfloat16)

    def columns_at(start):
        at = slice(start, start + LANES)
        cols = kernel_of(product(pivots, points[:, at], ((1,), (0,))))
        high_ref[:, at], middle_ref[:, at], little_ref[:, at] = thirds(cols)

    gram = kernel_of(product(pivots, others, ((1,), (0,))))
    equal = lax.broadcasted_iota(jnp.int32, gram.shape, 0) == lax.broadcasted_iota(jnp.int32, gram.shape, 1)
    gram = gram + jnp.where(equal, jitter, 0.0)

    def inverted(block, beside):
        strips = [block[s:s + STRIP, :] for s in range(0, half, STRIP)]
        return jnp.concatenate(inverse_factor(strips, beside), axis=0)

    beside = [functools.partial(columns_at, start) for start in range(0, points.shape[1], LANES)]
    one = inverted(gram[:half, :half], beside)
    below = product(gram[half:, :half], one, ((1,), (1,)), hp)
    back = product(below, one, ((1,), (0,)), hp)
    two = inverted(gram[half:, half:] - product(below, below, ((1,), (1,)), hp), beside)
    coeffs = coeff_ref[...]
    start = product(coeffs[:, :half], one, ((1,), (0,)), hp)
    later = product(coeffs[:, half:], two, ((1,), (0,)), hp)
    weights = jnp.concatenate([start - product(later, back, ((1,), (0,)), hp), later], axis=1)

    rows = weights.shape[0]
    stacked = jnp.concatenate(thirds(weights), axis=0)
    by_high = product(stacked, high_ref[...], ((1,), (0,)))
    by_middle = product(stacked[:2 * rows], middle_ref[...], ((1,), (0,)))
    by_little = product(stacked[:rows], little_ref[...], ((1,), (0,)))
    small = by_high[2 * rows:] + by_middle[rows:] + by_little
    probes = by_high[:rows] + (by_high[rows:2 * rows] + by_middle[:rows] + small) + noise_ref[...]
    probe_ref[...] = probes
    sent_ref[...] = probes.astype(jnp.bfloat16)

    inverse_ref[:half, :half] = one
    inverse_ref[:half, half:] = jnp.zeros((half, half), jnp.float32)
    inverse_ref[half:, :half] = -product(two, back, ((1,), (0,)), hp)
    inverse_ref[half:, half:] = two


def probes_of(pivots_t, points_t, coeffs_t, noise_t):
    size = pivots_t.shape[1]
    count = points_t.shape[1]
    return pl.pallas_call(
        probe_kernel,
        out_shape=(
            pltpu.VMEM((size, size), jnp.float32),
            pltpu.VMEM(noise_t.shape, jnp.float32),
            pltpu.VMEM(noise_t.shape, jnp.bfloat16),
        ),
        in_specs=in_vmem(4),
        out_specs=tuple(in_vmem(3)),
        scratch_shapes=[pltpu.VMEM((size, count), jnp.bfloat16)] * 3,
        cost_estimate=LONG,
        compiler_params=pltpu.CompilerParams(vmem_limit_bytes=32 * 1024 * 1024),
        name="probes",
    )(pivots_t, points_t, coeffs_t, noise_t)


def padded(value):
    return jnp.concatenate([value, jnp.zeros((LANES - value.shape[0], value.shape[1]), value.dtype)], axis=0)


def tile_terms(own, other, probes):
    return product(kernel_of(product(own, other, ((1,), (0,)))).astype(jnp.bfloat16), probes, ((1,), (1,)))


def factor_kernel(pivot_ref, point_ref, inverse_ref, awaited_ref, factor_ref, zero_ref):
    count = point_ref.shape[1]
    own = jnp.transpose(padded(extended(point_ref[...], True))).astype(jnp.bfloat16)
    pivots = padded(extended(pivot_ref[...], False)).astype(jnp.bfloat16)
    high, middle, _ = thirds(inverse_ref[...])
    for s in range(0, count, CHUNK):
        rows = own[s:s + CHUNK, :]
        cols_high, cols_middle, _ = thirds(kernel_of(product(rows, pivots, ((1,), (0,)))))
        factor_ref[s:s + CHUNK, :] = (
            product(cols_high, middle, ((1,), (1,))) + product(cols_middle, high, ((1,), (1,)))
        ) + product(cols_high, high, ((1,), (1,)))
    zero_ref[...] = jnp.zeros_like(zero_ref)


def factor_of(pivots_t, points_t, inverse, awaited):
    size = pivots_t.shape[1]
    depth, count = points_t.shape
    return pl.pallas_call(
        factor_kernel,
        out_shape=(
            jax.ShapeDtypeStruct((count, size), jnp.float32),
            pltpu.VMEM((depth, count), jnp.bfloat16),
        ),
        in_specs=in_vmem(3) + [pl.BlockSpec(memory_space=pl.ANY)],
        out_specs=tuple(in_vmem(2)),
        compiler_params=pltpu.CompilerParams(vmem_limit_bytes=32 * 1024 * 1024),
        cost_estimate=pl.CostEstimate(
            flops=6 * count * size * size // 8,
            bytes_accessed=6 * count * size // 8,
            transcendentals=count * size // 8,
        ),
        name="factor",
    )(pivots_t, points_t, inverse, awaited)


def band_kernel(pieces, first, last, *refs):
    own_ref = refs[0]
    depth, count = own_ref.shape
    rest = list(refs[1 + max(place for piece in pieces for place, _ in piece):])
    before_ref = None if first else rest.pop(0)
    own = jnp.transpose(padded(extended(own_ref[...], True))).astype(jnp.bfloat16)
    blocks = []
    for (point_at, point_row), (probe_at, probe_row) in pieces:
        points = refs[point_at][point_row:point_row + depth, :]
        blocks.append((padded(extended(points, False)).astype(jnp.bfloat16), refs[probe_at], probe_row))
    for s in range(0, count, CHUNK):
        total = None if first else before_ref[s:s + CHUNK, :]
        for other, probe_ref, probe_row in blocks:
            term = tile_terms(own[s:s + CHUNK, :], other, probe_ref[probe_row:, :])
            total = term if total is None else total + term
        if last:
            probe_ref, out_ref = rest
            scale = 1.0 / (count ** 0.5)
            out_ref[:, s:s + CHUNK] = jnp.transpose(total) * scale + noise_weight * probe_ref[:, s:s + CHUNK]
        else:
            rest[0][s:s + CHUNK, :] = total
    if not last:
        rest[1][...] = jnp.zeros_like(rest[1])


def band_sum(own, pieces, before=None, probes=None):
    depth, count = own.shape
    first, last = before is None, probes is not None
    operands = [own]
    places = []
    for piece in pieces:
        place = []
        for array, start in piece:
            known = [i for i, operand in enumerate(operands) if operand is array]
            if not known:
                operands.append(array)
            place.append((known[0] if known else len(operands) - 1, start))
        places.append(tuple(place))
    array, start = pieces[0][1]
    width = array.shape[0] - start
    operands += ([] if first else [before]) + ([probes] if last else [])
    if last:
        out_shape = jax.ShapeDtypeStruct((width, count), jnp.float32)
    else:
        out_shape = (pltpu.VMEM((count, width), jnp.float32), pltpu.VMEM((width, count), jnp.bfloat16))
    return pl.pallas_call(
        functools.partial(band_kernel, tuple(places), first, last),
        out_shape=out_shape,
        in_specs=in_vmem(len(operands)),
        out_specs=in_vmem(1)[0] if last else tuple(in_vmem(2)),
        compiler_params=pltpu.CompilerParams(vmem_limit_bytes=32 * 1024 * 1024),
        cost_estimate=pl.CostEstimate(
            flops=1 if first else len(pieces) * 4 * count * count * LANES,
            bytes_accessed=1 if first else 4 * count * width * len(operands),
            transcendentals=0 if first else len(pieces) * count * count,
        ),
        name="band_sum",
    )(*operands)


def shards(points, pivots, owners, coeffs, noise):
    tall = lax.axis_size("gy") == BAND + 1
    points = points.T
    depth = points.shape[0]
    row_sum = spread(pick(owners, pivots, points), "gx")
    if tall:
        far = swapped(points, "gy", 2)
        row_sum = row_sum + zero_like(far[:, :row_sum.shape[1]])
        pair = swapped(jnp.concatenate([points, far], axis=0), "gy", 1)
    else:
        near = direct_blocks(points)
    pivot_points = spread(row_sum, "gy")

    inverse, probes, sent = probes_of(pivot_points, points, coeffs.T, noise.T)
    total, zeros = band_sum(points, [((points, 0), (sent, 0))])
    if tall:
        leaving = sent + zero_like(pair[:depth])
        two = swapped(leaving, "gy", 2)
        one = swapped(leaving, "gy", 1) + zeros
        factor, zeros = factor_of(pivot_points, points, inverse, one)
        two = two + zeros
        cross_one = cross(jnp.concatenate([pair[:depth], one], axis=0), 1)
        three = swapped(two, "gy", 1)
        cross_two = cross(jnp.concatenate([far, two], axis=0), 2)
        total, zeros = band_sum(points, [((pair, 0), (one, 0)), ((far, 0), (two, 0))], total)
        cross_three = cross(jnp.concatenate([pair[depth:], three + zeros], axis=0), 3)
        crossed = [((stacked, 0), (stacked, depth)) for stacked in (cross_one, cross_two, cross_three)]
        total, _ = band_sum(points, [((pair, depth), (three, 0)), crossed[0]], total)
        total, _ = band_sum(points, crossed[1:2], total)
        kernel_probes = band_sum(points, crossed[2:], total, probes)
    else:
        factor, _ = factor_of(pivot_points, points, inverse, zeros)
        pieces = [((block, 0), (probe, 0)) for block, probe in zip(near, direct_blocks(sent))]
        total, _ = band_sum(points, pieces[:3], total)
        kernel_probes = band_sum(points, pieces[3:], total, probes)
    return (kernel_probes.T, factor)


def solution(mesh):
    in_specs = (P(("gx", "gy"), None), P(), P(), P(), P(("gx", "gy"), None))
    out_specs = (P(("gx", "gy"), None), P(("gx", "gy"), None))
    return jax.shard_map(shards, mesh=mesh, in_specs=in_specs, out_specs=out_specs, check_vma=False)
```

```python
import functools
import math

import jax
import jax.numpy as jnp
from jax import lax
from jax.experimental import pallas as pl
from jax.experimental.pallas import tpu as pltpu
from jax.sharding import PartitionSpec as P

PIVOTS = 128
KERNEL_SCALE = 32
BAND = 3
STRIP = 8
LANES = 128
EXTRA = 16
CHUNK = 256
LONG = pl.CostEstimate(flops=1 << 34, bytes_accessed=1, transcendentals=0)


jitter = 0.1
noise_weight = 0.5


def shifted(value, axis, steps):
    count = lax.axis_size(axis)
    return lax.ppermute(value, axis, [((i + steps) % count, i) for i in range(count)])


def swapped(value, axis, bit):
    return lax.ppermute(value, axis, [(i ^ bit, i) for i in range(lax.axis_size(axis))])


def spread(value, axis):
    count = lax.axis_size(axis)
    bit = 1
    while bit < count:
        wide = 2 if (count // bit).bit_length() % 2 == 0 else 4
        value = sum((swapped(value, axis, bit * k) for k in range(1, wide)), value)
        bit *= wide
    return value


def zero_like(value):
    return jnp.minimum(jnp.abs(value), 0)


def cross(piece, bits):
    outer, inner = lax.axis_size("gx"), lax.axis_size("gy")
    pairs = []
    for x in range(outer):
        for z in range(inner):
            source = (x - 1 if z ^ bits > z else x + 1) % outer
            pairs.append((source * inner + z, x * inner + z))
    return lax.ppermute(piece, ("gx", "gy"), pairs)


def direct_blocks(value):
    return [shifted(value, ("gx", "gy"), k) for k in range(-BAND, BAND + 1) if k != 0]


def in_vmem(count):
    return [pl.BlockSpec(memory_space=pltpu.VMEM)] * count


def thirds(value):
    high = value.astype(jnp.bfloat16)
    rest = value - high.astype(jnp.float32)
    middle = rest.astype(jnp.bfloat16)
    return high, middle, (rest - middle.astype(jnp.float32)).astype(jnp.bfloat16)


def product(left, right, contract, precision=None):
    return lax.dot_general(
        left, right, (contract, ((), ())), precision=precision, preferred_element_type=jnp.float32
    )


def extended(columns, ones_first):
    wide = columns.astype(jnp.float32)
    half = -0.5 * jnp.sum(wide * wide, axis=0, keepdims=True)
    terms = [term.astype(jnp.float32) for term in thirds(half)]
    shape = (EXTRA, columns.shape[1])
    level = lax.broadcasted_iota(jnp.int32, shape, 0)
    first = 0 if ones_first else 3
    below = jnp.where((level >= first) & (level < first + 3), 1.0, 0.0)
    for i, term in enumerate(terms):
        below = jnp.where(level == 3 - first + i, jnp.broadcast_to(term, shape), below)
    return jnp.concatenate([wide, below], axis=0)


def kernel_of(product_of_extended):
    return jnp.exp2(product_of_extended * (2.0 / KERNEL_SCALE * math.log2(math.e)))


def pick_kernel(owner_ref, pivot_ref, point_ref, out_ref):
    count = point_ref.shape[1]
    me = lax.axis_index(("gx", "gy"))
    wanted = [jnp.where(owner_ref[r] == me, pivot_ref[r:r + 1, :], -1) for r in range(2)]
    wanted = jnp.concatenate(wanted, axis=1)
    place = lax.broadcasted_iota(jnp.int32, (count, wanted.shape[1]), 0)
    chosen = jnp.where(place == wanted, 1.0, 0.0).astype(jnp.bfloat16)
    out_ref[...] = product(point_ref[...], chosen, ((1,), (0,))).astype(jnp.bfloat16)


def pick(owners, pivots, points_t):
    return pl.pallas_call(
        pick_kernel,
        out_shape=pltpu.VMEM((points_t.shape[0], 2 * PIVOTS), jnp.bfloat16),
        in_specs=[pl.BlockSpec(memory_space=pltpu.SMEM)] + in_vmem(2),
        out_specs=in_vmem(1)[0],
        name="pick",
    )(owners, pivots, points_t)


def column(strip, lane):
    return jnp.broadcast_to(strip[:, lane:lane + 1], strip.shape)


def column_of(square, lane):
    return jnp.broadcast_to(square[:, lane:lane + 1], (STRIP, LANES))


def row(strip, i):
    return jnp.broadcast_to(strip[i:i + 1, :], strip.shape)


def total_of(terms):
    while len(terms) > 1:
        terms = [terms[i] + terms[i + 1] if i + 1 < len(terms) else terms[i] for i in range(0, len(terms), 2)]
    return terms[0]


def four_pivots(a):
    rows = len(a)
    x = [[None] * (i + 1) for i in range(4)]
    scale = [None] * 4
    product_so_far = None
    for k in range(4):
        pivot = a[k][k]
        x[k][k] = product_so_far
        product_so_far = pivot if k == 0 else product_so_far * pivot
        scale[k] = lax.rsqrt(product_so_far)
        for i in range(k + 1, rows):
            for j in range(k + 1, min(i, 3) + 1):
                a[i][j] = pivot * a[i][j] - a[i][k] * a[j][k]
        for i in range(k + 1, 4):
            for j in range(k):
                x[i][j] = pivot * x[i][j] - a[i][k] * x[k][j]
            x[i][k] = -a[i][k] if k == 0 else -a[i][k] * x[k][k]
        yield
    factor = [[a[i][k] * scale[k] for k in range(4)] for i in range(4, rows)]
    return factor, x, scale


def combined(entries, columns):
    return total_of([column if entry is None else entry * column for entry, column in zip(entries, columns)])


def block_rows(columns, entered, fetch):
    a = [[row(columns[k], i) for k in range(i + 1)] for i in range(STRIP)]
    yield
    below, x, scale = yield from four_pivots([list(entries) for entries in a])
    one = [[scale[i] if entry is None else entry * scale[i] for entry in x[i]] for i in range(4)]
    rest = [
        [a[4 + i][4 + j] - total_of([below[i][k] * below[j][k] for k in range(4)]) for j in range(i + 1)]
        for i in range(4)
    ]

    def halfway(values):
        upper = [combined(one[k], values[:k + 1]) for k in range(4)]
        return upper, [values[4 + m] - total_of([below[m][j] * upper[j] for j in range(4)]) for m in range(4)]

    def updated(diagonal, factors):
        return [diagonal[j] - total_of([f * row(f, j) for f in factors]) for j in range(STRIP)]

    upper, lower = halfway(entered)
    coming = fetch()
    if coming is not None:
        found, left = halfway(coming[0])
        diagonal = updated(coming[1], found)
    _, x, scale = yield from four_pivots(rest)
    two = [[scale[i] if entry is None else entry * scale[i] for entry in x[i]] for i in range(4)]

    def rear(values):
        return [combined(two[k], values[:k + 1]) for k in range(4)]

    if coming is not None:
        more = rear(left)
        coming = found + more, updated(diagonal, more)

    def solve(values):
        front, values = halfway(values)
        return front + rear(values)

    return solve, upper + rear(lower), coming


def inverse_factor(strips, beside):
    lane = lax.broadcasted_iota(jnp.int32, (STRIP, LANES), 1)
    level = lax.broadcasted_iota(jnp.int32, (STRIP, LANES), 0)
    strips = list(strips)
    result = []
    waiting = []

    def finish(p, own, solve, rows):
        turned = []

        def subtract(r, factors):
            terms = [factors[k] * rows[k] for k in range(STRIP)]
            strips[r] = jnp.where(own, 0.0, strips[r]) - total_of(terms)

        def second(r):
            subtract(r, solve([column(strips[r], p * STRIP + j) for j in range(STRIP)]))

        def turn():
            turned.append(jnp.transpose(result[p]))

        def later(r):
            square = turned[0][r * STRIP:(r + 1) * STRIP, :]
            subtract(r, [column_of(square, k) for k in range(STRIP)])

        count = len(strips)
        steps = [functools.partial(second, p + 2)] if p + 2 < count else []
        if p + 3 < count:
            steps += [turn] + [functools.partial(later, r) for r in range(p + 3, count)]
        return steps

    columns = [column(strips[0], k) for k in range(STRIP)]
    for p in range(len(strips)):
        start = p * STRIP
        own = (lane >= start) & (lane < start + STRIP)
        if beside:
            waiting.append(beside.pop(0))
        entered = jnp.where(own, jnp.where(lane - start == level, 1.0, 0.0), strips[p])

        def fetch():
            if p + 1 == len(strips):
                return None
            return [[column(strips[p + 1], at + j) for j in range(STRIP)] for at in (start, start + STRIP)]

        steps = block_rows(columns, [row(entered, k) for k in range(STRIP)], fetch)
        while True:
            try:
                next(steps)
            except StopIteration as ended:
                solve, rows, coming = ended.value
                break
            for _ in range(2):
                if waiting:
                    waiting.pop(0)()
        while waiting:
            waiting.pop(0)()
        done = rows[0]
        for k in range(1, STRIP):
            done = jnp.where(level == k, rows[k], done)
        result.append(done)
        if coming is not None:
            found, columns = coming
            update = total_of([found[k] * rows[k] for k in range(STRIP)])
            strips[p + 1] = jnp.where(own, 0.0, strips[p + 1]) - update
            waiting = finish(p, own, solve, rows)
    return [jnp.where(lane < (p + 1) * STRIP, done, 0.0) for p, done in enumerate(result)]


def probe_kernel(
    pivot_ref, point_ref, coeff_ref, noise_ref, inverse_ref, probe_ref, sent_ref, high_ref, middle_ref, little_ref
):
    hp = lax.Precision.HIGHEST
    size = pivot_ref.shape[1]
    half = size // 2
    pivots = jnp.transpose(padded(extended(pivot_ref[...], True))).astype(jnp.bfloat16)
    others = padded(extended(pivot_ref[...], False)).astype(jnp.bfloat16)
    points = padded(extended(point_ref[...], False)).astype(jnp.bfloat16)

    def columns_at(start):
        at = slice(start, start + LANES)
        cols = kernel_of(product(pivots, points[:, at], ((1,), (0,))))
        high_ref[:, at], middle_ref[:, at], little_ref[:, at] = thirds(cols)

    gram = kernel_of(product(pivots, others, ((1,), (0,))))
    equal = lax.broadcasted_iota(jnp.int32, gram.shape, 0) == lax.broadcasted_iota(jnp.int32, gram.shape, 1)
    gram = gram + jnp.where(equal, jitter, 0.0)

    def inverted(block, beside):
        strips = [block[s:s + STRIP, :] for s in range(0, half, STRIP)]
        return jnp.concatenate(inverse_factor(strips, beside), axis=0)

    beside = [functools.partial(columns_at, start) for start in range(0, points.shape[1], LANES)]
    one = inverted(gram[:half, :half], beside)
    below = product(gram[half:, :half], one, ((1,), (1,)), hp)
    back = product(below, one, ((1,), (0,)), hp)
    two = inverted(gram[half:, half:] - product(below, below, ((1,), (1,)), hp), beside)
    coeffs = coeff_ref[...]
    start = product(coeffs[:, :half], one, ((1,), (0,)), hp)
    later = product(coeffs[:, half:], two, ((1,), (0,)), hp)
    weights = jnp.concatenate([start - product(later, back, ((1,), (0,)), hp), later], axis=1)

    rows = weights.shape[0]
    stacked = jnp.concatenate(thirds(weights), axis=0)
    by_high = product(stacked, high_ref[...], ((1,), (0,)))
    by_middle = product(stacked[:2 * rows], middle_ref[...], ((1,), (0,)))
    by_little = product(stacked[:rows], little_ref[...], ((1,), (0,)))
    small = by_high[2 * rows:] + by_middle[rows:] + by_little
    probes = by_high[:rows] + (by_high[rows:2 * rows] + by_middle[:rows] + small) + noise_ref[...]
    probe_ref[...] = probes
    sent_ref[...] = probes.astype(jnp.bfloat16)

    inverse_ref[:half, :half] = one
    inverse_ref[:half, half:] = jnp.zeros((half, half), jnp.float32)
    inverse_ref[half:, :half] = -product(two, back, ((1,), (0,)), hp)
    inverse_ref[half:, half:] = two


def probes_of(pivots_t, points_t, coeffs_t, noise_t):
    size = pivots_t.shape[1]
    count = points_t.shape[1]
    return pl.pallas_call(
        probe_kernel,
        out_shape=(
            pltpu.VMEM((size, size), jnp.float32),
            pltpu.VMEM(noise_t.shape, jnp.float32),
            pltpu.VMEM(noise_t.shape, jnp.bfloat16),
        ),
        in_specs=in_vmem(4),
        out_specs=tuple(in_vmem(3)),
        scratch_shapes=[pltpu.VMEM((size, count), jnp.bfloat16)] * 3,
        cost_estimate=LONG,
        compiler_params=pltpu.CompilerParams(vmem_limit_bytes=32 * 1024 * 1024),
        name="probes",
    )(pivots_t, points_t, coeffs_t, noise_t)


def padded(value):
    return jnp.concatenate([value, jnp.zeros((LANES - value.shape[0], value.shape[1]), value.dtype)], axis=0)


def tile_terms(own, other, probes):
    return product(kernel_of(product(own, other, ((1,), (0,)))).astype(jnp.bfloat16), probes, ((1,), (1,)))


def factor_kernel(pivot_ref, point_ref, inverse_ref, *refs):
    factor_ref, zero_ref = refs[-2:]
    count = point_ref.shape[1]
    own = jnp.transpose(padded(extended(point_ref[...], True))).astype(jnp.bfloat16)
    pivots = padded(extended(pivot_ref[...], False)).astype(jnp.bfloat16)
    high, middle, _ = thirds(inverse_ref[...])
    for s in range(0, count, CHUNK):
        rows = own[s:s + CHUNK, :]
        cols_high, cols_middle, _ = thirds(kernel_of(product(rows, pivots, ((1,), (0,)))))
        factor_ref[s:s + CHUNK, :] = (
            product(cols_high, middle, ((1,), (1,))) + product(cols_middle, high, ((1,), (1,)))
        ) + product(cols_high, high, ((1,), (1,)))
    zero_ref[...] = jnp.zeros_like(zero_ref)


def factor_of(pivots_t, points_t, inverse, awaited):
    size = pivots_t.shape[1]
    depth, count = points_t.shape
    return pl.pallas_call(
        factor_kernel,
        out_shape=(
            jax.ShapeDtypeStruct((count, size), jnp.float32),
            pltpu.VMEM((depth, count), jnp.bfloat16),
        ),
        in_specs=in_vmem(3) + [pl.BlockSpec(memory_space=pl.ANY)] * len(awaited),
        out_specs=tuple(in_vmem(2)),
        compiler_params=pltpu.CompilerParams(vmem_limit_bytes=32 * 1024 * 1024),
        cost_estimate=pl.CostEstimate(
            flops=6 * count * size * size // 8,
            bytes_accessed=6 * count * size // 8,
            transcendentals=count * size // 8,
        ),
        name="factor",
    )(pivots_t, points_t, inverse, *awaited)


def tile_kernel(own_ref, other_ref, awaited_ref, tile_ref):
    count = own_ref.shape[1]
    own = jnp.transpose(padded(extended(own_ref[...], True))).astype(jnp.bfloat16)
    other = padded(extended(other_ref[...], False)).astype(jnp.bfloat16)
    for s in range(0, count, CHUNK):
        tile_ref[s:s + CHUNK, :] = kernel_of(product(own[s:s + CHUNK, :], other, ((1,), (0,)))).astype(jnp.bfloat16)


def tile_of(own, other, awaited):
    count = own.shape[1]
    return pl.pallas_call(
        tile_kernel,
        out_shape=pltpu.VMEM((count, count), jnp.bfloat16),
        in_specs=in_vmem(2) + [pl.BlockSpec(memory_space=pl.ANY)],
        out_specs=in_vmem(1)[0],
        compiler_params=pltpu.CompilerParams(vmem_limit_bytes=32 * 1024 * 1024),
        cost_estimate=pl.CostEstimate(
            flops=2 * count * count * LANES, bytes_accessed=2 * count * count, transcendentals=count * count
        ),
        name="tile",
    )(own, other, awaited)


def last_kernel(tile_ref, block_probe_ref, before_ref, probe_ref, out_ref):
    count = tile_ref.shape[0]
    scale = 1.0 / (count ** 0.5)
    for s in range(0, count, CHUNK):
        total = before_ref[s:s + CHUNK, :] + product(tile_ref[s:s + CHUNK, :], block_probe_ref[...], ((1,), (1,)))
        out_ref[:, s:s + CHUNK] = jnp.transpose(total) * scale + noise_weight * probe_ref[:, s:s + CHUNK]


def last_sum(tile, block_probes, before, probes):
    return pl.pallas_call(
        last_kernel,
        out_shape=jax.ShapeDtypeStruct(probes.shape, jnp.float32),
        in_specs=in_vmem(4),
        out_specs=in_vmem(1)[0],
        compiler_params=pltpu.CompilerParams(vmem_limit_bytes=32 * 1024 * 1024),
        name="last_sum",
    )(tile, block_probes, before, probes)


def band_kernel(pieces, first, last, *refs):
    own_ref = refs[0]
    depth, count = own_ref.shape
    rest = list(refs[1 + max(place for piece in pieces for place, _ in piece):])
    before_ref = None if first else rest.pop(0)
    own = jnp.transpose(padded(extended(own_ref[...], True))).astype(jnp.bfloat16)
    blocks = []
    for (point_at, point_row), (probe_at, probe_row) in pieces:
        points = refs[point_at][point_row:point_row + depth, :]
        blocks.append((padded(extended(points, False)).astype(jnp.bfloat16), refs[probe_at], probe_row))
    for s in range(0, count, CHUNK):
        total = None if first else before_ref[s:s + CHUNK, :]
        for other, probe_ref, probe_row in blocks:
            term = tile_terms(own[s:s + CHUNK, :], other, probe_ref[probe_row:, :])
            total = term if total is None else total + term
        if last:
            probe_ref, out_ref = rest
            scale = 1.0 / (count ** 0.5)
            out_ref[:, s:s + CHUNK] = jnp.transpose(total) * scale + noise_weight * probe_ref[:, s:s + CHUNK]
        else:
            rest[0][s:s + CHUNK, :] = total
    if not last:
        rest[1][...] = jnp.zeros_like(rest[1])


def band_sum(own, pieces, before=None, probes=None):
    depth, count = own.shape
    first, last = before is None, probes is not None
    operands = [own]
    places = []
    for piece in pieces:
        place = []
        for array, start in piece:
            known = [i for i, operand in enumerate(operands) if operand is array]
            if not known:
                operands.append(array)
            place.append((known[0] if known else len(operands) - 1, start))
        places.append(tuple(place))
    array, start = pieces[0][1]
    width = array.shape[0] - start
    operands += ([] if first else [before]) + ([probes] if last else [])
    if last:
        out_shape = jax.ShapeDtypeStruct((width, count), jnp.float32)
    else:
        out_shape = (pltpu.VMEM((count, width), jnp.float32), pltpu.VMEM((width, count), jnp.bfloat16))
    return pl.pallas_call(
        functools.partial(band_kernel, tuple(places), first, last),
        out_shape=out_shape,
        in_specs=in_vmem(len(operands)),
        out_specs=in_vmem(1)[0] if last else tuple(in_vmem(2)),
        compiler_params=pltpu.CompilerParams(vmem_limit_bytes=32 * 1024 * 1024),
        cost_estimate=pl.CostEstimate(
            flops=1 if first else len(pieces) * 4 * count * count * LANES,
            bytes_accessed=1 if first else 4 * count * width * len(operands),
            transcendentals=0 if first else len(pieces) * count * count,
        ),
        name="band_sum",
    )(*operands)


def shards(points, pivots, owners, coeffs, noise):
    tall = lax.axis_size("gy") == BAND + 1
    points = points.T
    depth = points.shape[0]
    row_sum = spread(pick(owners, pivots, points), "gx")
    if tall:
        far = swapped(points, "gy", 2)
        row_sum = row_sum + zero_like(far[:, :row_sum.shape[1]])
        pair = swapped(jnp.concatenate([points, far], axis=0), "gy", 1)
    else:
        near = direct_blocks(points)
    pivot_points = spread(row_sum, "gy")

    inverse, probes, sent = probes_of(pivot_points, points, coeffs.T, noise.T)
    total, zeros = band_sum(points, [((points, 0), (sent, 0))])
    if tall:
        leaving = sent + zero_like(pair[:depth])
        two = swapped(leaving, "gy", 2)
        one = swapped(leaving, "gy", 1) + zeros
        last_points = cross(pair[depth:] + zeros, 3)
        factor, zeros = factor_of(pivot_points, points, inverse, [one, last_points])
        two = two + zeros
        three = swapped(two, "gy", 1)
        cross_two = cross(jnp.concatenate([far, two], axis=0), 2)
        cross_one = cross(jnp.concatenate([pair[:depth], one], axis=0), 1)
        total, zeros = band_sum(points, [((pair, 0), (one, 0)), ((far, 0), (two, 0))], total)
        three = three + zeros
        cross_three = cross(three, 3)
        total, _ = band_sum(points, [((pair, depth), (three, 0)), ((cross_one, 0), (cross_one, depth))], total)
        total, _ = band_sum(points, [((cross_two, 0), (cross_two, depth))], total)
        kernel_probes = last_sum(tile_of(points, last_points, total), cross_three, total, probes)
    else:
        factor, _ = factor_of(pivot_points, points, inverse, [zeros])
        pieces = [((block, 0), (probe, 0)) for block, probe in zip(near, direct_blocks(sent))]
        total, _ = band_sum(points, pieces[:3], total)
        kernel_probes = band_sum(points, pieces[3:], total, probes)
    return (kernel_probes.T, factor)


def solution(mesh):
    in_specs = (P(("gx", "gy"), None), P(), P(), P(), P(("gx", "gy"), None))
    out_specs = (P(("gx", "gy"), None), P(("gx", "gy"), None))
    return jax.shard_map(shards, mesh=mesh, in_specs=in_specs, out_specs=out_specs, check_vma=False)
```

```python
import functools
import math

import jax
import jax.numpy as jnp
from jax import lax
from jax.experimental import pallas as pl
from jax.experimental.pallas import tpu as pltpu
from jax.sharding import PartitionSpec as P

PIVOTS = 128
KERNEL_SCALE = 32
BAND = 3
STRIP = 8
LANES = 128
EXTRA = 16
CHUNK = 256
LONG = pl.CostEstimate(flops=1 << 34, bytes_accessed=1, transcendentals=0)


jitter = 0.1
noise_weight = 0.5


def shifted(value, axis, steps):
    count = lax.axis_size(axis)
    return lax.ppermute(value, axis, [((i + steps) % count, i) for i in range(count)])


def swapped(value, axis, bit):
    return lax.ppermute(value, axis, [(i ^ bit, i) for i in range(lax.axis_size(axis))])


def spread(value, axis):
    count = lax.axis_size(axis)
    bit = 1
    while bit < count:
        wide = 2 if (count // bit).bit_length() % 2 == 0 else 4
        value = sum((swapped(value, axis, bit * k) for k in range(1, wide)), value)
        bit *= wide
    return value


def zero_like(value):
    return jnp.minimum(jnp.abs(value), 0)


def cross(piece, bits):
    outer, inner = lax.axis_size("gx"), lax.axis_size("gy")
    pairs = []
    for x in range(outer):
        for z in range(inner):
            source = (x - 1 if z ^ bits > z else x + 1) % outer
            pairs.append((source * inner + z, x * inner + z))
    return lax.ppermute(piece, ("gx", "gy"), pairs)


def direct_blocks(value):
    return [shifted(value, ("gx", "gy"), k) for k in range(-BAND, BAND + 1) if k != 0]


def in_vmem(count):
    return [pl.BlockSpec(memory_space=pltpu.VMEM)] * count


def thirds(value):
    high = value.astype(jnp.bfloat16)
    rest = value - high.astype(jnp.float32)
    middle = rest.astype(jnp.bfloat16)
    return high, middle, (rest - middle.astype(jnp.float32)).astype(jnp.bfloat16)


def product(left, right, contract, precision=None):
    return lax.dot_general(
        left, right, (contract, ((), ())), precision=precision, preferred_element_type=jnp.float32
    )


def extended(columns, ones_first):
    wide = columns.astype(jnp.float32)
    half = -0.5 * jnp.sum(wide * wide, axis=0, keepdims=True)
    terms = [term.astype(jnp.float32) for term in thirds(half)]
    shape = (EXTRA, columns.shape[1])
    level = lax.broadcasted_iota(jnp.int32, shape, 0)
    first = 0 if ones_first else 3
    below = jnp.where((level >= first) & (level < first + 3), 1.0, 0.0)
    for i, term in enumerate(terms):
        below = jnp.where(level == 3 - first + i, jnp.broadcast_to(term, shape), below)
    return jnp.concatenate([wide, below], axis=0)


def kernel_of(product_of_extended):
    return jnp.exp2(product_of_extended * (2.0 / KERNEL_SCALE * math.log2(math.e)))


def pick_kernel(owner_ref, pivot_ref, point_ref, out_ref):
    count = point_ref.shape[1]
    me = lax.axis_index(("gx", "gy"))
    wanted = [jnp.where(owner_ref[r] == me, pivot_ref[r:r + 1, :], -1) for r in range(2)]
    wanted = jnp.concatenate(wanted, axis=1)
    place = lax.broadcasted_iota(jnp.int32, (count, wanted.shape[1]), 0)
    chosen = jnp.where(place == wanted, 1.0, 0.0).astype(jnp.bfloat16)
    out_ref[...] = product(point_ref[...], chosen, ((1,), (0,))).astype(jnp.bfloat16)


def pick(owners, pivots, points_t):
    return pl.pallas_call(
        pick_kernel,
        out_shape=pltpu.VMEM((points_t.shape[0], 2 * PIVOTS), jnp.bfloat16),
        in_specs=[pl.BlockSpec(memory_space=pltpu.SMEM)] + in_vmem(2),
        out_specs=in_vmem(1)[0],
        name="pick",
    )(owners, pivots, points_t)


def column(strip, lane):
    return jnp.broadcast_to(strip[:, lane:lane + 1], strip.shape)


def row(strip, i):
    return jnp.broadcast_to(strip[i:i + 1, :], strip.shape)


def total_of(terms):
    while len(terms) > 1:
        terms = [terms[i] + terms[i + 1] if i + 1 < len(terms) else terms[i] for i in range(0, len(terms), 2)]
    return terms[0]


def four_pivots(a):
    rows = len(a)
    x = [[None] * (i + 1) for i in range(4)]
    scale = [None] * 4
    product_so_far = None
    for k in range(4):
        pivot = a[k][k]
        x[k][k] = product_so_far
        product_so_far = pivot if k == 0 else product_so_far * pivot
        scale[k] = lax.rsqrt(product_so_far)
        for i in range(k + 1, rows):
            for j in range(k + 1, min(i, 3) + 1):
                a[i][j] = pivot * a[i][j] - a[i][k] * a[j][k]
        for i in range(k + 1, 4):
            for j in range(k):
                x[i][j] = pivot * x[i][j] - a[i][k] * x[k][j]
            x[i][k] = -a[i][k] if k == 0 else -a[i][k] * x[k][k]
        yield
    factor = [[a[i][k] * scale[k] for k in range(4)] for i in range(4, rows)]
    return factor, x, scale


def combined(entries, columns):
    return total_of([column if entry is None else entry * column for entry, column in zip(entries, columns)])


def block_rows(columns, entered, fetch):
    a = [[row(columns[k], i) for k in range(i + 1)] for i in range(STRIP)]
    yield
    below, x, scale = yield from four_pivots([list(entries) for entries in a])
    one = [[scale[i] if entry is None else entry * scale[i] for entry in x[i]] for i in range(4)]
    rest = [
        [a[4 + i][4 + j] - total_of([below[i][k] * below[j][k] for k in range(4)]) for j in range(i + 1)]
        for i in range(4)
    ]

    def halfway(values):
        upper = [combined(one[k], values[:k + 1]) for k in range(4)]
        return upper, [values[4 + m] - total_of([below[m][j] * upper[j] for j in range(4)]) for m in range(4)]

    def updated(diagonal, factors):
        return [diagonal[j] - total_of([f * row(f, j) for f in factors]) for j in range(STRIP)]

    upper, lower = halfway(entered)
    coming = fetch()
    if coming is not None:
        found, left = halfway(coming[0])
        diagonal = updated(coming[1], found)
    _, x, scale = yield from four_pivots(rest)
    two = [[scale[i] if entry is None else entry * scale[i] for entry in x[i]] for i in range(4)]

    def rear(values):
        return [combined(two[k], values[:k + 1]) for k in range(4)]

    if coming is not None:
        more = rear(left)
        coming = found + more, updated(diagonal, more)

    def solve(values):
        front, values = halfway(values)
        return front + rear(values)

    return solve, upper + rear(lower), coming


def inverse_factor(strips, beside):
    lane = lax.broadcasted_iota(jnp.int32, (STRIP, LANES), 1)
    level = lax.broadcasted_iota(jnp.int32, (STRIP, LANES), 0)
    strips = list(strips)
    result = []
    waiting = []

    def finish(p, own, solve, rows):
        def update(r):
            factors = solve([column(strips[r], p * STRIP + j) for j in range(STRIP)])
            terms = [factors[k] * rows[k] for k in range(STRIP)]
            strips[r] = jnp.where(own, 0.0, strips[r]) - total_of(terms)

        return [functools.partial(update, r) for r in range(p + 2, len(strips))]

    columns = [column(strips[0], k) for k in range(STRIP)]
    for p in range(len(strips)):
        start = p * STRIP
        own = (lane >= start) & (lane < start + STRIP)
        if beside:
            waiting.append(beside.pop(0))
        entered = jnp.where(own, jnp.where(lane - start == level, 1.0, 0.0), strips[p])

        def fetch():
            if p + 1 == len(strips):
                return None
            return [[column(strips[p + 1], at + j) for j in range(STRIP)] for at in (start, start + STRIP)]

        steps = block_rows(columns, [row(entered, k) for k in range(STRIP)], fetch)
        while True:
            try:
                next(steps)
            except StopIteration as ended:
                solve, rows, coming = ended.value
                break
            for _ in range(2):
                if waiting:
                    waiting.pop(0)()
        while waiting:
            waiting.pop(0)()
        done = rows[0]
        for k in range(1, STRIP):
            done = jnp.where(level == k, rows[k], done)
        result.append(done)
        if coming is not None:
            found, columns = coming
            update = total_of([found[k] * rows[k] for k in range(STRIP)])
            strips[p + 1] = jnp.where(own, 0.0, strips[p + 1]) - update
            waiting = finish(p, own, solve, rows)
    return [jnp.where(lane < (p + 1) * STRIP, done, 0.0) for p, done in enumerate(result)]


def probe_kernel(
    pivot_ref, point_ref, coeff_ref, noise_ref, inverse_ref, probe_ref, sent_ref, high_ref, middle_ref, little_ref
):
    hp = lax.Precision.HIGHEST
    size = pivot_ref.shape[1]
    half = size // 2
    pivots = jnp.transpose(padded(extended(pivot_ref[...], True))).astype(jnp.bfloat16)
    others = padded(extended(pivot_ref[...], False)).astype(jnp.bfloat16)
    points = padded(extended(point_ref[...], False)).astype(jnp.bfloat16)

    def columns_at(start):
        at = slice(start, start + LANES)
        cols = kernel_of(product(pivots, points[:, at], ((1,), (0,))))
        high_ref[:, at], middle_ref[:, at], little_ref[:, at] = thirds(cols)

    gram = kernel_of(product(pivots, others, ((1,), (0,))))
    equal = lax.broadcasted_iota(jnp.int32, gram.shape, 0) == lax.broadcasted_iota(jnp.int32, gram.shape, 1)
    gram = gram + jnp.where(equal, jitter, 0.0)

    def inverted(block, beside):
        strips = [block[s:s + STRIP, :] for s in range(0, half, STRIP)]
        return jnp.concatenate(inverse_factor(strips, beside), axis=0)

    beside = [functools.partial(columns_at, start) for start in range(0, points.shape[1], LANES)]
    one = inverted(gram[:half, :half], beside)
    below = product(gram[half:, :half], one, ((1,), (1,)), hp)
    back = product(below, one, ((1,), (0,)), hp)
    two = inverted(gram[half:, half:] - product(below, below, ((1,), (1,)), hp), beside)
    coeffs = coeff_ref[...]
    start = product(coeffs[:, :half], one, ((1,), (0,)), hp)
    later = product(coeffs[:, half:], two, ((1,), (0,)), hp)
    weights = jnp.concatenate([start - product(later, back, ((1,), (0,)), hp), later], axis=1)

    rows = weights.shape[0]
    stacked = jnp.concatenate(thirds(weights), axis=0)
    by_high = product(stacked, high_ref[...], ((1,), (0,)))
    by_middle = product(stacked[:2 * rows], middle_ref[...], ((1,), (0,)))
    by_little = product(stacked[:rows], little_ref[...], ((1,), (0,)))
    small = by_high[2 * rows:] + by_middle[rows:] + by_little
    probes = by_high[:rows] + (by_high[rows:2 * rows] + by_middle[:rows] + small) + noise_ref[...]
    probe_ref[...] = probes
    sent_ref[...] = probes.astype(jnp.bfloat16)

    inverse_ref[:half, :half] = one
    inverse_ref[:half, half:] = jnp.zeros((half, half), jnp.float32)
    inverse_ref[half:, :half] = -product(two, back, ((1,), (0,)), hp)
    inverse_ref[half:, half:] = two


def probes_of(pivots_t, points_t, coeffs_t, noise_t):
    size = pivots_t.shape[1]
    count = points_t.shape[1]
    return pl.pallas_call(
        probe_kernel,
        out_shape=(
            pltpu.VMEM((size, size), jnp.float32),
            pltpu.VMEM(noise_t.shape, jnp.float32),
            pltpu.VMEM(noise_t.shape, jnp.bfloat16),
        ),
        in_specs=in_vmem(4),
        out_specs=tuple(in_vmem(3)),
        scratch_shapes=[pltpu.VMEM((size, count), jnp.bfloat16)] * 3,
        cost_estimate=LONG,
        compiler_params=pltpu.CompilerParams(vmem_limit_bytes=32 * 1024 * 1024),
        name="probes",
    )(pivots_t, points_t, coeffs_t, noise_t)


def padded(value):
    return jnp.concatenate([value, jnp.zeros((LANES - value.shape[0], value.shape[1]), value.dtype)], axis=0)


def tile_terms(own, other, probes):
    return product(kernel_of(product(own, other, ((1,), (0,)))).astype(jnp.bfloat16), probes, ((1,), (1,)))


def factor_kernel(pivot_ref, point_ref, inverse_ref, awaited_ref, factor_ref, zero_ref):
    count = point_ref.shape[1]
    own = jnp.transpose(padded(extended(point_ref[...], True))).astype(jnp.bfloat16)
    pivots = padded(extended(pivot_ref[...], False)).astype(jnp.bfloat16)
    high, middle, _ = thirds(inverse_ref[...])
    for s in range(0, count, CHUNK):
        rows = own[s:s + CHUNK, :]
        cols_high, cols_middle, _ = thirds(kernel_of(product(rows, pivots, ((1,), (0,)))))
        factor_ref[s:s + CHUNK, :] = (
            product(cols_high, middle, ((1,), (1,))) + product(cols_middle, high, ((1,), (1,)))
        ) + product(cols_high, high, ((1,), (1,)))
    zero_ref[...] = jnp.zeros_like(zero_ref)


def factor_of(pivots_t, points_t, inverse, awaited):
    size = pivots_t.shape[1]
    depth, count = points_t.shape
    return pl.pallas_call(
        factor_kernel,
        out_shape=(
            jax.ShapeDtypeStruct((count, size), jnp.float32),
            pltpu.VMEM((depth, count), jnp.bfloat16),
        ),
        in_specs=in_vmem(3) + [pl.BlockSpec(memory_space=pl.ANY)],
        out_specs=tuple(in_vmem(2)),
        compiler_params=pltpu.CompilerParams(vmem_limit_bytes=32 * 1024 * 1024),
        cost_estimate=pl.CostEstimate(
            flops=6 * count * size * size // 8,
            bytes_accessed=6 * count * size // 8,
            transcendentals=count * size // 8,
        ),
        name="factor",
    )(pivots_t, points_t, inverse, awaited)


def band_kernel(pieces, first, last, *refs):
    own_ref = refs[0]
    depth, count = own_ref.shape
    rest = list(refs[1 + max(place for piece in pieces for place, _ in piece):])
    before_ref = None if first else rest.pop(0)
    own = jnp.transpose(padded(extended(own_ref[...], True))).astype(jnp.bfloat16)
    blocks = []
    for (point_at, point_row), (probe_at, probe_row) in pieces:
        points = refs[point_at][point_row:point_row + depth, :]
        blocks.append((padded(extended(points, False)).astype(jnp.bfloat16), refs[probe_at], probe_row))
    for s in range(0, count, CHUNK):
        total = None if first else before_ref[s:s + CHUNK, :]
        for other, probe_ref, probe_row in blocks:
            term = tile_terms(own[s:s + CHUNK, :], other, probe_ref[probe_row:, :])
            total = term if total is None else total + term
        if last:
            probe_ref, out_ref = rest
            scale = 1.0 / (count ** 0.5)
            out_ref[:, s:s + CHUNK] = jnp.transpose(total) * scale + noise_weight * probe_ref[:, s:s + CHUNK]
        else:
            rest[0][s:s + CHUNK, :] = total
    if not last:
        rest[1][...] = jnp.zeros_like(rest[1])


def band_sum(own, pieces, before=None, probes=None):
    depth, count = own.shape
    first, last = before is None, probes is not None
    operands = [own]
    places = []
    for piece in pieces:
        place = []
        for array, start in piece:
            known = [i for i, operand in enumerate(operands) if operand is array]
            if not known:
                operands.append(array)
            place.append((known[0] if known else len(operands) - 1, start))
        places.append(tuple(place))
    array, start = pieces[0][1]
    width = array.shape[0] - start
    operands += ([] if first else [before]) + ([probes] if last else [])
    if last:
        out_shape = jax.ShapeDtypeStruct((width, count), jnp.float32)
    else:
        out_shape = (pltpu.VMEM((count, width), jnp.float32), pltpu.VMEM((width, count), jnp.bfloat16))
    return pl.pallas_call(
        functools.partial(band_kernel, tuple(places), first, last),
        out_shape=out_shape,
        in_specs=in_vmem(len(operands)),
        out_specs=in_vmem(1)[0] if last else tuple(in_vmem(2)),
        compiler_params=pltpu.CompilerParams(vmem_limit_bytes=32 * 1024 * 1024),
        cost_estimate=pl.CostEstimate(
            flops=1 if first else len(pieces) * 4 * count * count * LANES,
            bytes_accessed=1 if first else 4 * count * width * len(operands),
            transcendentals=0 if first else len(pieces) * count * count,
        ),
        name="band_sum",
    )(*operands)


def shards(points, pivots, owners, coeffs, noise):
    tall = lax.axis_size("gy") == BAND + 1
    points = points.T
    depth = points.shape[0]
    row_sum = spread(pick(owners, pivots, points), "gx")
    if tall:
        far = swapped(points, "gy", 2)
        row_sum = row_sum + zero_like(far[:, :row_sum.shape[1]])
        pair = swapped(jnp.concatenate([points, far], axis=0), "gy", 1)
    else:
        near = direct_blocks(points)
    pivot_points = spread(row_sum, "gy")

    inverse, probes, sent = probes_of(pivot_points, points, coeffs.T, noise.T)
    total, zeros = band_sum(points, [((points, 0), (sent, 0))])
    if tall:
        leaving = sent + zero_like(pair[:depth])
        two = swapped(leaving, "gy", 2)
        one = swapped(leaving, "gy", 1) + zeros
        factor, zeros = factor_of(pivot_points, points, inverse, one)
        two = two + zeros
        cross_one = cross(jnp.concatenate([pair[:depth], one], axis=0), 1)
        three = swapped(two, "gy", 1)
        cross_two = cross(jnp.concatenate([far, two], axis=0), 2)
        total, zeros = band_sum(points, [((pair, 0), (one, 0)), ((far, 0), (two, 0))], total)
        cross_three = cross(jnp.concatenate([pair[depth:], three + zeros], axis=0), 3)
        crossed = [((stacked, 0), (stacked, depth)) for stacked in (cross_one, cross_two, cross_three)]
        total, _ = band_sum(points, [((pair, depth), (three, 0)), crossed[0]], total)
        total, _ = band_sum(points, crossed[1:2], total)
        kernel_probes = band_sum(points, crossed[2:], total, probes)
    else:
        factor, _ = factor_of(pivot_points, points, inverse, zeros)
        pieces = [((block, 0), (probe, 0)) for block, probe in zip(near, direct_blocks(sent))]
        total, _ = band_sum(points, pieces[:3], total)
        kernel_probes = band_sum(points, pieces[3:], total, probes)
    return (kernel_probes.T, factor)


def solution(mesh):
    in_specs = (P(("gx", "gy"), None), P(), P(), P(), P(("gx", "gy"), None))
    out_specs = (P(("gx", "gy"), None), P(("gx", "gy"), None))
    return jax.shard_map(shards, mesh=mesh, in_specs=in_specs, out_specs=out_specs, check_vma=False)
```

```python
import functools
import math

import jax
import jax.numpy as jnp
from jax import lax
from jax.experimental import pallas as pl
from jax.experimental.pallas import tpu as pltpu
from jax.sharding import PartitionSpec as P

PIVOTS = 128
KERNEL_SCALE = 32
BAND = 3
STRIP = 8
LANES = 128
EXTRA = 16
CHUNK = 256
LONG = pl.CostEstimate(flops=1 << 34, bytes_accessed=1, transcendentals=0)


jitter = 0.1
noise_weight = 0.5


def shifted(value, axis, steps):
    count = lax.axis_size(axis)
    return lax.ppermute(value, axis, [((i + steps) % count, i) for i in range(count)])


def swapped(value, axis, bit):
    return lax.ppermute(value, axis, [(i ^ bit, i) for i in range(lax.axis_size(axis))])


def spread(value, axis):
    count = lax.axis_size(axis)
    bit = 1
    while bit < count:
        wide = 2 if (count // bit).bit_length() % 2 == 0 else 4
        value = sum((swapped(value, axis, bit * k) for k in range(1, wide)), value)
        bit *= wide
    return value


def zero_like(value):
    return jnp.minimum(jnp.abs(value), 0)


def cross(piece, bits):
    outer, inner = lax.axis_size("gx"), lax.axis_size("gy")
    pairs = []
    for x in range(outer):
        for z in range(inner):
            source = (x - 1 if z ^ bits > z else x + 1) % outer
            pairs.append((source * inner + z, x * inner + z))
    return lax.ppermute(piece, ("gx", "gy"), pairs)


def direct_blocks(value):
    return [shifted(value, ("gx", "gy"), k) for k in range(-BAND, BAND + 1) if k != 0]


def in_vmem(count):
    return [pl.BlockSpec(memory_space=pltpu.VMEM)] * count


def thirds(value):
    high = value.astype(jnp.bfloat16)
    rest = value - high.astype(jnp.float32)
    middle = rest.astype(jnp.bfloat16)
    return high, middle, (rest - middle.astype(jnp.float32)).astype(jnp.bfloat16)


def product(left, right, contract, precision=None):
    return lax.dot_general(
        left, right, (contract, ((), ())), precision=precision, preferred_element_type=jnp.float32
    )


def extended(columns, ones_first):
    wide = columns.astype(jnp.float32)
    half = -0.5 * jnp.sum(wide * wide, axis=0, keepdims=True)
    terms = [term.astype(jnp.float32) for term in thirds(half)]
    shape = (EXTRA, columns.shape[1])
    level = lax.broadcasted_iota(jnp.int32, shape, 0)
    first = 0 if ones_first else 3
    below = jnp.where((level >= first) & (level < first + 3), 1.0, 0.0)
    for i, term in enumerate(terms):
        below = jnp.where(level == 3 - first + i, jnp.broadcast_to(term, shape), below)
    return jnp.concatenate([wide, below], axis=0)


def kernel_of(product_of_extended):
    return jnp.exp2(product_of_extended * (2.0 / KERNEL_SCALE * math.log2(math.e)))


def pick_kernel(owner_ref, pivot_ref, point_ref, out_ref):
    count = point_ref.shape[1]
    me = lax.axis_index(("gx", "gy"))
    wanted = [jnp.where(owner_ref[r] == me, pivot_ref[r:r + 1, :], -1) for r in range(2)]
    wanted = jnp.concatenate(wanted, axis=1)
    place = lax.broadcasted_iota(jnp.int32, (count, wanted.shape[1]), 0)
    chosen = jnp.where(place == wanted, 1.0, 0.0).astype(jnp.bfloat16)
    out_ref[...] = product(point_ref[...], chosen, ((1,), (0,))).astype(jnp.bfloat16)


def pick(owners, pivots, points_t):
    return pl.pallas_call(
        pick_kernel,
        out_shape=pltpu.VMEM((points_t.shape[0], 2 * PIVOTS), jnp.bfloat16),
        in_specs=[pl.BlockSpec(memory_space=pltpu.SMEM)] + in_vmem(2),
        out_specs=in_vmem(1)[0],
        name="pick",
    )(owners, pivots, points_t)


def column(strip, lane):
    return jnp.broadcast_to(strip[:, lane:lane + 1], strip.shape)


def row(strip, i):
    return jnp.broadcast_to(strip[i:i + 1, :], strip.shape)


def total_of(terms):
    while len(terms) > 1:
        terms = [terms[i] + terms[i + 1] if i + 1 < len(terms) else terms[i] for i in range(0, len(terms), 2)]
    return terms[0]


def four_pivots(a):
    rows = len(a)
    x = [[None] * (i + 1) for i in range(4)]
    scale = [None] * 4
    product_so_far = None
    for k in range(4):
        pivot = a[k][k]
        x[k][k] = product_so_far
        product_so_far = pivot if k == 0 else product_so_far * pivot
        scale[k] = lax.rsqrt(product_so_far)
        for i in range(k + 1, rows):
            for j in range(k + 1, min(i, 3) + 1):
                a[i][j] = pivot * a[i][j] - a[i][k] * a[j][k]
        for i in range(k + 1, 4):
            for j in range(k):
                x[i][j] = pivot * x[i][j] - a[i][k] * x[k][j]
            x[i][k] = -a[i][k] if k == 0 else -a[i][k] * x[k][k]
        yield
    factor = [[a[i][k] * scale[k] for k in range(4)] for i in range(4, rows)]
    return factor, x, scale


def combined(entries, columns):
    return total_of([column if entry is None else entry * column for entry, column in zip(entries, columns)])


def block_rows(columns, entered, fetch):
    a = [[row(columns[k], i) for k in range(i + 1)] for i in range(STRIP)]
    yield
    below, x, scale = yield from four_pivots([list(entries) for entries in a])
    one = [[scale[i] if entry is None else entry * scale[i] for entry in x[i]] for i in range(4)]
    rest = [
        [a[4 + i][4 + j] - total_of([below[i][k] * below[j][k] for k in range(4)]) for j in range(i + 1)]
        for i in range(4)
    ]

    def halfway(values):
        upper = [combined(one[k], values[:k + 1]) for k in range(4)]
        return upper, [values[4 + m] - total_of([below[m][j] * upper[j] for j in range(4)]) for m in range(4)]

    def updated(diagonal, factors):
        return [diagonal[j] - total_of([f * row(f, j) for f in factors]) for j in range(STRIP)]

    upper, lower = halfway(entered)
    coming = fetch()
    if coming is not None:
        found, left = halfway(coming[0])
        diagonal = updated(coming[1], found)
    _, x, scale = yield from four_pivots(rest)
    two = [[scale[i] if entry is None else entry * scale[i] for entry in x[i]] for i in range(4)]

    def rear(values):
        return [combined(two[k], values[:k + 1]) for k in range(4)]

    if coming is not None:
        more = rear(left)
        coming = found + more, updated(diagonal, more)

    def solve(values):
        front, values = halfway(values)
        return front + rear(values)

    return solve, upper + rear(lower), coming


def inverse_factor(strips, beside):
    lane = lax.broadcasted_iota(jnp.int32, (STRIP, LANES), 1)
    level = lax.broadcasted_iota(jnp.int32, (STRIP, LANES), 0)
    strips = list(strips)
    result = []
    waiting = []

    def finish(p, own, solve, rows):
        def update(r):
            factors = solve([column(strips[r], p * STRIP + j) for j in range(STRIP)])
            terms = [factors[k] * rows[k] for k in range(STRIP)]
            strips[r] = jnp.where(own, 0.0, strips[r]) - total_of(terms)

        return [functools.partial(update, r) for r in range(p + 2, len(strips))]

    columns = [column(strips[0], k) for k in range(STRIP)]
    for p in range(len(strips)):
        start = p * STRIP
        own = (lane >= start) & (lane < start + STRIP)
        if beside:
            waiting.append(beside.pop(0))
        entered = jnp.where(own, jnp.where(lane - start == level, 1.0, 0.0), strips[p])

        def fetch():
            if p + 1 == len(strips):
                return None
            return [[column(strips[p + 1], at + j) for j in range(STRIP)] for at in (start, start + STRIP)]

        steps = block_rows(columns, [row(entered, k) for k in range(STRIP)], fetch)
        while True:
            try:
                next(steps)
            except StopIteration as ended:
                solve, rows, coming = ended.value
                break
            for _ in range(2):
                if waiting:
                    waiting.pop(0)()
        while waiting:
            waiting.pop(0)()
        done = rows[0]
        for k in range(1, STRIP):
            done = jnp.where(level == k, rows[k], done)
        result.append(done)
        if coming is not None:
            found, columns = coming
            update = total_of([found[k] * rows[k] for k in range(STRIP)])
            strips[p + 1] = jnp.where(own, 0.0, strips[p + 1]) - update
            waiting = finish(p, own, solve, rows)
    return [jnp.where(lane < (p + 1) * STRIP, done, 0.0) for p, done in enumerate(result)]


def probe_kernel(
    pivot_ref, point_ref, coeff_ref, noise_ref, inverse_ref, probe_ref, sent_ref, high_ref, middle_ref, little_ref
):
    hp = lax.Precision.HIGHEST
    size = pivot_ref.shape[1]
    half = size // 2
    pivots = jnp.transpose(padded(extended(pivot_ref[...], True))).astype(jnp.bfloat16)
    others = padded(extended(pivot_ref[...], False)).astype(jnp.bfloat16)
    points = padded(extended(point_ref[...], False)).astype(jnp.bfloat16)

    def columns_at(start):
        at = slice(start, start + LANES)
        cols = kernel_of(product(pivots, points[:, at], ((1,), (0,))))
        high_ref[:, at], middle_ref[:, at], little_ref[:, at] = thirds(cols)

    gram = kernel_of(product(pivots, others, ((1,), (0,))))
    equal = lax.broadcasted_iota(jnp.int32, gram.shape, 0) == lax.broadcasted_iota(jnp.int32, gram.shape, 1)
    gram = gram + jnp.where(equal, jitter, 0.0)

    def inverted(block, beside):
        strips = [block[s:s + STRIP, :] for s in range(0, half, STRIP)]
        return jnp.concatenate(inverse_factor(strips, beside), axis=0)

    beside = [functools.partial(columns_at, start) for start in range(0, points.shape[1], LANES)]
    one = inverted(gram[:half, :half], beside)
    below = product(gram[half:, :half], one, ((1,), (1,)), hp)
    back = product(below, one, ((1,), (0,)), hp)
    two = inverted(gram[half:, half:] - product(below, below, ((1,), (1,)), hp), beside)
    coeffs = coeff_ref[...]
    start = product(coeffs[:, :half], one, ((1,), (0,)), hp)
    later = product(coeffs[:, half:], two, ((1,), (0,)), hp)
    weights = jnp.concatenate([start - product(later, back, ((1,), (0,)), hp), later], axis=1)

    rows = weights.shape[0]
    stacked = jnp.concatenate(thirds(weights), axis=0)
    by_high = product(stacked, high_ref[...], ((1,), (0,)))
    by_middle = product(stacked[:2 * rows], middle_ref[...], ((1,), (0,)))
    by_little = product(stacked[:rows], little_ref[...], ((1,), (0,)))
    small = by_high[2 * rows:] + by_middle[rows:] + by_little
    probes = by_high[:rows] + (by_high[rows:2 * rows] + by_middle[:rows] + small) + noise_ref[...]
    probe_ref[...] = probes
    sent_ref[...] = probes.astype(jnp.bfloat16)

    inverse_ref[:half, :half] = one
    inverse_ref[:half, half:] = jnp.zeros((half, half), jnp.float32)
    inverse_ref[half:, :half] = -product(two, back, ((1,), (0,)), hp)
    inverse_ref[half:, half:] = two


def probes_of(pivots_t, points_t, coeffs_t, noise_t):
    size = pivots_t.shape[1]
    count = points_t.shape[1]
    return pl.pallas_call(
        probe_kernel,
        out_shape=(
            pltpu.VMEM((size, size), jnp.float32),
            pltpu.VMEM(noise_t.shape, jnp.float32),
            pltpu.VMEM(noise_t.shape, jnp.bfloat16),
        ),
        in_specs=in_vmem(4),
        out_specs=tuple(in_vmem(3)),
        scratch_shapes=[pltpu.VMEM((size, count), jnp.bfloat16)] * 3,
        cost_estimate=LONG,
        compiler_params=pltpu.CompilerParams(vmem_limit_bytes=32 * 1024 * 1024),
        name="probes",
    )(pivots_t, points_t, coeffs_t, noise_t)


def padded(value):
    return jnp.concatenate([value, jnp.zeros((LANES - value.shape[0], value.shape[1]), value.dtype)], axis=0)


def tile_terms(own, other, probes):
    return product(kernel_of(product(own, other, ((1,), (0,)))).astype(jnp.bfloat16), probes, ((1,), (1,)))


def factor_kernel(pivot_ref, point_ref, inverse_ref, awaited_ref, factor_ref, zero_ref):
    count = point_ref.shape[1]
    own = jnp.transpose(padded(extended(point_ref[...], True))).astype(jnp.bfloat16)
    pivots = padded(extended(pivot_ref[...], False)).astype(jnp.bfloat16)
    high, middle, _ = thirds(inverse_ref[...])
    for s in range(0, count, CHUNK):
        rows = own[s:s + CHUNK, :]
        cols_high, cols_middle, _ = thirds(kernel_of(product(rows, pivots, ((1,), (0,)))))
        factor_ref[s:s + CHUNK, :] = (
            product(cols_high, middle, ((1,), (1,))) + product(cols_middle, high, ((1,), (1,)))
        ) + product(cols_high, high, ((1,), (1,)))
    zero_ref[...] = jnp.zeros_like(zero_ref)


def factor_of(pivots_t, points_t, inverse, awaited):
    size = pivots_t.shape[1]
    depth, count = points_t.shape
    return pl.pallas_call(
        factor_kernel,
        out_shape=(
            jax.ShapeDtypeStruct((count, size), jnp.float32),
            pltpu.VMEM((depth, count), jnp.bfloat16),
        ),
        in_specs=in_vmem(3) + [pl.BlockSpec(memory_space=pl.ANY)],
        out_specs=tuple(in_vmem(2)),
        compiler_params=pltpu.CompilerParams(vmem_limit_bytes=32 * 1024 * 1024),
        cost_estimate=pl.CostEstimate(
            flops=6 * count * size * size // 8,
            bytes_accessed=6 * count * size // 8,
            transcendentals=count * size // 8,
        ),
        name="factor",
    )(pivots_t, points_t, inverse, awaited)


def band_kernel(pieces, first, last, *refs):
    own_ref = refs[0]
    depth, count = own_ref.shape
    rest = list(refs[1 + max(place for piece in pieces for place, _ in piece):])
    before_ref = None if first else rest.pop(0)
    own = jnp.transpose(padded(extended(own_ref[...], True))).astype(jnp.bfloat16)
    blocks = []
    for (point_at, point_row), (probe_at, probe_row) in pieces:
        points = refs[point_at][point_row:point_row + depth, :]
        blocks.append((padded(extended(points, False)).astype(jnp.bfloat16), refs[probe_at], probe_row))
    for s in range(0, count, CHUNK):
        total = None if first else before_ref[s:s + CHUNK, :]
        for other, probe_ref, probe_row in blocks:
            term = tile_terms(own[s:s + CHUNK, :], other, probe_ref[probe_row:, :])
            total = term if total is None else total + term
        if last:
            probe_ref, out_ref = rest
            scale = 1.0 / (count ** 0.5)
            out_ref[:, s:s + CHUNK] = jnp.transpose(total) * scale + noise_weight * probe_ref[:, s:s + CHUNK]
        else:
            rest[0][s:s + CHUNK, :] = total
    if not last:
        rest[1][...] = jnp.zeros_like(rest[1])


def band_sum(own, pieces, before=None, probes=None):
    depth, count = own.shape
    first, last = before is None, probes is not None
    operands = [own]
    places = []
    for piece in pieces:
        place = []
        for array, start in piece:
            known = [i for i, operand in enumerate(operands) if operand is array]
            if not known:
                operands.append(array)
            place.append((known[0] if known else len(operands) - 1, start))
        places.append(tuple(place))
    array, start = pieces[0][1]
    width = array.shape[0] - start
    operands += ([] if first else [before]) + ([probes] if last else [])
    if last:
        out_shape = jax.ShapeDtypeStruct((width, count), jnp.float32)
    else:
        out_shape = (pltpu.VMEM((count, width), jnp.float32), pltpu.VMEM((width, count), jnp.bfloat16))
    return pl.pallas_call(
        functools.partial(band_kernel, tuple(places), first, last),
        out_shape=out_shape,
        in_specs=in_vmem(len(operands)),
        out_specs=in_vmem(1)[0] if last else tuple(in_vmem(2)),
        compiler_params=pltpu.CompilerParams(vmem_limit_bytes=32 * 1024 * 1024),
        cost_estimate=pl.CostEstimate(
            flops=1 if first else len(pieces) * 4 * count * count * LANES,
            bytes_accessed=1 if first else 4 * count * width * len(operands),
            transcendentals=0 if first else len(pieces) * count * count,
        ),
        name="band_sum",
    )(*operands)


def shards(points, pivots, owners, coeffs, noise):
    tall = lax.axis_size("gy") == BAND + 1
    points = points.T
    depth = points.shape[0]
    row_sum = spread(pick(owners, pivots, points), "gx")
    if tall:
        far = swapped(points, "gy", 2)
        row_sum = row_sum + zero_like(far[:, :row_sum.shape[1]])
        pair = swapped(jnp.concatenate([points, far], axis=0), "gy", 1)
    else:
        near = direct_blocks(points)
    pivot_points = spread(row_sum, "gy")

    inverse, probes, sent = probes_of(pivot_points, points, coeffs.T, noise.T)
    total, zeros = band_sum(points, [((points, 0), (sent, 0))])
    if tall:
        leaving = sent + zero_like(pair[:depth])
        two = swapped(leaving, "gy", 2)
        one = swapped(leaving, "gy", 1) + zeros
        factor, zeros = factor_of(pivot_points, points, inverse, one)
        two = two + zeros
        cross_one = cross(jnp.concatenate([pair[:depth], one], axis=0), 1)
        three = swapped(two, "gy", 1)
        cross_two = cross(jnp.concatenate([far, pair[depth:], two], axis=0), 2)
        total, _ = band_sum(points, [((pair, 0), (one, 0)), ((far, 0), (two, 0))], total)
        total, zeros = band_sum(points, [((cross_one, 0), (cross_one, depth))], total)
        three = three + zeros
        cross_three = cross(three, 3)
        total, _ = band_sum(points, [((cross_two, 0), (cross_two, 2 * depth)), ((pair, depth), (three, 0))], total)
        kernel_probes = band_sum(points, [((cross_two, depth), (cross_three, 0))], total, probes)
    else:
        factor, _ = factor_of(pivot_points, points, inverse, zeros)
        pieces = [((block, 0), (probe, 0)) for block, probe in zip(near, direct_blocks(sent))]
        total, _ = band_sum(points, pieces[:3], total)
        kernel_probes = band_sum(points, pieces[3:], total, probes)
    return (kernel_probes.T, factor)


def solution(mesh):
    in_specs = (P(("gx", "gy"), None), P(), P(), P(), P(("gx", "gy"), None))
    out_specs = (P(("gx", "gy"), None), P(("gx", "gy"), None))
    return jax.shard_map(shards, mesh=mesh, in_specs=in_specs, out_specs=out_specs, check_vma=False)
```

```python
import functools
import math

import jax
import jax.numpy as jnp
from jax import lax
from jax.experimental import pallas as pl
from jax.experimental.pallas import tpu as pltpu
from jax.sharding import PartitionSpec as P

PIVOTS = 128
KERNEL_SCALE = 32
BAND = 3
STRIP = 8
LANES = 128
EXTRA = 16
CHUNK = 256
LONG = pl.CostEstimate(flops=1 << 34, bytes_accessed=1, transcendentals=0)


jitter = 0.1
noise_weight = 0.5


def shifted(value, axis, steps):
    count = lax.axis_size(axis)
    return lax.ppermute(value, axis, [((i + steps) % count, i) for i in range(count)])


def swapped(value, axis, bit):
    return lax.ppermute(value, axis, [(i ^ bit, i) for i in range(lax.axis_size(axis))])


def spread(value, axis):
    count = lax.axis_size(axis)
    bit = 1
    while bit < count:
        wide = 2 if (count // bit).bit_length() % 2 == 0 else 4
        value = sum((swapped(value, axis, bit * k) for k in range(1, wide)), value)
        bit *= wide
    return value


def zero_like(value):
    return jnp.minimum(jnp.abs(value), 0)


def cross(piece, bits):
    outer, inner = lax.axis_size("gx"), lax.axis_size("gy")
    pairs = []
    for x in range(outer):
        for z in range(inner):
            source = (x - 1 if z ^ bits > z else x + 1) % outer
            pairs.append((source * inner + z, x * inner + z))
    return lax.ppermute(piece, ("gx", "gy"), pairs)


def direct_blocks(value):
    return [shifted(value, ("gx", "gy"), k) for k in range(-BAND, BAND + 1) if k != 0]


def in_vmem(count):
    return [pl.BlockSpec(memory_space=pltpu.VMEM)] * count


def thirds(value):
    high = value.astype(jnp.bfloat16)
    rest = value - high.astype(jnp.float32)
    middle = rest.astype(jnp.bfloat16)
    return high, middle, (rest - middle.astype(jnp.float32)).astype(jnp.bfloat16)


def product(left, right, contract, precision=None):
    return lax.dot_general(
        left, right, (contract, ((), ())), precision=precision, preferred_element_type=jnp.float32
    )


def extended(columns, ones_first):
    wide = columns.astype(jnp.float32)
    half = -0.5 * jnp.sum(wide * wide, axis=0, keepdims=True)
    terms = [term.astype(jnp.float32) for term in thirds(half)]
    shape = (EXTRA, columns.shape[1])
    level = lax.broadcasted_iota(jnp.int32, shape, 0)
    first = 0 if ones_first else 3
    below = jnp.where((level >= first) & (level < first + 3), 1.0, 0.0)
    for i, term in enumerate(terms):
        below = jnp.where(level == 3 - first + i, jnp.broadcast_to(term, shape), below)
    return jnp.concatenate([wide, below], axis=0)


def kernel_of(product_of_extended):
    return jnp.exp2(product_of_extended * (2.0 / KERNEL_SCALE * math.log2(math.e)))


def pick_kernel(owner_ref, pivot_ref, point_ref, out_ref):
    count = point_ref.shape[1]
    me = lax.axis_index(("gx", "gy"))
    wanted = [jnp.where(owner_ref[r] == me, pivot_ref[r:r + 1, :], -1) for r in range(2)]
    wanted = jnp.concatenate(wanted, axis=1)
    place = lax.broadcasted_iota(jnp.int32, (count, wanted.shape[1]), 0)
    chosen = jnp.where(place == wanted, 1.0, 0.0).astype(jnp.bfloat16)
    out_ref[...] = product(point_ref[...], chosen, ((1,), (0,))).astype(jnp.bfloat16)


def pick(owners, pivots, points_t):
    return pl.pallas_call(
        pick_kernel,
        out_shape=pltpu.VMEM((points_t.shape[0], 2 * PIVOTS), jnp.bfloat16),
        in_specs=[pl.BlockSpec(memory_space=pltpu.SMEM)] + in_vmem(2),
        out_specs=in_vmem(1)[0],
        name="pick",
    )(owners, pivots, points_t)


def column(strip, lane):
    return jnp.broadcast_to(strip[:, lane:lane + 1], strip.shape)


def row(strip, i):
    return jnp.broadcast_to(strip[i:i + 1, :], strip.shape)


def total_of(terms):
    while len(terms) > 1:
        terms = [terms[i] + terms[i + 1] if i + 1 < len(terms) else terms[i] for i in range(0, len(terms), 2)]
    return terms[0]


def four_pivots(a):
    rows = len(a)
    x = [[None] * (i + 1) for i in range(4)]
    scale = [None] * 4
    product_so_far = None
    for k in range(4):
        pivot = a[k][k]
        x[k][k] = product_so_far
        product_so_far = pivot if k == 0 else product_so_far * pivot
        scale[k] = lax.rsqrt(product_so_far)
        for i in range(k + 1, rows):
            for j in range(k + 1, min(i, 3) + 1):
                a[i][j] = pivot * a[i][j] - a[i][k] * a[j][k]
        for i in range(k + 1, 4):
            for j in range(k):
                x[i][j] = pivot * x[i][j] - a[i][k] * x[k][j]
            x[i][k] = -a[i][k] if k == 0 else -a[i][k] * x[k][k]
        yield
    factor = [[a[i][k] * scale[k] for k in range(4)] for i in range(4, rows)]
    return factor, x, scale


def combined(entries, columns):
    return total_of([column if entry is None else entry * column for entry, column in zip(entries, columns)])


def block_rows(columns, entered, fetch):
    a = [[row(columns[k], i) for k in range(i + 1)] for i in range(STRIP)]
    yield
    below, x, scale = yield from four_pivots([list(entries) for entries in a])
    one = [[scale[i] if entry is None else entry * scale[i] for entry in x[i]] for i in range(4)]
    rest = [
        [a[4 + i][4 + j] - total_of([below[i][k] * below[j][k] for k in range(4)]) for j in range(i + 1)]
        for i in range(4)
    ]

    def halfway(values):
        upper = [combined(one[k], values[:k + 1]) for k in range(4)]
        return upper, [values[4 + m] - total_of([below[m][j] * upper[j] for j in range(4)]) for m in range(4)]

    def updated(diagonal, factors):
        return [diagonal[j] - total_of([f * row(f, j) for f in factors]) for j in range(STRIP)]

    upper, lower = halfway(entered)
    coming = fetch()
    if coming is not None:
        found, left = halfway(coming[0])
        diagonal = updated(coming[1], found)
    _, x, scale = yield from four_pivots(rest)
    two = [[scale[i] if entry is None else entry * scale[i] for entry in x[i]] for i in range(4)]

    def rear(values):
        return [combined(two[k], values[:k + 1]) for k in range(4)]

    if coming is not None:
        more = rear(left)
        coming = found + more, updated(diagonal, more)

    def solve(values):
        front, values = halfway(values)
        return front + rear(values)

    return solve, upper + rear(lower), coming


def inverse_factor(strips, beside):
    lane = lax.broadcasted_iota(jnp.int32, (STRIP, LANES), 1)
    level = lax.broadcasted_iota(jnp.int32, (STRIP, LANES), 0)
    strips = list(strips)
    result = []
    waiting = []

    def finish(p, own, solve, rows):
        def update(r):
            factors = solve([column(strips[r], p * STRIP + j) for j in range(STRIP)])
            terms = [factors[k] * rows[k] for k in range(STRIP)]
            strips[r] = jnp.where(own, 0.0, strips[r]) - total_of(terms)

        return [functools.partial(update, r) for r in range(p + 2, len(strips))]

    columns = [column(strips[0], k) for k in range(STRIP)]
    for p in range(len(strips)):
        start = p * STRIP
        own = (lane >= start) & (lane < start + STRIP)
        if beside:
            waiting.append(beside.pop(0))
        entered = jnp.where(own, jnp.where(lane - start == level, 1.0, 0.0), strips[p])

        def fetch():
            if p + 1 == len(strips):
                return None
            return [[column(strips[p + 1], at + j) for j in range(STRIP)] for at in (start, start + STRIP)]

        steps = block_rows(columns, [row(entered, k) for k in range(STRIP)], fetch)
        while True:
            try:
                next(steps)
            except StopIteration as ended:
                solve, rows, coming = ended.value
                break
            for _ in range(2):
                if waiting:
                    waiting.pop(0)()
        while waiting:
            waiting.pop(0)()
        done = rows[0]
        for k in range(1, STRIP):
            done = jnp.where(level == k, rows[k], done)
        result.append(done)
        if coming is not None:
            found, columns = coming
            update = total_of([found[k] * rows[k] for k in range(STRIP)])
            strips[p + 1] = jnp.where(own, 0.0, strips[p + 1]) - update
            waiting = finish(p, own, solve, rows)
    return [jnp.where(lane < (p + 1) * STRIP, done, 0.0) for p, done in enumerate(result)]


def probe_kernel(
    pivot_ref, point_ref, coeff_ref, noise_ref, inverse_ref, probe_ref, sent_ref, high_ref, middle_ref, little_ref
):
    hp = lax.Precision.HIGHEST
    size = pivot_ref.shape[1]
    half = size // 2
    pivots = jnp.transpose(padded(extended(pivot_ref[...], True))).astype(jnp.bfloat16)
    others = padded(extended(pivot_ref[...], False)).astype(jnp.bfloat16)
    points = padded(extended(point_ref[...], False)).astype(jnp.bfloat16)

    def columns_at(start):
        at = slice(start, start + LANES)
        cols = kernel_of(product(pivots, points[:, at], ((1,), (0,))))
        high_ref[:, at], middle_ref[:, at], little_ref[:, at] = thirds(cols)

    gram = kernel_of(product(pivots, others, ((1,), (0,))))
    equal = lax.broadcasted_iota(jnp.int32, gram.shape, 0) == lax.broadcasted_iota(jnp.int32, gram.shape, 1)
    gram = gram + jnp.where(equal, jitter, 0.0)

    def inverted(block, beside):
        strips = [block[s:s + STRIP, :] for s in range(0, half, STRIP)]
        return jnp.concatenate(inverse_factor(strips, beside), axis=0)

    beside = [functools.partial(columns_at, start) for start in range(0, points.shape[1], LANES)]
    one = inverted(gram[:half, :half], beside)
    below = product(gram[half:, :half], one, ((1,), (1,)), hp)
    back = product(below, one, ((1,), (0,)), hp)
    two = inverted(gram[half:, half:] - product(below, below, ((1,), (1,)), hp), beside)
    coeffs = coeff_ref[...]
    start = product(coeffs[:, :half], one, ((1,), (0,)), hp)
    later = product(coeffs[:, half:], two, ((1,), (0,)), hp)
    weights = jnp.concatenate([start - product(later, back, ((1,), (0,)), hp), later], axis=1)

    rows = weights.shape[0]
    stacked = jnp.concatenate(thirds(weights), axis=0)
    by_high = product(stacked, high_ref[...], ((1,), (0,)))
    by_middle = product(stacked[:2 * rows], middle_ref[...], ((1,), (0,)))
    by_little = product(stacked[:rows], little_ref[...], ((1,), (0,)))
    small = by_high[2 * rows:] + by_middle[rows:] + by_little
    probes = by_high[:rows] + (by_high[rows:2 * rows] + by_middle[:rows] + small) + noise_ref[...]
    probe_ref[...] = probes
    sent_ref[...] = probes.astype(jnp.bfloat16)

    inverse_ref[:half, :half] = one
    inverse_ref[:half, half:] = jnp.zeros((half, half), jnp.float32)
    inverse_ref[half:, :half] = -product(two, back, ((1,), (0,)), hp)
    inverse_ref[half:, half:] = two


def probes_of(pivots_t, points_t, coeffs_t, noise_t):
    size = pivots_t.shape[1]
    count = points_t.shape[1]
    return pl.pallas_call(
        probe_kernel,
        out_shape=(
            pltpu.VMEM((size, size), jnp.float32),
            pltpu.VMEM(noise_t.shape, jnp.float32),
            pltpu.VMEM(noise_t.shape, jnp.bfloat16),
        ),
        in_specs=in_vmem(4),
        out_specs=tuple(in_vmem(3)),
        scratch_shapes=[pltpu.VMEM((size, count), jnp.bfloat16)] * 3,
        cost_estimate=LONG,
        compiler_params=pltpu.CompilerParams(vmem_limit_bytes=32 * 1024 * 1024),
        name="probes",
    )(pivots_t, points_t, coeffs_t, noise_t)


def padded(value):
    return jnp.concatenate([value, jnp.zeros((LANES - value.shape[0], value.shape[1]), value.dtype)], axis=0)


def tile_terms(own, other, probes):
    return product(probes, kernel_of(product(own, other, ((1,), (0,)))).astype(jnp.bfloat16), ((1,), (1,)))


def factor_kernel(pivot_ref, point_ref, inverse_ref, awaited_ref, factor_ref, zero_ref):
    count = point_ref.shape[1]
    own = jnp.transpose(padded(extended(point_ref[...], True))).astype(jnp.bfloat16)
    pivots = padded(extended(pivot_ref[...], False)).astype(jnp.bfloat16)
    high, middle, _ = thirds(inverse_ref[...])
    for s in range(0, count, CHUNK):
        rows = own[s:s + CHUNK, :]
        cols_high, cols_middle, _ = thirds(kernel_of(product(rows, pivots, ((1,), (0,)))))
        factor_ref[s:s + CHUNK, :] = (
            product(cols_high, middle, ((1,), (1,))) + product(cols_middle, high, ((1,), (1,)))
        ) + product(cols_high, high, ((1,), (1,)))
    zero_ref[...] = jnp.zeros_like(zero_ref)


def factor_of(pivots_t, points_t, inverse, awaited):
    size = pivots_t.shape[1]
    depth, count = points_t.shape
    return pl.pallas_call(
        factor_kernel,
        out_shape=(
            jax.ShapeDtypeStruct((count, size), jnp.float32),
            pltpu.VMEM((depth, count), jnp.bfloat16),
        ),
        in_specs=in_vmem(3) + [pl.BlockSpec(memory_space=pl.ANY)],
        out_specs=tuple(in_vmem(2)),
        compiler_params=pltpu.CompilerParams(vmem_limit_bytes=32 * 1024 * 1024),
        cost_estimate=pl.CostEstimate(
            flops=6 * count * size * size // 8,
            bytes_accessed=6 * count * size // 8,
            transcendentals=count * size // 8,
        ),
        name="factor",
    )(pivots_t, points_t, inverse, awaited)


def band_kernel(pieces, first, last, *refs):
    own_ref = refs[0]
    depth, count = own_ref.shape
    rest = list(refs[1 + max(place for piece in pieces for place, _ in piece):])
    before_ref = None if first else rest.pop(0)
    own = jnp.transpose(padded(extended(own_ref[...], True))).astype(jnp.bfloat16)
    blocks = []
    for (point_at, point_row), (probe_at, probe_row) in pieces:
        points = refs[point_at][point_row:point_row + depth, :]
        blocks.append((padded(extended(points, False)).astype(jnp.bfloat16), refs[probe_at], probe_row))
    for s in range(0, count, CHUNK):
        total = None if first else before_ref[:, s:s + CHUNK]
        for other, probe_ref, probe_row in blocks:
            term = tile_terms(own[s:s + CHUNK, :], other, probe_ref[probe_row:, :])
            total = term if total is None else total + term
        if last:
            probe_ref, out_ref = rest
            scale = 1.0 / (count ** 0.5)
            out_ref[:, s:s + CHUNK] = total * scale + noise_weight * probe_ref[:, s:s + CHUNK]
        else:
            rest[0][:, s:s + CHUNK] = total
    if not last:
        rest[1][...] = jnp.zeros_like(rest[1])


def band_sum(own, pieces, before=None, probes=None):
    depth, count = own.shape
    first, last = before is None, probes is not None
    operands = [own]
    places = []
    for piece in pieces:
        place = []
        for array, start in piece:
            known = [i for i, operand in enumerate(operands) if operand is array]
            if not known:
                operands.append(array)
            place.append((known[0] if known else len(operands) - 1, start))
        places.append(tuple(place))
    array, start = pieces[0][1]
    width = array.shape[0] - start
    operands += ([] if first else [before]) + ([probes] if last else [])
    if last:
        out_shape = jax.ShapeDtypeStruct((width, count), jnp.float32)
    else:
        out_shape = (pltpu.VMEM((width, count), jnp.float32), pltpu.VMEM((width, count), jnp.bfloat16))
    return pl.pallas_call(
        functools.partial(band_kernel, tuple(places), first, last),
        out_shape=out_shape,
        in_specs=in_vmem(len(operands)),
        out_specs=in_vmem(1)[0] if last else tuple(in_vmem(2)),
        compiler_params=pltpu.CompilerParams(vmem_limit_bytes=32 * 1024 * 1024),
        cost_estimate=pl.CostEstimate(
            flops=1 if first else len(pieces) * 4 * count * count * LANES,
            bytes_accessed=1 if first else 4 * count * width * len(operands),
            transcendentals=0 if first else len(pieces) * count * count,
        ),
        name="band_sum",
    )(*operands)


def shards(points, pivots, owners, coeffs, noise):
    tall = lax.axis_size("gy") == BAND + 1
    points = points.T
    depth = points.shape[0]
    row_sum = spread(pick(owners, pivots, points), "gx")
    if tall:
        far = swapped(points, "gy", 2)
        row_sum = row_sum + zero_like(far[:, :row_sum.shape[1]])
        pair = swapped(jnp.concatenate([points, far], axis=0), "gy", 1)
    else:
        near = direct_blocks(points)
    pivot_points = spread(row_sum, "gy")

    inverse, probes, sent = probes_of(pivot_points, points, coeffs.T, noise.T)
    total, zeros = band_sum(points, [((points, 0), (sent, 0))])
    if tall:
        leaving = sent + zero_like(pair[:depth])
        two = swapped(leaving, "gy", 2)
        one = swapped(leaving, "gy", 1) + zeros
        factor, zeros = factor_of(pivot_points, points, inverse, one)
        two = two + zeros
        cross_one = cross(jnp.concatenate([pair[:depth], one], axis=0), 1)
        three = swapped(two, "gy", 1)
        cross_two = cross(jnp.concatenate([far, two], axis=0), 2)
        total, zeros = band_sum(points, [((pair, 0), (one, 0)), ((far, 0), (two, 0))], total)
        cross_three = cross(jnp.concatenate([pair[depth:], three + zeros], axis=0), 3)
        crossed = [((stacked, 0), (stacked, depth)) for stacked in (cross_one, cross_two, cross_three)]
        total, _ = band_sum(points, [((pair, depth), (three, 0)), crossed[0]], total)
        total, _ = band_sum(points, crossed[1:2], total)
        kernel_probes = band_sum(points, crossed[2:], total, probes)
    else:
        factor, _ = factor_of(pivot_points, points, inverse, zeros)
        pieces = [((block, 0), (probe, 0)) for block, probe in zip(near, direct_blocks(sent))]
        total, _ = band_sum(points, pieces[:3], total)
        kernel_probes = band_sum(points, pieces[3:], total, probes)
    return (kernel_probes.T, factor)


def solution(mesh):
    in_specs = (P(("gx", "gy"), None), P(), P(), P(), P(("gx", "gy"), None))
    out_specs = (P(("gx", "gy"), None), P(("gx", "gy"), None))
    return jax.shard_map(shards, mesh=mesh, in_specs=in_specs, out_specs=out_specs, check_vma=False)
```

```python
import functools
import math

import jax
import jax.numpy as jnp
from jax import lax
from jax.experimental import pallas as pl
from jax.experimental.pallas import tpu as pltpu
from jax.sharding import PartitionSpec as P

PIVOTS = 128
KERNEL_SCALE = 32
BAND = 3
STRIP = 8
LANES = 128
EXTRA = 16
CHUNK = 256
LONG = pl.CostEstimate(flops=1 << 34, bytes_accessed=1, transcendentals=0)


jitter = 0.1
noise_weight = 0.5


def shifted(value, axis, steps):
    count = lax.axis_size(axis)
    return lax.ppermute(value, axis, [((i + steps) % count, i) for i in range(count)])


def swapped(value, axis, bit):
    return lax.ppermute(value, axis, [(i ^ bit, i) for i in range(lax.axis_size(axis))])


def spread(value, axis):
    count = lax.axis_size(axis)
    bit = 1
    while bit < count:
        wide = 2 if (count // bit).bit_length() % 2 == 0 else 4
        value = sum((swapped(value, axis, bit * k) for k in range(1, wide)), value)
        bit *= wide
    return value


def zero_like(value):
    return jnp.minimum(jnp.abs(value), 0)


def cross(piece, bits):
    outer, inner = lax.axis_size("gx"), lax.axis_size("gy")
    pairs = []
    for x in range(outer):
        for z in range(inner):
            source = (x - 1 if z ^ bits > z else x + 1) % outer
            pairs.append((source * inner + z, x * inner + z))
    return lax.ppermute(piece, ("gx", "gy"), pairs)


def direct_blocks(value):
    return [shifted(value, ("gx", "gy"), k) for k in range(-BAND, BAND + 1) if k != 0]


def in_vmem(count):
    return [pl.BlockSpec(memory_space=pltpu.VMEM)] * count


def thirds(value):
    high = value.astype(jnp.bfloat16)
    rest = value - high.astype(jnp.float32)
    middle = rest.astype(jnp.bfloat16)
    return high, middle, (rest - middle.astype(jnp.float32)).astype(jnp.bfloat16)


def product(left, right, contract, precision=None):
    return lax.dot_general(
        left, right, (contract, ((), ())), precision=precision, preferred_element_type=jnp.float32
    )


def extended(columns, ones_first):
    wide = columns.astype(jnp.float32)
    half = -0.5 * jnp.sum(wide * wide, axis=0, keepdims=True)
    terms = [term.astype(jnp.float32) for term in thirds(half)]
    shape = (EXTRA, columns.shape[1])
    level = lax.broadcasted_iota(jnp.int32, shape, 0)
    first = 0 if ones_first else 3
    below = jnp.where((level >= first) & (level < first + 3), 1.0, 0.0)
    for i, term in enumerate(terms):
        below = jnp.where(level == 3 - first + i, jnp.broadcast_to(term, shape), below)
    return jnp.concatenate([wide, below], axis=0)


def kernel_of(product_of_extended):
    return jnp.exp2(product_of_extended * (2.0 / KERNEL_SCALE * math.log2(math.e)))


def pick_kernel(owner_ref, pivot_ref, point_ref, out_ref):
    count = point_ref.shape[1]
    me = lax.axis_index(("gx", "gy"))
    wanted = [jnp.where(owner_ref[r] == me, pivot_ref[r:r + 1, :], -1) for r in range(2)]
    wanted = jnp.concatenate(wanted, axis=1)
    place = lax.broadcasted_iota(jnp.int32, (count, wanted.shape[1]), 0)
    chosen = jnp.where(place == wanted, 1.0, 0.0).astype(jnp.bfloat16)
    out_ref[...] = product(point_ref[...], chosen, ((1,), (0,))).astype(jnp.bfloat16)


def pick(owners, pivots, points_t):
    return pl.pallas_call(
        pick_kernel,
        out_shape=pltpu.VMEM((points_t.shape[0], 2 * PIVOTS), jnp.bfloat16),
        in_specs=[pl.BlockSpec(memory_space=pltpu.SMEM)] + in_vmem(2),
        out_specs=in_vmem(1)[0],
        name="pick",
    )(owners, pivots, points_t)


def column(strip, lane):
    return jnp.broadcast_to(strip[:, lane:lane + 1], strip.shape)


def row(strip, i):
    return jnp.broadcast_to(strip[i:i + 1, :], strip.shape)


def total_of(terms):
    while len(terms) > 1:
        terms = [terms[i] + terms[i + 1] if i + 1 < len(terms) else terms[i] for i in range(0, len(terms), 2)]
    return terms[0]


def four_pivots(a):
    rows = len(a)
    x = [[None] * (i + 1) for i in range(4)]
    scale = [None] * 4
    product_so_far = None
    for k in range(4):
        pivot = a[k][k]
        x[k][k] = product_so_far
        product_so_far = pivot if k == 0 else product_so_far * pivot
        scale[k] = lax.rsqrt(product_so_far)
        for i in range(k + 1, rows):
            for j in range(k + 1, min(i, 3) + 1):
                a[i][j] = pivot * a[i][j] - a[i][k] * a[j][k]
        for i in range(k + 1, 4):
            for j in range(k):
                x[i][j] = pivot * x[i][j] - a[i][k] * x[k][j]
            x[i][k] = -a[i][k] if k == 0 else -a[i][k] * x[k][k]
        yield
    factor = [[a[i][k] * scale[k] for k in range(4)] for i in range(4, rows)]
    return factor, x, scale


def combined(entries, columns):
    return total_of([column if entry is None else entry * column for entry, column in zip(entries, columns)])


def block_rows(columns, entered, fetch):
    a = [[row(columns[k], i) for k in range(i + 1)] for i in range(STRIP)]
    yield
    below, x, scale = yield from four_pivots([list(entries) for entries in a])
    one = [[scale[i] if entry is None else entry * scale[i] for entry in x[i]] for i in range(4)]
    rest = [
        [a[4 + i][4 + j] - total_of([below[i][k] * below[j][k] for k in range(4)]) for j in range(i + 1)]
        for i in range(4)
    ]

    def halfway(values):
        upper = [combined(one[k], values[:k + 1]) for k in range(4)]
        return upper, [values[4 + m] - total_of([below[m][j] * upper[j] for j in range(4)]) for m in range(4)]

    def updated(diagonal, factors):
        return [diagonal[j] - total_of([f * row(f, j) for f in factors]) for j in range(STRIP)]

    upper, lower = halfway(entered)
    coming = fetch()
    if coming is not None:
        found, left = halfway(coming[0])
        diagonal = updated(coming[1], found)
    _, x, scale = yield from four_pivots(rest)
    two = [[scale[i] if entry is None else entry * scale[i] for entry in x[i]] for i in range(4)]

    def rear(values):
        return [combined(two[k], values[:k + 1]) for k in range(4)]

    if coming is not None:
        more = rear(left)
        coming = found + more, updated(diagonal, more)

    def solve(values):
        front, values = halfway(values)
        return front + rear(values)

    return solve, upper + rear(lower), coming


def inverse_factor(strips, beside):
    lane = lax.broadcasted_iota(jnp.int32, (STRIP, LANES), 1)
    level = lax.broadcasted_iota(jnp.int32, (STRIP, LANES), 0)
    strips = list(strips)
    result = []
    waiting = []

    def finish(p, own, solve, rows):
        def update(r):
            factors = solve([column(strips[r], p * STRIP + j) for j in range(STRIP)])
            terms = [factors[k] * rows[k] for k in range(STRIP)]
            strips[r] = jnp.where(own, 0.0, strips[r]) - total_of(terms)

        return [functools.partial(update, r) for r in range(p + 2, len(strips))]

    columns = [column(strips[0], k) for k in range(STRIP)]
    for p in range(len(strips)):
        start = p * STRIP
        own = (lane >= start) & (lane < start + STRIP)
        if beside:
            waiting.append(beside.pop(0))
        entered = jnp.where(own, jnp.where(lane - start == level, 1.0, 0.0), strips[p])

        def fetch():
            if p + 1 == len(strips):
                return None
            return [[column(strips[p + 1], at + j) for j in range(STRIP)] for at in (start, start + STRIP)]

        steps = block_rows(columns, [row(entered, k) for k in range(STRIP)], fetch)
        while True:
            try:
                next(steps)
            except StopIteration as ended:
                solve, rows, coming = ended.value
                break
            for _ in range(2):
                if waiting:
                    waiting.pop(0)()
        while waiting:
            waiting.pop(0)()
        done = rows[0]
        for k in range(1, STRIP):
            done = jnp.where(level == k, rows[k], done)
        result.append(done)
        if coming is not None:
            found, columns = coming
            update = total_of([found[k] * rows[k] for k in range(STRIP)])
            strips[p + 1] = jnp.where(own, 0.0, strips[p + 1]) - update
            waiting = finish(p, own, solve, rows)
    return [jnp.where(lane < (p + 1) * STRIP, done, 0.0) for p, done in enumerate(result)]


def probe_kernel(
    pivot_ref, point_ref, coeff_ref, noise_ref, inverse_ref, probe_ref, sent_ref, high_ref, middle_ref, little_ref
):
    hp = lax.Precision.HIGHEST
    size = pivot_ref.shape[1]
    half = size // 2
    pivots = jnp.transpose(padded(extended(pivot_ref[...], True))).astype(jnp.bfloat16)
    others = padded(extended(pivot_ref[...], False)).astype(jnp.bfloat16)
    points = padded(extended(point_ref[...], False)).astype(jnp.bfloat16)

    def columns_at(start):
        at = slice(start, start + LANES)
        cols = kernel_of(product(pivots, points[:, at], ((1,), (0,))))
        high_ref[:, at], middle_ref[:, at], little_ref[:, at] = thirds(cols)

    gram = kernel_of(product(pivots, others, ((1,), (0,))))
    equal = lax.broadcasted_iota(jnp.int32, gram.shape, 0) == lax.broadcasted_iota(jnp.int32, gram.shape, 1)
    gram = gram + jnp.where(equal, jitter, 0.0)

    def inverted(block, beside):
        strips = [block[s:s + STRIP, :] for s in range(0, half, STRIP)]
        return jnp.concatenate(inverse_factor(strips, beside), axis=0)

    beside = [functools.partial(columns_at, start) for start in range(0, points.shape[1], LANES)]
    one = inverted(gram[:half, :half], beside)
    below = product(gram[half:, :half], one, ((1,), (1,)), hp)
    back = product(below, one, ((1,), (0,)), hp)
    two = inverted(gram[half:, half:] - product(below, below, ((1,), (1,)), hp), beside)
    coeffs = coeff_ref[...]
    start = product(coeffs[:, :half], one, ((1,), (0,)), hp)
    later = product(coeffs[:, half:], two, ((1,), (0,)), hp)
    weights = jnp.concatenate([start - product(later, back, ((1,), (0,)), hp), later], axis=1)

    rows = weights.shape[0]
    stacked = jnp.concatenate(thirds(weights), axis=0)
    by_high = product(stacked, high_ref[...], ((1,), (0,)))
    by_middle = product(stacked[:2 * rows], middle_ref[...], ((1,), (0,)))
    by_little = product(stacked[:rows], little_ref[...], ((1,), (0,)))
    small = by_high[2 * rows:] + by_middle[rows:] + by_little
    probes = by_high[:rows] + (by_high[rows:2 * rows] + by_middle[:rows] + small) + noise_ref[...]
    probe_ref[...] = probes
    sent_ref[...] = probes.astype(jnp.bfloat16)

    inverse_ref[:half, :half] = one
    inverse_ref[:half, half:] = jnp.zeros((half, half), jnp.float32)
    inverse_ref[half:, :half] = back
    inverse_ref[half:, half:] = two


def probes_of(pivots_t, points_t, coeffs_t, noise_t):
    size = pivots_t.shape[1]
    count = points_t.shape[1]
    return pl.pallas_call(
        probe_kernel,
        out_shape=(
            pltpu.VMEM((size, size), jnp.float32),
            pltpu.VMEM(noise_t.shape, jnp.float32),
            pltpu.VMEM(noise_t.shape, jnp.bfloat16),
        ),
        in_specs=in_vmem(4),
        out_specs=tuple(in_vmem(3)),
        scratch_shapes=[pltpu.VMEM((size, count), jnp.bfloat16)] * 3,
        cost_estimate=LONG,
        compiler_params=pltpu.CompilerParams(vmem_limit_bytes=32 * 1024 * 1024),
        name="probes",
    )(pivots_t, points_t, coeffs_t, noise_t)


def padded(value):
    return jnp.concatenate([value, jnp.zeros((LANES - value.shape[0], value.shape[1]), value.dtype)], axis=0)


def tile_terms(own, other, probes):
    return product(kernel_of(product(own, other, ((1,), (0,)))).astype(jnp.bfloat16), probes, ((1,), (1,)))


def factor_kernel(pivot_ref, point_ref, inverse_ref, awaited_ref, factor_ref, zero_ref):
    count = point_ref.shape[1]
    own = jnp.transpose(padded(extended(point_ref[...], True))).astype(jnp.bfloat16)
    pivots = padded(extended(pivot_ref[...], False)).astype(jnp.bfloat16)
    half = inverse_ref.shape[0] // 2
    later = inverse_ref[half:, half:]
    corner = -product(later, inverse_ref[half:, :half], ((1,), (0,)), lax.Precision.HIGHEST)
    inverse = jnp.concatenate([inverse_ref[:half, :], jnp.concatenate([corner, later], axis=1)], axis=0)
    high, middle, _ = thirds(inverse)
    for s in range(0, count, CHUNK):
        rows = own[s:s + CHUNK, :]
        cols_high, cols_middle, _ = thirds(kernel_of(product(rows, pivots, ((1,), (0,)))))
        factor_ref[s:s + CHUNK, :] = (
            product(cols_high, middle, ((1,), (1,))) + product(cols_middle, high, ((1,), (1,)))
        ) + product(cols_high, high, ((1,), (1,)))
    zero_ref[...] = jnp.zeros_like(zero_ref)


def factor_of(pivots_t, points_t, inverse, awaited):
    size = pivots_t.shape[1]
    depth, count = points_t.shape
    return pl.pallas_call(
        factor_kernel,
        out_shape=(
            jax.ShapeDtypeStruct((count, size), jnp.float32),
            pltpu.VMEM((depth, count), jnp.bfloat16),
        ),
        in_specs=in_vmem(3) + [pl.BlockSpec(memory_space=pl.ANY)],
        out_specs=tuple(in_vmem(2)),
        compiler_params=pltpu.CompilerParams(vmem_limit_bytes=32 * 1024 * 1024),
        cost_estimate=pl.CostEstimate(
            flops=6 * count * size * size // 8,
            bytes_accessed=6 * count * size // 8,
            transcendentals=count * size // 8,
        ),
        name="factor",
    )(pivots_t, points_t, inverse, awaited)


def band_kernel(pieces, first, last, *refs):
    own_ref = refs[0]
    depth, count = own_ref.shape
    rest = list(refs[1 + max(place for piece in pieces for place, _ in piece):])
    before_ref = None if first else rest.pop(0)
    own = jnp.transpose(padded(extended(own_ref[...], True))).astype(jnp.bfloat16)
    blocks = []
    for (point_at, point_row), (probe_at, probe_row) in pieces:
        points = refs[point_at][point_row:point_row + depth, :]
        blocks.append((padded(extended(points, False)).astype(jnp.bfloat16), refs[probe_at], probe_row))
    for s in range(0, count, CHUNK):
        total = None if first else before_ref[s:s + CHUNK, :]
        for other, probe_ref, probe_row in blocks:
            term = tile_terms(own[s:s + CHUNK, :], other, probe_ref[probe_row:, :])
            total = term if total is None else total + term
        if last:
            probe_ref, out_ref = rest
            scale = 1.0 / (count ** 0.5)
            out_ref[:, s:s + CHUNK] = jnp.transpose(total) * scale + noise_weight * probe_ref[:, s:s + CHUNK]
        else:
            rest[0][s:s + CHUNK, :] = total
    if not last:
        rest[1][...] = jnp.zeros_like(rest[1])


def band_sum(own, pieces, before=None, probes=None):
    depth, count = own.shape
    first, last = before is None, probes is not None
    operands = [own]
    places = []
    for piece in pieces:
        place = []
        for array, start in piece:
            known = [i for i, operand in enumerate(operands) if operand is array]
            if not known:
                operands.append(array)
            place.append((known[0] if known else len(operands) - 1, start))
        places.append(tuple(place))
    array, start = pieces[0][1]
    width = array.shape[0] - start
    operands += ([] if first else [before]) + ([probes] if last else [])
    if last:
        out_shape = jax.ShapeDtypeStruct((width, count), jnp.float32)
    else:
        out_shape = (pltpu.VMEM((count, width), jnp.float32), pltpu.VMEM((width, count), jnp.bfloat16))
    return pl.pallas_call(
        functools.partial(band_kernel, tuple(places), first, last),
        out_shape=out_shape,
        in_specs=in_vmem(len(operands)),
        out_specs=in_vmem(1)[0] if last else tuple(in_vmem(2)),
        compiler_params=pltpu.CompilerParams(vmem_limit_bytes=32 * 1024 * 1024),
        cost_estimate=pl.CostEstimate(
            flops=1 if first else len(pieces) * 4 * count * count * LANES,
            bytes_accessed=1 if first else 4 * count * width * len(operands),
            transcendentals=0 if first else len(pieces) * count * count,
        ),
        name="band_sum",
    )(*operands)


def shards(points, pivots, owners, coeffs, noise):
    tall = lax.axis_size("gy") == BAND + 1
    points = points.T
    depth = points.shape[0]
    row_sum = spread(pick(owners, pivots, points), "gx")
    if tall:
        far = swapped(points, "gy", 2)
        row_sum = row_sum + zero_like(far[:, :row_sum.shape[1]])
        pair = swapped(jnp.concatenate([points, far], axis=0), "gy", 1)
    else:
        near = direct_blocks(points)
    pivot_points = spread(row_sum, "gy")

    inverse, probes, sent = probes_of(pivot_points, points, coeffs.T, noise.T)
    total, zeros = band_sum(points, [((points, 0), (sent, 0))])
    if tall:
        leaving = sent + zero_like(pair[:depth])
        two = swapped(leaving, "gy", 2)
        one = swapped(leaving, "gy", 1) + zeros
        factor, zeros = factor_of(pivot_points, points, inverse, one)
        two = two + zeros
        cross_one = cross(jnp.concatenate([pair[:depth], one], axis=0), 1)
        three = swapped(two, "gy", 1)
        cross_two = cross(jnp.concatenate([far, pair[depth:], two], axis=0), 2)
        pieces = [((pair, 0), (one, 0)), ((far, 0), (two, 0)), ((cross_one, 0), (cross_one, depth))]
        total, zeros = band_sum(points, pieces, total)
        three = three + zeros
        cross_three = cross(three, 3)
        total, _ = band_sum(points, [((pair, depth), (three, 0)), ((cross_two, 0), (cross_two, 2 * depth))], total)
        kernel_probes = band_sum(points, [((cross_two, depth), (cross_three, 0))], total, probes)
    else:
        factor, _ = factor_of(pivot_points, points, inverse, zeros)
        pieces = [((block, 0), (probe, 0)) for block, probe in zip(near, direct_blocks(sent))]
        total, _ = band_sum(points, pieces[:3], total)
        kernel_probes = band_sum(points, pieces[3:], total, probes)
    return (kernel_probes.T, factor)


def solution(mesh):
    in_specs = (P(("gx", "gy"), None), P(), P(), P(), P(("gx", "gy"), None))
    out_specs = (P(("gx", "gy"), None), P(("gx", "gy"), None))
    return jax.shard_map(shards, mesh=mesh, in_specs=in_specs, out_specs=out_specs, check_vma=False)
```

```python
import functools
import math

import jax
import jax.numpy as jnp
from jax import lax
from jax.experimental import pallas as pl
from jax.experimental.pallas import tpu as pltpu
from jax.sharding import PartitionSpec as P

PIVOTS = 128
KERNEL_SCALE = 32
BAND = 3
STRIP = 8
LANES = 128
EXTRA = 16
CHUNK = 256
LONG = pl.CostEstimate(flops=1 << 34, bytes_accessed=1, transcendentals=0)


jitter = 0.1
noise_weight = 0.5


def shifted(value, axis, steps):
    count = lax.axis_size(axis)
    return lax.ppermute(value, axis, [((i + steps) % count, i) for i in range(count)])


def swapped(value, axis, bit):
    return lax.ppermute(value, axis, [(i ^ bit, i) for i in range(lax.axis_size(axis))])


def spread(value, axis):
    count = lax.axis_size(axis)
    bit = 1
    while bit < count:
        wide = 2 if (count // bit).bit_length() % 2 == 0 else 4
        value = sum((swapped(value, axis, bit * k) for k in range(1, wide)), value)
        bit *= wide
    return value


def zero_like(value):
    return jnp.minimum(jnp.abs(value), 0)


def cross(piece, bits):
    outer, inner = lax.axis_size("gx"), lax.axis_size("gy")
    pairs = []
    for x in range(outer):
        for z in range(inner):
            source = (x - 1 if z ^ bits > z else x + 1) % outer
            pairs.append((source * inner + z, x * inner + z))
    return lax.ppermute(piece, ("gx", "gy"), pairs)


def direct_blocks(value):
    return [shifted(value, ("gx", "gy"), k) for k in range(-BAND, BAND + 1) if k != 0]


def in_vmem(count):
    return [pl.BlockSpec(memory_space=pltpu.VMEM)] * count


def thirds(value):
    high = value.astype(jnp.bfloat16)
    rest = value - high.astype(jnp.float32)
    middle = rest.astype(jnp.bfloat16)
    return high, middle, (rest - middle.astype(jnp.float32)).astype(jnp.bfloat16)


def product(left, right, contract, precision=None):
    return lax.dot_general(
        left, right, (contract, ((), ())), precision=precision, preferred_element_type=jnp.float32
    )


def extended(columns, ones_first):
    wide = columns.astype(jnp.float32)
    half = -0.5 * jnp.sum(wide * wide, axis=0, keepdims=True)
    terms = [term.astype(jnp.float32) for term in thirds(half)]
    shape = (EXTRA, columns.shape[1])
    level = lax.broadcasted_iota(jnp.int32, shape, 0)
    first = 0 if ones_first else 3
    below = jnp.where((level >= first) & (level < first + 3), 1.0, 0.0)
    for i, term in enumerate(terms):
        below = jnp.where(level == 3 - first + i, jnp.broadcast_to(term, shape), below)
    return jnp.concatenate([wide, below], axis=0)


def kernel_of(product_of_extended):
    return jnp.exp2(product_of_extended * (2.0 / KERNEL_SCALE * math.log2(math.e)))


def pick_kernel(owner_ref, pivot_ref, point_ref, out_ref):
    count = point_ref.shape[1]
    me = lax.axis_index(("gx", "gy"))
    wanted = [jnp.where(owner_ref[r] == me, pivot_ref[r:r + 1, :], -1) for r in range(2)]
    wanted = jnp.concatenate(wanted, axis=1)
    place = lax.broadcasted_iota(jnp.int32, (count, wanted.shape[1]), 0)
    chosen = jnp.where(place == wanted, 1.0, 0.0).astype(jnp.bfloat16)
    out_ref[...] = product(point_ref[...], chosen, ((1,), (0,))).astype(jnp.bfloat16)


def pick(owners, pivots, points_t):
    return pl.pallas_call(
        pick_kernel,
        out_shape=pltpu.VMEM((points_t.shape[0], 2 * PIVOTS), jnp.bfloat16),
        in_specs=[pl.BlockSpec(memory_space=pltpu.SMEM)] + in_vmem(2),
        out_specs=in_vmem(1)[0],
        name="pick",
    )(owners, pivots, points_t)


def column(strip, lane):
    return jnp.broadcast_to(strip[:, lane:lane + 1], strip.shape)


def row(strip, i):
    return jnp.broadcast_to(strip[i:i + 1, :], strip.shape)


def total_of(terms):
    while len(terms) > 1:
        terms = [terms[i] + terms[i + 1] if i + 1 < len(terms) else terms[i] for i in range(0, len(terms), 2)]
    return terms[0]


def four_pivots(a):
    rows = len(a)
    x = [[None] * (i + 1) for i in range(4)]
    scale = [None] * 4
    product_so_far = None
    for k in range(4):
        pivot = a[k][k]
        x[k][k] = product_so_far
        product_so_far = pivot if k == 0 else product_so_far * pivot
        scale[k] = lax.rsqrt(product_so_far)
        for i in range(k + 1, rows):
            for j in range(k + 1, min(i, 3) + 1):
                a[i][j] = pivot * a[i][j] - a[i][k] * a[j][k]
        for i in range(k + 1, 4):
            for j in range(k):
                x[i][j] = pivot * x[i][j] - a[i][k] * x[k][j]
            x[i][k] = -a[i][k] if k == 0 else -a[i][k] * x[k][k]
        yield
    factor = [[a[i][k] * scale[k] for k in range(4)] for i in range(4, rows)]
    return factor, x, scale


def combined(entries, columns):
    return total_of([column if entry is None else entry * column for entry, column in zip(entries, columns)])


def block_rows(columns, entered, fetch):
    a = [[row(columns[k], i) for k in range(i + 1)] for i in range(STRIP)]
    yield
    below, x, scale = yield from four_pivots([list(entries) for entries in a])
    one = [[scale[i] if entry is None else entry * scale[i] for entry in x[i]] for i in range(4)]
    rest = [
        [a[4 + i][4 + j] - total_of([below[i][k] * below[j][k] for k in range(4)]) for j in range(i + 1)]
        for i in range(4)
    ]

    def halfway(values):
        upper = [combined(one[k], values[:k + 1]) for k in range(4)]
        return upper, [values[4 + m] - total_of([below[m][j] * upper[j] for j in range(4)]) for m in range(4)]

    def updated(diagonal, factors):
        return [diagonal[j] - total_of([f * row(f, j) for f in factors]) for j in range(STRIP)]

    upper, lower = halfway(entered)
    coming = fetch()
    if coming is not None:
        found, left = halfway(coming[0])
        diagonal = updated(coming[1], found)
    _, x, scale = yield from four_pivots(rest)
    two = [[scale[i] if entry is None else entry * scale[i] for entry in x[i]] for i in range(4)]

    def rear(values):
        return [combined(two[k], values[:k + 1]) for k in range(4)]

    if coming is not None:
        more = rear(left)
        coming = found + more, updated(diagonal, more)

    def solve(values):
        front, values = halfway(values)
        return front + rear(values)

    def solve_back(values):
        last = [total_of([two[k][m] * values[4 + k] for k in range(m, 4)]) for m in range(4)]
        rest = [values[j] - total_of([below[m][j] * last[m] for m in range(4)]) for j in range(4)]
        return [total_of([one[k][j] * rest[k] for k in range(j, 4)]) for j in range(4)] + last

    return solve, solve_back, upper + rear(lower), coming


def inverse_factor(strips, beside):
    lane = lax.broadcasted_iota(jnp.int32, (STRIP, LANES), 1)
    level = lax.broadcasted_iota(jnp.int32, (STRIP, LANES), 0)
    strips = list(strips)
    result = []
    waiting = []

    def finish(p, own, solve, solve_back, rows):
        spanned = []

        def subtract(r, factors, rows):
            terms = [factors[k] * rows[k] for k in range(STRIP)]
            strips[r] = jnp.where(own, 0.0, strips[r]) - total_of(terms)

        def columns_of(r):
            return [column(strips[r], p * STRIP + j) for j in range(STRIP)]

        def second(r):
            subtract(r, solve(columns_of(r)), rows)

        def span():
            spanned.extend(solve_back(rows))

        def later(r):
            subtract(r, columns_of(r), spanned)

        count = len(strips)
        steps = [functools.partial(second, p + 2)] if p + 2 < count else []
        if p + 3 < count:
            steps += [span] + [functools.partial(later, r) for r in range(p + 3, count)]
        return steps

    columns = [column(strips[0], k) for k in range(STRIP)]
    for p in range(len(strips)):
        start = p * STRIP
        own = (lane >= start) & (lane < start + STRIP)
        if beside:
            waiting.append(beside.pop(0))
        entered = jnp.where(own, jnp.where(lane - start == level, 1.0, 0.0), strips[p])

        def fetch():
            if p + 1 == len(strips):
                return None
            return [[column(strips[p + 1], at + j) for j in range(STRIP)] for at in (start, start + STRIP)]

        steps = block_rows(columns, [row(entered, k) for k in range(STRIP)], fetch)
        while True:
            try:
                next(steps)
            except StopIteration as ended:
                solve, solve_back, rows, coming = ended.value
                break
            for _ in range(2):
                if waiting:
                    waiting.pop(0)()
        while waiting:
            waiting.pop(0)()
        done = rows[0]
        for k in range(1, STRIP):
            done = jnp.where(level == k, rows[k], done)
        result.append(done)
        if coming is not None:
            found, columns = coming
            update = total_of([found[k] * rows[k] for k in range(STRIP)])
            strips[p + 1] = jnp.where(own, 0.0, strips[p + 1]) - update
            waiting = finish(p, own, solve, solve_back, rows)
    return [jnp.where(lane < (p + 1) * STRIP, done, 0.0) for p, done in enumerate(result)]


def probe_kernel(
    pivot_ref, point_ref, coeff_ref, noise_ref, inverse_ref, probe_ref, sent_ref, high_ref, middle_ref, little_ref
):
    hp = lax.Precision.HIGHEST
    size = pivot_ref.shape[1]
    half = size // 2
    pivots = jnp.transpose(padded(extended(pivot_ref[...], True))).astype(jnp.bfloat16)
    others = padded(extended(pivot_ref[...], False)).astype(jnp.bfloat16)
    points = padded(extended(point_ref[...], False)).astype(jnp.bfloat16)

    def columns_at(start):
        at = slice(start, start + LANES)
        cols = kernel_of(product(pivots, points[:, at], ((1,), (0,))))
        high_ref[:, at], middle_ref[:, at], little_ref[:, at] = thirds(cols)

    gram = kernel_of(product(pivots, others, ((1,), (0,))))
    equal = lax.broadcasted_iota(jnp.int32, gram.shape, 0) == lax.broadcasted_iota(jnp.int32, gram.shape, 1)
    gram = gram + jnp.where(equal, jitter, 0.0)

    def inverted(block, beside):
        strips = [block[s:s + STRIP, :] for s in range(0, half, STRIP)]
        return jnp.concatenate(inverse_factor(strips, beside), axis=0)

    beside = [functools.partial(columns_at, start) for start in range(0, points.shape[1], LANES)]
    one = inverted(gram[:half, :half], beside)
    below = product(gram[half:, :half], one, ((1,), (1,)), hp)
    back = product(below, one, ((1,), (0,)), hp)
    two = inverted(gram[half:, half:] - product(below, below, ((1,), (1,)), hp), beside)
    coeffs = coeff_ref[...]
    start = product(coeffs[:, :half], one, ((1,), (0,)), hp)
    later = product(coeffs[:, half:], two, ((1,), (0,)), hp)
    weights = jnp.concatenate([start - product(later, back, ((1,), (0,)), hp), later], axis=1)

    rows = weights.shape[0]
    stacked = jnp.concatenate(thirds(weights), axis=0)
    by_high = product(stacked, high_ref[...], ((1,), (0,)))
    by_middle = product(stacked[:2 * rows], middle_ref[...], ((1,), (0,)))
    by_little = product(stacked[:rows], little_ref[...], ((1,), (0,)))
    small = by_high[2 * rows:] + by_middle[rows:] + by_little
    probes = by_high[:rows] + (by_high[rows:2 * rows] + by_middle[:rows] + small) + noise_ref[...]
    probe_ref[...] = probes
    sent_ref[...] = probes.astype(jnp.bfloat16)

    inverse_ref[:half, :half] = one
    inverse_ref[:half, half:] = jnp.zeros((half, half), jnp.float32)
    inverse_ref[half:, :half] = -product(two, back, ((1,), (0,)), hp)
    inverse_ref[half:, half:] = two


def probes_of(pivots_t, points_t, coeffs_t, noise_t):
    size = pivots_t.shape[1]
    count = points_t.shape[1]
    return pl.pallas_call(
        probe_kernel,
        out_shape=(
            pltpu.VMEM((size, size), jnp.float32),
            pltpu.VMEM(noise_t.shape, jnp.float32),
            pltpu.VMEM(noise_t.shape, jnp.bfloat16),
        ),
        in_specs=in_vmem(4),
        out_specs=tuple(in_vmem(3)),
        scratch_shapes=[pltpu.VMEM((size, count), jnp.bfloat16)] * 3,
        cost_estimate=LONG,
        compiler_params=pltpu.CompilerParams(vmem_limit_bytes=32 * 1024 * 1024),
        name="probes",
    )(pivots_t, points_t, coeffs_t, noise_t)


def padded(value):
    return jnp.concatenate([value, jnp.zeros((LANES - value.shape[0], value.shape[1]), value.dtype)], axis=0)


def tile_terms(own, other, probes):
    return product(kernel_of(product(own, other, ((1,), (0,)))).astype(jnp.bfloat16), probes, ((1,), (1,)))


def factor_kernel(pivot_ref, point_ref, inverse_ref, awaited_ref, factor_ref, zero_ref):
    count = point_ref.shape[1]
    own = jnp.transpose(padded(extended(point_ref[...], True))).astype(jnp.bfloat16)
    pivots = padded(extended(pivot_ref[...], False)).astype(jnp.bfloat16)
    high, middle, _ = thirds(inverse_ref[...])
    for s in range(0, count, CHUNK):
        rows = own[s:s + CHUNK, :]
        cols_high, cols_middle, _ = thirds(kernel_of(product(rows, pivots, ((1,), (0,)))))
        factor_ref[s:s + CHUNK, :] = (
            product(cols_high, middle, ((1,), (1,))) + product(cols_middle, high, ((1,), (1,)))
        ) + product(cols_high, high, ((1,), (1,)))
    zero_ref[...] = jnp.zeros_like(zero_ref)


def factor_of(pivots_t, points_t, inverse, awaited):
    size = pivots_t.shape[1]
    depth, count = points_t.shape
    return pl.pallas_call(
        factor_kernel,
        out_shape=(
            jax.ShapeDtypeStruct((count, size), jnp.float32),
            pltpu.VMEM((depth, count), jnp.bfloat16),
        ),
        in_specs=in_vmem(3) + [pl.BlockSpec(memory_space=pl.ANY)],
        out_specs=tuple(in_vmem(2)),
        compiler_params=pltpu.CompilerParams(vmem_limit_bytes=32 * 1024 * 1024),
        cost_estimate=pl.CostEstimate(
            flops=6 * count * size * size // 8,
            bytes_accessed=6 * count * size // 8,
            transcendentals=count * size // 8,
        ),
        name="factor",
    )(pivots_t, points_t, inverse, awaited)


def band_kernel(pieces, first, last, *refs):
    own_ref = refs[0]
    depth, count = own_ref.shape
    rest = list(refs[1 + max(place for piece in pieces for place, _ in piece):])
    before_ref = None if first else rest.pop(0)
    own = jnp.transpose(padded(extended(own_ref[...], True))).astype(jnp.bfloat16)
    blocks = []
    for (point_at, point_row), (probe_at, probe_row) in pieces:
        points = refs[point_at][point_row:point_row + depth, :]
        blocks.append((padded(extended(points, False)).astype(jnp.bfloat16), refs[probe_at], probe_row))
    for s in range(0, count, CHUNK):
        total = None if first else before_ref[s:s + CHUNK, :]
        for other, probe_ref, probe_row in blocks:
            term = tile_terms(own[s:s + CHUNK, :], other, probe_ref[probe_row:, :])
            total = term if total is None else total + term
        if last:
            probe_ref, out_ref = rest
            scale = 1.0 / (count ** 0.5)
            out_ref[:, s:s + CHUNK] = jnp.transpose(total) * scale + noise_weight * probe_ref[:, s:s + CHUNK]
        else:
            rest[0][s:s + CHUNK, :] = total
    if not last:
        rest[1][...] = jnp.zeros_like(rest[1])


def band_sum(own, pieces, before=None, probes=None):
    depth, count = own.shape
    first, last = before is None, probes is not None
    operands = [own]
    places = []
    for piece in pieces:
        place = []
        for array, start in piece:
            known = [i for i, operand in enumerate(operands) if operand is array]
            if not known:
                operands.append(array)
            place.append((known[0] if known else len(operands) - 1, start))
        places.append(tuple(place))
    array, start = pieces[0][1]
    width = array.shape[0] - start
    operands += ([] if first else [before]) + ([probes] if last else [])
    if last:
        out_shape = jax.ShapeDtypeStruct((width, count), jnp.float32)
    else:
        out_shape = (pltpu.VMEM((count, width), jnp.float32), pltpu.VMEM((width, count), jnp.bfloat16))
    return pl.pallas_call(
        functools.partial(band_kernel, tuple(places), first, last),
        out_shape=out_shape,
        in_specs=in_vmem(len(operands)),
        out_specs=in_vmem(1)[0] if last else tuple(in_vmem(2)),
        compiler_params=pltpu.CompilerParams(vmem_limit_bytes=32 * 1024 * 1024),
        cost_estimate=pl.CostEstimate(
            flops=1 if first else len(pieces) * 4 * count * count * LANES,
            bytes_accessed=1 if first else 4 * count * width * len(operands),
            transcendentals=0 if first else len(pieces) * count * count,
        ),
        name="band_sum",
    )(*operands)


def shards(points, pivots, owners, coeffs, noise):
    tall = lax.axis_size("gy") == BAND + 1
    points = points.T
    depth = points.shape[0]
    row_sum = spread(pick(owners, pivots, points), "gx")
    if tall:
        far = swapped(points, "gy", 2)
        row_sum = row_sum + zero_like(far[:, :row_sum.shape[1]])
        pair = swapped(jnp.concatenate([points, far], axis=0), "gy", 1)
    else:
        near = direct_blocks(points)
    pivot_points = spread(row_sum, "gy")

    inverse, probes, sent = probes_of(pivot_points, points, coeffs.T, noise.T)
    total, zeros = band_sum(points, [((points, 0), (sent, 0))])
    if tall:
        leaving = sent + zero_like(pair[:depth])
        two = swapped(leaving, "gy", 2)
        one = swapped(leaving, "gy", 1) + zeros
        factor, zeros = factor_of(pivot_points, points, inverse, one)
        two = two + zeros
        cross_one = cross(jnp.concatenate([pair[:depth], one], axis=0), 1)
        three = swapped(two, "gy", 1)
        cross_two = cross(jnp.concatenate([far, two], axis=0), 2)
        total, zeros = band_sum(points, [((pair, 0), (one, 0)), ((far, 0), (two, 0))], total)
        cross_three = cross(jnp.concatenate([pair[depth:], three + zeros], axis=0), 3)
        crossed = [((stacked, 0), (stacked, depth)) for stacked in (cross_one, cross_two, cross_three)]
        total, _ = band_sum(points, [((pair, depth), (three, 0)), crossed[0]], total)
        total, _ = band_sum(points, crossed[1:2], total)
        kernel_probes = band_sum(points, crossed[2:], total, probes)
    else:
        factor, _ = factor_of(pivot_points, points, inverse, zeros)
        pieces = [((block, 0), (probe, 0)) for block, probe in zip(near, direct_blocks(sent))]
        total, _ = band_sum(points, pieces[:3], total)
        kernel_probes = band_sum(points, pieces[3:], total, probes)
    return (kernel_probes.T, factor)


def solution(mesh):
    in_specs = (P(("gx", "gy"), None), P(), P(), P(), P(("gx", "gy"), None))
    out_specs = (P(("gx", "gy"), None), P(("gx", "gy"), None))
    return jax.shard_map(shards, mesh=mesh, in_specs=in_specs, out_specs=out_specs, check_vma=False)
```
